32 devices in a mesh: batch: 16 (over z, x, core), query: 2 (over y).
Axes of the slice: x: 2, y: 2, z: 4, core: 2. Of those that a mesh axis runs over, the one named last changes fastest.
Arguments:
- latents: bfloat16 [96, 100, 768], P('batch', 'query'), may hold values from -6 to 6
- queries: bfloat16 [96, 96, 768], P('batch', 'query'), may hold values from -6 to 6
- order: int32 [96, 196], P('batch'), may hold values from 0 to 195, each once within a row
- weight_query: bfloat16 [768, 768], P(('batch', 'query')), may hold values from -0.21875 to 0.21875
- bias_query: bfloat16 [768], P(('batch', 'query')), may hold values from -4 to 4
- weight_key: bfloat16 [768, 768], P(('batch', 'query')), may hold values from -0.21875 to 0.21875
- weight_value: bfloat16 [768, 768], P(('batch', 'query')), may hold values from -0.21875 to 0.21875
- bias_value: bfloat16 [768], P(('batch', 'query')), may hold values from -0.75 to 0.75
- weight_out: bfloat16 [768, 768], P(('batch', 'query')), may hold values from -1.75 to 1.75
- bias_out: bfloat16 [768], P(('batch', 'query')), may hold values from -4 to 4
- gain_query: bfloat16 [768], P(('batch', 'query')), may hold values from 0.099609375 to 1.8984375
- shift_query: bfloat16 [768], P(('batch', 'query')), may hold values from -4 to 4
- gain_key: bfloat16 [768], P(('batch', 'query')), may hold values from 0.099609375 to 1.8984375
- gain_value: bfloat16 [768], P(('batch', 'query')), may hold values from 0.099609375 to 1.8984375
- shift_value: bfloat16 [768], P(('batch', 'query')), may hold values from -1.5 to 1.5
- scale_attention: bfloat16 [768], P(('batch', 'query')), may hold values from 0.5 to 2
- weight_up: bfloat16 [768, 3072], P(('batch', 'query')), may hold values from -0.21875 to 0.21875
- bias_up: bfloat16 [3072], P(('batch', 'query')), may hold values from -4 to 4
- weight_down: bfloat16 [3072, 768], P(('batch', 'query')), may hold values from -0.109375 to 0.109375
- bias_down: bfloat16 [768], P(('batch', 'query')), may hold values from -4 to 4
- gain_feed: bfloat16 [768], P(('batch', 'query')), may hold values from 0.099609375 to 1.8984375
- shift_feed: bfloat16 [768], P(('batch', 'query')), may hold values from -4 to 4
- scale_feed: bfloat16 [768], P(('batch', 'query')), may hold values from 0.5 to 2
- cotangent: bfloat16 [96, 96, 768], P('batch', 'query'), may hold values from -6 to 6
Outputs:
- mixed: bfloat16 [96, 96, 768], P('batch', 'query')
- latents_gradient: float32 [96, 100, 768], P('batch', 'query')
- queries_gradient: float32 [96, 96, 768], P('batch', 'query')
- weight_query_gradient: float32 [768, 768], P(('batch', 'query'))
- bias_query_gradient: float32 [768], P(('batch', 'query'))
- weight_key_gradient: float32 [768, 768], P(('batch', 'query'))
- weight_value_gradient: float32 [768, 768], P(('batch', 'query'))
- bias_value_gradient: float32 [768], P(('batch', 'query'))
- weight_out_gradient: float32 [768, 768], P(('batch', 'query'))
- bias_out_gradient: float32 [768], P(('batch', 'query'))
- gain_query_gradient: float32 [768], P(('batch', 'query'))
- shift_query_gradient: float32 [768], P(('batch', 'query'))
- gain_key_gradient: float32 [768], P(('batch', 'query'))
- gain_value_gradient: float32 [768], P(('batch', 'query'))
- shift_value_gradient: float32 [768], P(('batch', 'query'))
- scale_attention_gradient: float32 [768], P(('batch', 'query'))
- weight_up_gradient: float32 [768, 3072], P(('batch', 'query'))
- bias_up_gradient: float32 [3072], P(('batch', 'query'))
- weight_down_gradient: float32 [3072, 768], P(('batch', 'query'))
- bias_down_gradient: float32 [768], P(('batch', 'query'))
- gain_feed_gradient: float32 [768], P(('batch', 'query'))
- shift_feed_gradient: float32 [768], P(('batch', 'query'))
- scale_feed_gradient: float32 [768], P(('batch', 'query'))
The draws below stay inside these ranges and needn't reach their ends.
Inputs may be any that keep to these rules, and one draw needn't show every extreme that they name: Each row names every patch of its crop once: the first 100 entries belong to the latents' rows in order, the others to the queries' rows in order.
All inputs are finite; a program needn't handle non-finite values.
Results may differ from the reference program's by a relative error of at most 0.015.
Values may be sent and summed in bfloat16 or wider, within the bound.
No kernel may reach another device: no remote copies, remote signals or barrier semaphores. Data moves between devices by JAX's collectives and lax.ppermute only.
A program may use at most 192 MiB of HBM per device.

```python
import math
import jax
import jax.numpy as jnp
from jax import lax

D = 768
FF = 3072
HEADS = 12
HEAD_DIM = 64
GRID = 14
VISIBLE = 100
PATCHES = 196
MASKED = 96
CROPS = 96


def spiked(entries, own_key, source, target, parts, factor):
    def block_of(dim):
        return (jnp.arange(entries.shape[dim]) // (entries.shape[dim] // parts)).reshape((-1,) + (1,) * (entries.ndim - 1 - dim))

    near = jax.random.permutation(own_key, parts)[block_of(target)]
    far = (block_of(target) + parts // 2) % parts
    return jnp.where((block_of(source) == near) | (block_of(source) == far), factor * entries, entries)


def shard_levels(rng, extent, pieces, smallest, top_value):
    level, own = 1.0, jax.random.fold_in(rng, 6)
    for position, parts in pieces:
        heights = jnp.exp(jax.random.uniform(jax.random.fold_in(own, position), (parts,), jnp.float32, smallest / len(pieces), top_value / len(pieces)))
        level = level * jnp.repeat(heights, extent[position] // parts).reshape([-1 if axis == position else 1 for axis in range(len(extent))])
    return level


def noise(key, extent, deviation, bound, pieces=(), held_as=jnp.bfloat16):
    array = jax.random.normal(key, extent, jnp.float32) * deviation
    if len(pieces) > 0:
        array = shard_levels(key, extent, pieces, -0.22, 0.18) * array
    return jnp.clip(array, min=-bound, max=bound).astype(held_as)


def noise_with(own_key, dims, width, most, split, heavy, dtype=jnp.bfloat16):
    drawn = width * jax.random.normal(own_key, dims, jnp.float32)
    if split:
        drawn = drawn * shard_levels(own_key, dims, split, -0.22, 0.18)
    return jnp.clip(spiked(drawn, jax.random.fold_in(own_key, 3), *heavy), -most, most).astype(dtype)


def setup_inputs(seed: int = 0) -> dict:
    splits = jax.random.split(jax.random.key(seed), 25)
    return {
        "latents": noise(splits[0], (CROPS, VISIBLE, D), 1.0, 6.0, ((0, 16), (1, 2))),
        "queries": noise(splits[1], (CROPS, MASKED, D), 1.0, 6.0, ((0, 16), (1, 2))),
        "order": jax.vmap(lambda own: jax.random.permutation(own, PATCHES))(jax.random.split(splits[2], CROPS)).reshape((CROPS, PATCHES)).astype(jnp.int32),
        "weight_query": noise(splits[3], (D, D), D ** -0.5, 0.21875, ((0, 32),)),
        "bias_query": noise(splits[4], (D,), 0.3, 4.0, ((0, 32),)),
        "weight_key": noise(splits[5], (D, D), D ** -0.5, 0.21875, ((0, 32),)),
        "weight_value": noise(splits[6], (D, D), D ** -0.5, 0.21875, ((0, 32),)),
        "bias_value": noise(splits[7], (D,), 0.05, 0.75, ((0, 32),)),
        "weight_out": noise(splits[8], (D, D), (D // 64) ** -0.5, 1.75, ((0, 32),)),
        "bias_out": noise(splits[9], (D,), 0.3, 4.0, ((0, 32),)),
        "gain_query": jnp.clip(1.0 + 0.18 * jax.random.normal(splits[10], (D,), jnp.float32), 0.099609375, 1.8984375).astype(jnp.bfloat16),
        "shift_query": noise(splits[11], (D,), 0.3, 4.0, ((0, 32),)),
        "gain_key": jnp.clip(1.0 + 0.18 * jax.random.normal(splits[12], (D,), jnp.float32), 0.099609375, 1.8984375).astype(jnp.bfloat16),
        "gain_value": jnp.clip(1.0 + 0.18 * jax.random.normal(splits[13], (D,), jnp.float32), 0.099609375, 1.8984375).astype(jnp.bfloat16),
        "shift_value": noise(splits[14], (D,), 0.1, 1.5, ((0, 32),)),
        "scale_attention": jnp.clip(jnp.exp(math.log(2.0) - 1.3862944 * jax.random.uniform(splits[15], (D,), jnp.float32) ** shard_levels(splits[15], (D,), ((0, 32),), -0.2, 0.2)), 0.5, 2.0).astype(jnp.bfloat16),
        "weight_up": noise(splits[16], (D, FF), D ** -0.5, 0.21875, ((0, 32),)),
        "bias_up": noise(splits[17], (FF,), 0.3, 4.0, ((0, 32),)),
        "weight_down": noise(splits[18], (FF, D), FF ** -0.5, 0.109375, ((0, 32),)),
        "bias_down": noise(splits[19], (D,), 0.3, 4.0, ((0, 32),)),
        "gain_feed": jnp.clip(1.0 + 0.18 * jax.random.normal(splits[20], (D,), jnp.float32), 0.099609375, 1.8984375).astype(jnp.bfloat16),
        "shift_feed": noise(splits[21], (D,), 0.3, 4.0, ((0, 32),)),
        "scale_feed": jnp.clip(jnp.exp(math.log(2.0) - 1.3862944 * jax.random.uniform(splits[22], (D,), jnp.float32) ** shard_levels(splits[22], (D,), ((0, 32),), -0.2, 0.2)), 0.5, 2.0).astype(jnp.bfloat16),
        "cotangent": noise_with(splits[23], (CROPS, MASKED, D), 1.0, 6.0, ((0, 16), (1, 2)), (0, 2, 16, 2.0)),
    }


epsilon = 1e-06
highest = lax.Precision.HIGHEST

@jax.custom_vjp
def low(v):
    return lax.optimization_barrier(v.astype(jnp.bfloat16)).astype(jnp.float32)

@jax.custom_vjp
def low_back(v):
    return v

def low_keep(v):
    return (low(v), None)

def low_pass(kept, grad):
    return (grad,)

def back_keep(v):
    return (v, None)

def back_low(kept, grad):
    return (low(grad),)
low.defvjp(low_keep, low_pass)
low_back.defvjp(back_keep, back_low)

def normalize(values, norm_gain, norm_shift):
    centered = values - lax.optimization_barrier(jnp.mean(values, axis=-1, keepdims=True))
    variance = lax.optimization_barrier(jnp.mean(centered * centered, axis=-1, keepdims=True))
    return centered * lax.rsqrt(variance + epsilon) * norm_gain + norm_shift

def positions(patch_index, feature_width):
    grid_row = (patch_index // GRID).astype(jnp.float32)
    grid_column = (patch_index % GRID).astype(jnp.float32)
    quarter = feature_width // 4
    frequency = 1.0 / 10000.0 ** (jnp.arange(quarter).astype(jnp.float32) / quarter)
    row_angle = grid_row[..., None] * frequency
    column_angle = grid_column[..., None] * frequency
    return jnp.concatenate([jnp.sin(row_angle), jnp.cos(row_angle), jnp.sin(column_angle), jnp.cos(column_angle)], axis=-1)

def project(inputs, matrix):
    return jnp.einsum('gtk,kn->gtn', inputs, matrix, precision=highest)

def block_forward(params, latent_rows, query_rows, index_rows):
    weight_query, bias_query, weight_key, weight_value, bias_value, weight_out, bias_out, gain_query, shift_query, gain_key, gain_value, shift_value, scale_attention, weight_up, bias_up, weight_down, bias_down, gain_feed, shift_feed, scale_feed = params
    group = query_rows.shape[0]
    visible_pos = positions(index_rows[:, :VISIBLE], D)
    masked_pos = positions(index_rows[:, VISIBLE:], D)
    query_normed = low(normalize(query_rows + masked_pos, gain_query, shift_query))
    kv_rows = jnp.concatenate([latent_rows, query_rows], axis=1)
    kv_pos = jnp.concatenate([visible_pos, masked_pos], axis=1)
    key_normed = low(normalize(kv_rows + kv_pos, gain_key, 0.0))
    value_normed = low(normalize(kv_rows, gain_value, shift_value))
    query_proj = low_back(low(project(query_normed, weight_query) + bias_query))
    key_proj = low_back(low(project(key_normed, weight_key)))
    value_proj = low_back(low(project(value_normed, weight_value) + bias_value))
    query_heads = query_proj.reshape(group, MASKED, HEADS, HEAD_DIM)
    key_heads = key_proj.reshape(group, PATCHES, HEADS, HEAD_DIM)
    value_heads = value_proj.reshape(group, PATCHES, HEADS, HEAD_DIM)
    scores = low_back(jnp.einsum('gmhe,gnhe->ghmn', query_heads, key_heads, precision=highest) * HEAD_DIM ** (-0.5))
    probs = low(jax.nn.softmax(scores, axis=-1))
    attended = low_back(low(jnp.einsum('ghmn,gnhe->gmhe', probs, value_heads, precision=highest)))
    attended = attended.reshape(group, MASKED, D)
    branch = low_back(project(attended, weight_out) + bias_out)
    middle = query_rows + scale_attention * branch
    feed_normed = low(normalize(middle, gain_feed, shift_feed))
    raised = low_back(project(feed_normed, weight_up) + bias_up)
    activated = low(jax.nn.gelu(raised, approximate=False))
    lowered = low_back(project(activated, weight_down) + bias_down)
    return middle + scale_feed * lowered

def reference(latents, queries, order, weight_query, bias_query, weight_key, weight_value, bias_value, weight_out, bias_out, gain_query, shift_query, gain_key, gain_value, shift_value, scale_attention, weight_up, bias_up, weight_down, bias_down, gain_feed, shift_feed, scale_feed, cotangent):
    params = tuple((entry.astype(jnp.float32) for entry in (weight_query, bias_query, weight_key, weight_value, bias_value, weight_out, bias_out, gain_query, shift_query, gain_key, gain_value, shift_value, scale_attention, weight_up, bias_up, weight_down, bias_down, gain_feed, shift_feed, scale_feed)))
    group = math.gcd(CROPS, 16)
    blocks = CROPS // group
    grouped_order = order.reshape(blocks, group, PATCHES)

    def forward(weights, latent_input, query_input):

        def one_group(inputs):
            latent_rows, query_rows, index_rows = inputs
            return block_forward(weights, latent_rows, query_rows, index_rows)
        outputs = lax.map(jax.checkpoint(one_group), (latent_input.reshape(blocks, group, VISIBLE, D), query_input.reshape(blocks, group, MASKED, D), grouped_order))
        return outputs.reshape(CROPS, MASKED, D)
    result, pullback = jax.vjp(forward, params, latents.astype(jnp.float32), queries.astype(jnp.float32))
    param_grads, latent_grad, query_grad = pullback(cotangent.astype(jnp.float32))
    return (result.astype(jnp.bfloat16), latent_grad, query_grad, param_grads[0], param_grads[1], param_grads[2], param_grads[3], param_grads[4], param_grads[5], param_grads[6], param_grads[7], param_grads[8], param_grads[9], param_grads[10], param_grads[11], param_grads[12], param_grads[13], param_grads[14], param_grads[15], param_grads[16], param_grads[17], param_grads[18], param_grads[19])
```

```python
import jax
import jax.numpy as jnp
from jax import lax
from jax.sharding import PartitionSpec as P

HEADS = 12
GRID = 14


epsilon = 1e-06


def normalize(values, norm_gain, norm_shift):
    centered = values - jnp.mean(values, axis=-1, keepdims=True)
    variance = jnp.mean(centered * centered, axis=-1, keepdims=True)
    return centered * lax.rsqrt(variance + epsilon) * norm_gain + norm_shift


def normalize_plain(values, norm_gain):
    return normalize(values, norm_gain, 0.0)


def exact_gelu(values):
    return jax.nn.gelu(values, approximate=False)


def positions(patch_index, feature_width):
    grid_row = (patch_index // GRID).astype(jnp.float32)
    grid_column = (patch_index % GRID).astype(jnp.float32)
    quarter = feature_width // 4
    frequency = 1.0 / 10000.0 ** (jnp.arange(quarter).astype(jnp.float32) / quarter)
    row_angle = grid_row[..., None] * frequency
    column_angle = grid_column[..., None] * frequency
    return jnp.concatenate(
        [jnp.sin(row_angle), jnp.cos(row_angle), jnp.sin(column_angle), jnp.cos(column_angle)],
        axis=-1,
    )


def project(inputs, matrix):
    return jnp.einsum("ctk,kn->ctn", inputs, matrix, preferred_element_type=jnp.float32)


def project_back(gradient, matrix):
    return jnp.einsum("ctn,kn->ctk", gradient, matrix, preferred_element_type=jnp.float32)


def outer_sum(inputs, gradient):
    return jnp.einsum("ctk,ctn->kn", inputs, gradient, preferred_element_type=jnp.float32)


def column_sum(values):
    return jnp.sum(values.astype(jnp.float32), axis=(0, 1))


def attention_scores(query_heads, key_heads, factor):
    return (
        jnp.einsum("cmhe,cnhe->chmn", query_heads, key_heads, preferred_element_type=jnp.float32)
        * factor
    )


class Net:
    def __init__(self):
        batch = lax.axis_size("batch")
        self.ring = batch // 4
        self.count = batch * lax.axis_size("query")
        index = lax.axis_index("batch")
        self.at_ring, self.at_x, self.at_core = index // 4, (index // 2) % 2, index % 2
        self.at_y = lax.axis_index("query")
        self.swaps = {"x": (self.swap_x, self.at_x), "y": (self.swap_y, self.at_y), "core": (self.swap_core, self.at_core)}

    def over_batch(self, values, target):
        return lax.ppermute(values, "batch", [(b, target(b)) for b in range(4 * self.ring)])

    def turn(self, values, step):
        return self.over_batch(values, lambda b: (b + 4 * step) % (4 * self.ring))

    def swap_x(self, values):
        return self.over_batch(values, lambda b: b ^ 2)

    def swap_core(self, values):
        return self.over_batch(values, lambda b: b ^ 1)

    def swap_y(self, values):
        return lax.ppermute(values, "query", [(0, 1), (1, 0)])

    def join(self, values, name, axis):
        swap, at = self.swaps[name]
        other = swap(values)
        first = jnp.where(at == 0, values, other)
        last = jnp.where(at == 0, other, values)
        return jnp.stack([first, last], axis=axis)

    def gather(self, part_a, part_b):
        rows = part_a.shape[0]
        own = jnp.concatenate([part_a, part_b])
        ringed = jnp.zeros((self.ring,) + own.shape, own.dtype)
        ringed = lax.dynamic_update_index_in_dim(ringed, own, self.at_ring, 0)
        for step in range(1, self.ring):
            came = self.turn(own, step)
            ringed = lax.dynamic_update_index_in_dim(ringed, came, (self.at_ring - step) % self.ring, 0)
        one = self.join(ringed[:, :rows], "x", 1)
        two = self.join(ringed[:, rows:], "y", 1)
        one = self.join(one, "y", 2)
        two = self.join(two, "x", 1)
        one = self.join(one, "core", 2)
        two = self.join(two, "core", 2)
        return one.reshape((self.count,) + one.shape[4:]), two.reshape((self.count,) + two.shape[4:])

    def halve(self, values, name, axis):
        swap, at = self.swaps[name]
        away = lax.dynamic_index_in_dim(values, 1 - at, axis, keepdims=False)
        keep = lax.dynamic_index_in_dim(values, at, axis, keepdims=False)
        return (keep.astype(jnp.float32) + swap(away).astype(jnp.float32)).astype(values.dtype)

    def scatter(self, part_a, part_b):
        split = lambda part: part.reshape((self.ring, 2, 2, 2) + part.shape[1:])
        one, two = split(part_a), split(part_b)
        one = self.halve(one, "core", 2)
        two = self.halve(two, "core", 2)
        one = self.halve(one, "x", 1)
        two = self.halve(two, "y", 2)
        one = self.halve(one, "y", 1)
        two = self.halve(two, "x", 1)
        rows = one.shape[1]
        ringed = jnp.concatenate([one, two], axis=1)
        total = lax.dynamic_index_in_dim(ringed, self.at_ring, 0, keepdims=False).astype(jnp.float32)
        for step in range(1, self.ring):
            away = lax.dynamic_index_in_dim(ringed, (self.at_ring + step) % self.ring, 0, keepdims=False)
            total = total + self.turn(away, step).astype(jnp.float32)
        return total[:rows], total[rows:]


def local(
    latents,
    queries,
    order,
    weight_query,
    bias_query,
    weight_key,
    weight_value,
    bias_value,
    weight_out,
    bias_out,
    gain_query,
    shift_query,
    gain_key,
    gain_value,
    shift_value,
    scale_attention,
    weight_up,
    bias_up,
    weight_down,
    bias_down,
    gain_feed,
    shift_feed,
    scale_feed,
    cotangent,
):
    net = Net()
    query_slot = lax.axis_index("query")
    crops_all, visible_half, _ = latents.shape
    masked_half = queries.shape[1]
    mine = crops_all // 2
    packed = jnp.concatenate([latents, queries, cotangent], axis=1)
    keep = lax.dynamic_slice_in_dim(packed, query_slot * mine, mine, 0)
    away = lax.dynamic_slice_in_dim(packed, (1 - query_slot) * mine, mine, 0)
    came = net.swap_y(away)
    order_mine = lax.dynamic_slice_in_dim(order, query_slot * mine, mine, 0)

    def both(first, last):
        parts = (keep[:, first:last], came[:, first:last])
        return jnp.concatenate(
            [jnp.where(query_slot == 0, parts[0], parts[1]), jnp.where(query_slot == 0, parts[1], parts[0])], axis=1
        )

    latents = both(0, visible_half)
    queries = both(visible_half, visible_half + masked_half)
    cotangent = both(visible_half + masked_half, visible_half + 2 * masked_half)
    shard, feature_width = weight_query.shape
    small = (
        bias_query, bias_value, bias_out, gain_query, shift_query, gain_key, gain_value, shift_value,
        scale_attention, bias_down, gain_feed, shift_feed, scale_feed, bias_up,
    )
    line = jnp.concatenate(small)
    line = jnp.pad(line, (0, 8 * feature_width - line.shape[0])).reshape(8, feature_width)
    group_a = net.gather(jnp.concatenate([weight_query, weight_key, line]), jnp.concatenate([weight_value, weight_out]))
    group_b = net.gather(weight_up.reshape(-1, feature_width)[: 2 * shard], weight_up.reshape(-1, feature_width)[2 * shard :])
    group_c = net.gather(weight_down[: 2 * shard], weight_down[2 * shard :])
    whole = lambda part: part.reshape(-1, part.shape[-1])
    query_matrix = whole(group_a[0][:, :shard])
    key_matrix = whole(group_a[0][:, shard : 2 * shard])
    value_matrix = whole(group_a[1][:, :shard])
    out_matrix = whole(group_a[1][:, shard:])
    lines = group_a[0][:, 2 * shard :].reshape(net.count, -1)
    small_whole = []
    at = 0
    for entry in small:
        small_whole.append(lines[:, at : at + entry.shape[0]].reshape(-1))
        at += entry.shape[0]
    (
        query_bias, value_bias, out_bias, query_gain, query_shift, key_gain, value_gain, value_shift,
        attend_scale, down_bias, feed_gain, feed_shift, feed_scale, up_bias,
    ) = small_whole
    up_matrix = jnp.concatenate(group_b, axis=1).reshape(feature_width, -1)
    down_matrix = jnp.concatenate(group_c, axis=1).reshape(-1, feature_width)
    query_bias = query_bias.astype(jnp.float32)
    value_bias = value_bias.astype(jnp.float32)
    out_bias = out_bias.astype(jnp.float32)
    query_gain = query_gain.astype(jnp.float32)
    query_shift = query_shift.astype(jnp.float32)
    key_gain = key_gain.astype(jnp.float32)
    value_gain = value_gain.astype(jnp.float32)
    value_shift = value_shift.astype(jnp.float32)
    attend_scale = attend_scale.astype(jnp.float32)
    head_size = feature_width // HEADS
    factor = head_size ** (-0.5)
    latent_work, query_work, cotangent_work = (latents, queries, cotangent)
    crops = queries.shape[0]
    visible_half = latents.shape[1]
    masked_half = queries.shape[1]
    visible_index = order_mine[:, :visible_half]
    masked_index = order_mine[:, visible_half:]
    visible_pos = positions(visible_index, feature_width)
    masked_pos = positions(masked_index, feature_width)
    query_input = query_work.astype(jnp.float32)
    latent_input = latent_work.astype(jnp.float32)
    own_rows = jnp.concatenate([latent_input, query_input], axis=1)
    own_pos = jnp.concatenate([visible_pos, masked_pos], axis=1)
    query_normed_full, query_pull = jax.vjp(
        normalize, query_input + masked_pos, query_gain, query_shift
    )
    key_normed_full, key_pull = jax.vjp(normalize_plain, own_rows + own_pos, key_gain)
    value_normed_full, value_pull = jax.vjp(normalize, own_rows, value_gain, value_shift)
    query_normed = query_normed_full.astype(jnp.bfloat16)
    key_normed = key_normed_full.astype(jnp.bfloat16)
    value_normed = value_normed_full.astype(jnp.bfloat16)
    query_proj = (project(query_normed, query_matrix) + query_bias).astype(jnp.bfloat16)
    key_own = project(key_normed, key_matrix).astype(jnp.bfloat16)
    value_own = (project(value_normed, value_matrix) + value_bias).astype(jnp.bfloat16)
    up_bias = up_bias.astype(jnp.float32)
    down_bias = down_bias.astype(jnp.float32)
    feed_gain = feed_gain.astype(jnp.float32)
    feed_shift = feed_shift.astype(jnp.float32)
    feed_scale = feed_scale.astype(jnp.float32)
    key_all, value_all = key_own, value_own
    query_heads = query_proj.reshape(crops, masked_half, HEADS, head_size)
    key_heads = key_all.reshape(crops, -1, HEADS, head_size)
    value_heads = value_all.reshape(crops, -1, HEADS, head_size)
    scores = attention_scores(query_heads, key_heads, factor)
    top_score = jnp.max(scores, axis=-1, keepdims=True)
    log_total = top_score + jnp.log(jnp.sum(jnp.exp(scores - top_score), axis=-1, keepdims=True))
    probs_low = jnp.exp(scores - log_total).astype(jnp.bfloat16)
    attended = jnp.einsum(
        "chmn,cnhe->cmhe", probs_low, value_heads, preferred_element_type=jnp.float32
    )
    attended = attended.astype(jnp.bfloat16).reshape(crops, masked_half, feature_width)
    branch = project(attended, out_matrix) + out_bias
    middle = query_input + attend_scale * branch
    feed_normed_full, feed_pull = jax.vjp(normalize, middle, feed_gain, feed_shift)
    feed_normed = feed_normed_full.astype(jnp.bfloat16)
    raised = project(feed_normed, up_matrix) + up_bias
    activated_full, gelu_pull = jax.vjp(exact_gelu, raised)
    activated = activated_full.astype(jnp.bfloat16)
    lowered = project(activated, down_matrix) + down_bias
    mixed_full = middle + feed_scale * lowered
    upstream = cotangent_work.astype(jnp.float32)
    lowered_grad = (feed_scale * upstream).astype(jnp.bfloat16)
    scale_feed_term = jnp.sum(upstream * lowered, axis=(0, 1))
    bias_down_term = column_sum(lowered_grad)
    weight_down_term = outer_sum(activated, lowered_grad)
    raised_grad = gelu_pull(project_back(lowered_grad, down_matrix))[0].astype(jnp.bfloat16)
    bias_up_term = column_sum(raised_grad)
    weight_up_term = outer_sum(feed_normed, raised_grad)
    middle_part, gain_feed_term, shift_feed_term = feed_pull(project_back(raised_grad, up_matrix))
    middle_grad = upstream + middle_part
    pieces = lambda term: term.astype(jnp.bfloat16).reshape(net.count, -1, feature_width)
    down_pieces = pieces(weight_down_term)
    down_sum = jnp.concatenate(net.scatter(down_pieces[:, : 2 * shard], down_pieces[:, 2 * shard :]))
    up_pieces = pieces(weight_up_term)
    up_sum = jnp.concatenate(net.scatter(up_pieces[:, : 2 * shard], up_pieces[:, 2 * shard :])).reshape(shard, -1)
    branch_grad = (attend_scale * middle_grad).astype(jnp.bfloat16)
    scale_attention_term = jnp.sum(middle_grad * branch, axis=(0, 1))
    bias_out_term = column_sum(branch_grad)
    weight_out_term = outer_sum(attended, branch_grad)
    attended_grad = project_back(branch_grad, out_matrix).astype(jnp.bfloat16)
    attended_heads = attended_grad.reshape(crops, masked_half, HEADS, head_size)
    scores_again = attention_scores(query_heads, key_heads, factor)
    probs_again = jnp.exp(scores_again - log_total)
    probs_again_low = probs_again.astype(jnp.bfloat16)
    probs_grad = jnp.einsum(
        "cmhe,cnhe->chmn", attended_heads, value_heads, preferred_element_type=jnp.float32
    )
    score_grad = (
        probs_again * (probs_grad - jnp.sum(probs_grad * probs_again, axis=-1, keepdims=True))
    ).astype(jnp.bfloat16)
    query_grad = (
        jnp.einsum("chmn,cnhe->cmhe", score_grad, key_heads, preferred_element_type=jnp.float32)
        * factor
    ).astype(jnp.bfloat16)
    query_grad = query_grad.reshape(crops, masked_half, feature_width)
    key_part = (
        jnp.einsum("chmn,cmhe->cnhe", score_grad, query_heads, preferred_element_type=jnp.float32)
        * factor
    ).reshape(crops, -1, feature_width)
    value_part = jnp.einsum(
        "chmn,cmhe->cnhe", probs_again_low, attended_heads, preferred_element_type=jnp.float32
    ).reshape(crops, -1, feature_width)
    key_sum, value_sum = key_part, value_part
    key_grad = key_sum.astype(jnp.bfloat16)
    value_grad = value_sum.astype(jnp.bfloat16)
    weight_query_term = outer_sum(query_normed, query_grad)
    bias_query_term = column_sum(query_grad)
    weight_key_term = outer_sum(key_normed, key_grad)
    weight_value_term = outer_sum(value_normed, value_grad)
    bias_value_term = column_sum(value_grad)
    query_input_part, gain_query_term, shift_query_term = query_pull(
        project_back(query_grad, query_matrix)
    )
    own_from_key, gain_key_term = key_pull(project_back(key_grad, key_matrix))
    own_from_value, gain_value_term, shift_value_term = value_pull(
        project_back(value_grad, value_matrix)
    )
    own_grad = own_from_key + own_from_value
    latents_work_grad = own_grad[:, :visible_half]
    queries_work_grad = middle_grad + query_input_part + own_grad[:, visible_half:]
    small_terms = (
        bias_query_term, bias_value_term, bias_out_term, gain_query_term, shift_query_term, gain_key_term,
        gain_value_term, shift_value_term, scale_attention_term, bias_down_term, gain_feed_term, shift_feed_term,
        scale_feed_term, bias_up_term,
    )
    lines = jnp.concatenate([term.reshape(net.count, -1) for term in small_terms], axis=1)
    lines = jnp.pad(lines, ((0, 0), (0, 8 * feature_width - lines.shape[1]))).reshape(net.count, 8, feature_width)
    sum_a, sum_b = net.scatter(
        jnp.concatenate([pieces(weight_query_term), pieces(weight_key_term), lines.astype(jnp.bfloat16)], axis=1),
        jnp.concatenate([pieces(weight_value_term), pieces(weight_out_term)], axis=1),
    )
    small_sums = []
    at = 0
    line = sum_a[2 * shard :].reshape(-1)
    for entry in small:
        small_sums.append(line[at : at + entry.shape[0]])
        at += entry.shape[0]

    def split(rows, half):
        keep = lax.dynamic_slice_in_dim(rows, query_slot * half, half, 1)
        away = lax.dynamic_slice_in_dim(rows, (1 - query_slot) * half, half, 1)
        return keep, away

    keeps, aways = zip(
        split(mixed_full.astype(jnp.bfloat16), masked_half // 2),
        split(latents_work_grad, visible_half // 2),
        split(queries_work_grad, masked_half // 2),
    )
    away = jnp.concatenate([part.astype(jnp.bfloat16) for part in aways], axis=1)
    came = net.swap_y(away)
    at = 0
    results = []
    for part in keeps:
        other = came[:, at : at + part.shape[1]].astype(part.dtype)
        at += part.shape[1]
        first = jnp.where(query_slot == 0, part, other)
        last = jnp.where(query_slot == 0, other, part)
        results.append(jnp.concatenate([first, last], axis=0))
    return (
        results[0],
        results[1],
        results[2],
        sum_a[:shard],
        small_sums[0],
        sum_a[shard : 2 * shard],
        sum_b[:shard],
        small_sums[1],
        sum_b[shard:],
        small_sums[2],
        small_sums[3],
        small_sums[4],
        small_sums[5],
        small_sums[6],
        small_sums[7],
        small_sums[8],
        up_sum,
        small_sums[13],
        down_sum,
        small_sums[9],
        small_sums[10],
        small_sums[11],
        small_sums[12],
    )


def solution(mesh):
    in_specs = (
        P("batch", "query", None),
        P("batch", "query", None),
        P("batch", None),
        P(("batch", "query"), None),
        P(("batch", "query")),
        P(("batch", "query"), None),
        P(("batch", "query"), None),
        P(("batch", "query")),
        P(("batch", "query"), None),
        P(("batch", "query")),
        P(("batch", "query")),
        P(("batch", "query")),
        P(("batch", "query")),
        P(("batch", "query")),
        P(("batch", "query")),
        P(("batch", "query")),
        P(("batch", "query"), None),
        P(("batch", "query")),
        P(("batch", "query"), None),
        P(("batch", "query")),
        P(("batch", "query")),
        P(("batch", "query")),
        P(("batch", "query")),
        P("batch", "query", None),
    )
    out_specs = (
        P("batch", "query", None),
        P("batch", "query", None),
        P("batch", "query", None),
        P(("batch", "query"), None),
        P(("batch", "query")),
        P(("batch", "query"), None),
        P(("batch", "query"), None),
        P(("batch", "query")),
        P(("batch", "query"), None),
        P(("batch", "query")),
        P(("batch", "query")),
        P(("batch", "query")),
        P(("batch", "query")),
        P(("batch", "query")),
        P(("batch", "query")),
        P(("batch", "query")),
        P(("batch", "query"), None),
        P(("batch", "query")),
        P(("batch", "query"), None),
        P(("batch", "query")),
        P(("batch", "query")),
        P(("batch", "query")),
        P(("batch", "query")),
    )
    return jax.shard_map(local, mesh=mesh, in_specs=in_specs, out_specs=out_specs, check_vma=False)
```

```python
import functools
import math

import jax
import jax.numpy as jnp
import ml_dtypes
import numpy as np
from jax import lax
from jax.experimental import pallas as pl
from jax.experimental.pallas import tpu as pltpu
from jax.sharding import PartitionSpec as P

HEADS = 12
GRID = 14
GROUP = 4
EPSILON = 1e-06
BIAS_QUERY = 0
BIAS_VALUE = 1
BIAS_OUT = 2
GAIN_QUERY = 3
SHIFT_QUERY = 4
GAIN_KEY = 5
GAIN_VALUE = 6
SHIFT_VALUE = 7
SCALE_ATTENTION = 8
BIAS_DOWN = 9
GAIN_FEED = 10
SHIFT_FEED = 11
SCALE_FEED = 12
SMALLS = 13
BIAS_ROW = 16
LINE_ROWS = 24
ANY = pl.ANY
SMEM = pltpu.SMEM


class Net:
    def __init__(self):
        batch = lax.axis_size("batch")
        self.ring = batch // 4
        self.units = batch
        self.count = batch * lax.axis_size("query")
        index = lax.axis_index("batch")
        self.at_ring, self.at_x, self.at_core = index // 4, (index // 2) % 2, index % 2
        self.at_y = lax.axis_index("query")
        slot = jnp.arange(batch)
        core, x, step = slot // (2 * self.ring), (slot // self.ring) % 2, slot % self.ring
        rest = 2 * (x ^ self.at_x) + (core ^ self.at_core)
        self.gathered = (4 * ((self.at_ring - step) % self.ring) + rest).astype(jnp.int32)
        self.scattered = (4 * ((self.at_ring + step) % self.ring) + rest).astype(jnp.int32)

    def over_batch(self, values, target):
        return lax.ppermute(values, "batch", [(b, target(b)) for b in range(self.units)])

    def turn(self, values, step):
        return self.over_batch(values, lambda b: (b + 4 * step) % self.units)

    def turns(self, values):
        return [values] + [self.turn(values, step) for step in range(1, self.ring)]

    def swap_x(self, values):
        return self.over_batch(values, lambda b: b ^ 2)

    def swap_core(self, values):
        return self.over_batch(values, lambda b: b ^ 1)

    def swap_y(self, values):
        return lax.ppermute(values, "query", [(0, 1), (1, 0)])

    def pair(self, own, came, tiles):
        first = jnp.where(self.at_y == 0, own, came)
        last = jnp.where(self.at_y == 0, came, own)
        slots, rows, width = own.shape
        both = jnp.stack([part.reshape(slots, tiles, -1, width) for part in (first, last)], axis=2)
        return jnp.moveaxis(both, 1, 0).reshape(tiles, slots, -1, width)

    def core_pairs(self, parts):
        return list(parts) + [self.swap_core(part) for part in parts]

    def aligned(self, parts):
        if parts[0].shape[2] % 16 == 0:
            return parts, self.gathered
        tiles, _, _, width = parts[0].shape
        back = jnp.zeros_like(self.gathered).at[self.gathered].set(jnp.arange(self.units, dtype=jnp.int32))
        whole = jnp.concatenate(parts, axis=1)[:, back].reshape(tiles, 16, -1, width)
        return [whole], jnp.arange(16, dtype=jnp.int32)

    def slots(self, rows):
        if rows // self.units % 16 == 0:
            return self.units, self.scattered
        return 16, jnp.arange(16, dtype=jnp.int32)

    def unaligned(self, keep, send):
        if keep.ndim == 5:
            return jnp.moveaxis(keep, 1, 2), jnp.moveaxis(send, 1, 2)
        tiles, _, _, width = keep.shape
        if keep.shape[1] * 2 != self.units or keep.shape[2] % 16 != 0:
            whole = jnp.concatenate([keep, send], axis=1).reshape(tiles, self.units, -1, width)[:, self.scattered]
            keep, send = whole[:, : self.units // 2], whole[:, self.units // 2 :]
        return [part.reshape(tiles, self.units // 2, 2, -1, width) for part in (keep, send)]

    def mine(self, part):
        return lax.dynamic_index_in_dim(part, self.at_y, 2, keepdims=False).astype(jnp.float32)

    def other(self, part):
        return lax.dynamic_index_in_dim(part, 1 - self.at_y, 2, keepdims=False).astype(jnp.float32)

    def scatter_first(self, part_a, part_b):
        (keep_a, send_a), (keep_b, send_b) = self.unaligned(*part_a), self.unaligned(*part_b)
        return keep_a, keep_b, self.swap_core(send_a), self.swap_core(send_b)

    def scatter_second(self, first):
        keep_a, keep_b, came_a, came_b = first
        ring, f32, low = self.ring, jnp.float32, jnp.bfloat16
        away_a = (keep_a[:, ring:].astype(f32) + came_a[:, ring:].astype(f32)).astype(low)
        away_b = (self.other(keep_b) + self.other(came_b)).astype(low)
        return first, self.swap_x(away_a), self.swap_y(away_b)

    def scatter_third(self, second):
        (keep_a, keep_b, came_a, came_b), next_a, next_b = second
        ring, f32, low = self.ring, jnp.float32, jnp.bfloat16
        keep_a, came_a = keep_a[:, :ring], came_a[:, :ring]
        away_a = (self.other(keep_a) + self.other(came_a) + self.other(next_a)).astype(low)
        base_b = self.mine(keep_b) + self.mine(came_b) + next_b.astype(f32)
        away_b = base_b[:, ring:].astype(low)
        base_a = self.mine(keep_a) + self.mine(came_a) + self.mine(next_a)
        return base_a, base_b[:, :ring], self.swap_y(away_a), self.swap_x(away_b)

    def scatter_fourth(self, third):
        base_a, base_b, last_a, last_b = third
        f32, low = jnp.float32, jnp.bfloat16
        sum_a, sum_b = base_a + last_a.astype(f32), base_b + last_b.astype(f32)
        flat = lambda part: part.reshape(-1, part.shape[-1])
        pieces = [jnp.concatenate([flat(sum_a[:, step]), flat(sum_b[:, step])]) for step in range(self.ring)]
        return sum_a, pieces[0], [self.turn(pieces[step].astype(low), step) for step in range(1, self.ring)]

    def scatter_last(self, fourth):
        like, total, came = fourth
        for piece in came:
            total = total + piece.astype(jnp.float32)
        shape = (like.shape[0],) + like.shape[2:]
        rows = shape[0] * shape[1]
        return total[:rows].reshape(shape), total[rows:]


def standard(values):
    centered = values - jnp.mean(values, axis=-1, keepdims=True)
    scale = lax.rsqrt(jnp.mean(centered * centered, axis=-1, keepdims=True) + EPSILON)
    return centered * scale, scale


def standard_back(grad, normed, scale, gain):
    slope = grad * gain
    inner = jnp.mean(slope * normed, axis=-1, keepdims=True)
    return (slope - jnp.mean(slope, axis=-1, keepdims=True) - normed * inner) * scale


def wide(ref):
    return ref[...].astype(jnp.float32)


def dot(left, right, left_dim=1, right_dim=0):
    return lax.dot_general(left, right, (((left_dim,), (right_dim,)), ((), ())), preferred_element_type=jnp.float32)


def rows_sum(values):
    return jnp.sum(values, axis=0, keepdims=True)


def by_head(rows):
    lane = lax.broadcasted_iota(jnp.int32, rows.shape, 1)
    head = rows.shape[1] // GROUP
    zero = jnp.zeros_like(rows)
    return jnp.concatenate(
        [jnp.where((lane >= head * h) & (lane < head * (h + 1)), rows, zero) for h in range(GROUP)], axis=0
    )


def from_heads(stacked):
    count = stacked.shape[0] // GROUP
    head = stacked.shape[1] // GROUP
    lane = lax.broadcasted_iota(jnp.int32, (count, stacked.shape[1]), 1)
    result = stacked[:count]
    for h in range(1, GROUP):
        result = jnp.where(lane >= head * h, stacked[count * h : count * (h + 1)], result)
    return result


def fetch(slots_ref, parts, tile, whole, sem):
    slot = 0
    for part in parts:
        rows = part.shape[2]
        for index in range(part.shape[1]):
            place = pl.multiple_of(slots_ref[slot] * rows, 16)
            pltpu.make_async_copy(part.at[tile, index], whole.at[pl.ds(place, rows)], sem).start()
            slot += 1


def store(slots_ref, whole, keep_ref, send_ref, tile, sem):
    slot = 0
    for part in (keep_ref, send_ref):
        rows = part.shape[-2]
        for index in range(part.shape[-3]):
            if len(part.shape) == 4:
                place = pl.multiple_of(slots_ref[slot] * rows, 16)
                pltpu.make_async_copy(whole.at[pl.ds(place, rows)], part.at[tile, index], sem).start()
            else:
                for half in range(2):
                    place = pl.multiple_of((2 * slots_ref[slot] + half) * rows, 16)
                    pltpu.make_async_copy(whole.at[pl.ds(place, rows)], part.at[tile, half, index], sem).start()
            slot += 1


def finish(whole, sem):
    pltpu.make_async_copy(whole, whole, sem).wait()


def layout(visible, masked):
    padded = -(-visible // 8) * 8
    starts = (0, masked, 2 * masked, 2 * masked + padded)
    return starts, -(-(2 * masked + 2 * padded) // 16) * 16


def prepare_kernel(
    place_ref, own_ref, came_ref, own_latent_ref, came_latent_ref, table_ref,
    key_ref, value_ref, key_scale_ref, value_scale_ref, rows_ref,
):
    starts, _ = layout(own_latent_ref.shape[1], own_ref.shape[1])
    rows_ref[...] = jnp.zeros_like(rows_ref)
    for start, ref in zip(starts, (own_ref, came_ref, own_latent_ref, came_latent_ref)):
        rows_ref[start : start + ref.shape[1]] = wide(ref.at[0])
    rows = rows_ref[...]
    place = place_ref[0]
    lane = lax.broadcasted_iota(jnp.int32, (rows.shape[0], table_ref.shape[0]), 1)
    wanted = jnp.where((lane & 16) == 0, place[:, 0:1], place[:, 1:2])
    chosen = jnp.where((lane & 15) == wanted, 1.0, 0.0).astype(jnp.bfloat16)
    position = dot(chosen, table_ref[...])
    key_ref[0], key_scale_ref[0] = standard(rows + position)
    value_ref[0], value_scale_ref[0] = standard(rows)


def attend_kernel(visible, factor, parts_a, parts_b, *refs):
    slots_ref, key_hat_ref, value_hat_ref, own_ref, came_ref, small_ref = refs[:6]
    part_a, part_b, refs = refs[6 : 6 + parts_a], refs[6 + parts_a : 6 + parts_a + parts_b], refs[6 + parts_a + parts_b :]
    query_ref, key_ref, value_ref, probs_ref, attended_ref, branch_ref, feed_hat_ref, feed_scale_ref, feed_ref = refs[-14:-5]
    query_w, key_w, value_w, out_w, sems = refs[-5:]

    @pl.when(pl.program_id(0) == 0)
    def _():
        for index, (parts, tile, whole) in enumerate(
            ((part_a, 0, query_w), (part_a, 1, key_w), (part_b, 0, value_w), (part_b, 1, out_w))
        ):
            fetch(slots_ref, parts, tile, whole, sems.at[index])
        for index, whole in enumerate((query_w, key_w, value_w, out_w)):
            finish(whole, sems.at[index])

    small = lambda row: small_ref[row : row + 1]
    count = attended_ref.shape[1]
    low = jnp.bfloat16
    query_normed = (key_hat_ref[0, :count] * small(GAIN_QUERY) + small(SHIFT_QUERY)).astype(low)
    key_normed = (key_hat_ref[0] * small(GAIN_KEY)).astype(low)
    value_normed = (value_hat_ref[0] * small(GAIN_VALUE) + small(SHIFT_VALUE)).astype(low)
    query_ref[0] = (dot(query_normed, query_w[...]) + small(BIAS_QUERY)).astype(low)
    key_ref[0] = dot(key_normed, key_w[...]).astype(low)
    value_ref[0] = (dot(value_normed, value_w[...]) + small(BIAS_VALUE)).astype(low)
    width = key_ref.shape[2] // probs_ref.shape[1]
    for quad in range(probs_ref.shape[1]):
        lanes = slice(width * quad, width * (quad + 1))
        scores = dot(key_ref[0, :, lanes], by_head(query_ref[0, :, lanes]), 1, 1) * factor
        row = lax.broadcasted_iota(jnp.int32, scores.shape, 0)
        starts, _ = layout(visible, own_ref.shape[1])
        real = (row < starts[2] + visible) | ((row >= starts[3]) & (row < starts[3] + visible))
        scores = jnp.where(real, scores, -1e30)
        raised = jnp.exp(scores - jnp.max(scores, axis=0, keepdims=True))
        probs = (raised * (1.0 / rows_sum(raised))).astype(low)
        probs_ref[0, quad] = probs
        attended_ref[0, :, lanes] = from_heads(dot(probs, value_ref[0, :, lanes], 0, 0)).astype(low)
    branch = dot(attended_ref[0], out_w[...]) + small(BIAS_OUT)
    branch_ref[0] = branch
    queries = jnp.concatenate([wide(own_ref.at[0]), wide(came_ref.at[0])], axis=0)
    hat, scale = standard(queries + small(SCALE_ATTENTION) * branch)
    feed_hat_ref[0] = hat
    feed_scale_ref[0] = scale
    feed_ref[0] = (hat * small(GAIN_FEED) + small(SHIFT_FEED)).astype(low)


def feed_kernel(last, parts_down, parts_up, *refs):
    slots_ref, out_slots_ref, feed_ref, cot_own_ref, cot_came_ref, small_ref = refs[:6]
    refs = refs[6:]
    if last:
        lowered_in, back_in, own_ref, came_ref, branch_ref, hat_ref, scale_ref = refs[:7]
        refs = refs[7:]
    part_down, refs = refs[:parts_down], refs[parts_down:]
    part_up, refs = refs[:parts_up], refs[parts_up:]
    down_w, up_w, down_grad, up_grad, sems = refs[-5:]
    refs = refs[-15:-5] if last else refs[-12:-5]
    down_keep, down_send, up_keep, up_send, bias_up_grad = refs[:5]
    low = jnp.bfloat16
    tiles = up_w.shape[0]
    width = down_w.shape[1]
    small = lambda row: small_ref[row : row + 1]
    fetch(slots_ref, part_up, 0, up_w.at[0], sems.at[0])
    fetch(slots_ref, part_down, 0, down_w, sems.at[tiles])
    for tile in range(1, tiles):
        fetch(slots_ref, part_up, tile, up_w.at[tile], sems.at[tile])

    def of_crops(first_ref, second_ref):
        parts = []
        for crop in range(first_ref.shape[0]):
            parts += [wide(first_ref.at[crop]), wide(second_ref.at[crop])]
        return jnp.concatenate(parts, axis=0)

    feed = feed_ref[...]
    feed_t = feed.T
    cotangent = of_crops(cot_own_ref, cot_came_ref)
    low_grad = (small(SCALE_FEED) * cotangent).astype(low)
    for tile in range(tiles):
        strip = slice(width * tile, width * (tile + 1))
        finish(up_w.at[tile], sems.at[tile])
        raised = dot(feed, up_w[tile]) + small(BIAS_ROW + last * tiles + tile)
        share = 0.5 * (1.0 + lax.erf(raised * (0.5**0.5)))
        activated = (raised * share).astype(low)
        slope = share + raised * jnp.exp(-0.5 * raised * raised) * ((2.0 * math.pi) ** -0.5)
        down_grad[strip] = dot(activated, low_grad, 0, 0).astype(low)
        if tile == tiles - 1:
            store(out_slots_ref, down_grad, down_keep, down_send, 0, sems.at[tiles + 1])
        if tile == 0:
            finish(down_w, sems.at[tiles])
        raised_grad = (dot(low_grad, down_w[strip], 1, 1) * slope).astype(low)
        up_grad[tile] = dot(feed_t, raised_grad).astype(low)
        store(out_slots_ref, up_grad.at[tile], up_keep, up_send, tile, sems.at[tiles + 2 + tile])
        bias_up_grad[tile : tile + 1] = rows_sum(raised_grad.astype(jnp.float32))
        more = dot(activated, down_w[strip])
        lowered = more if tile == 0 else lowered + more
        more = dot(raised_grad, up_w[tile], 1, 1)
        grad = more if tile == 0 else grad + more
    if last:
        lowered = lowered + lowered_in[...]
        grad = grad + back_in[...]
        mixed_own_ref, mixed_came_ref, middle_grad_ref, branch_grad_ref, sums_ref = refs[5:10]
        lowered = lowered + small(BIAS_DOWN)
        middle = of_crops(own_ref, came_ref) + small(SCALE_ATTENTION) * branch_ref[...]
        mixed = (middle + small(SCALE_FEED) * lowered).astype(low)
        half = mixed_own_ref.shape[1]
        for crop in range(mixed_own_ref.shape[0]):
            mixed_own_ref[crop] = mixed[2 * half * crop : 2 * half * crop + half]
            mixed_came_ref[crop] = mixed[2 * half * crop + half : 2 * half * (crop + 1)]
        hat = hat_ref[...]
        middle_grad = cotangent + standard_back(grad, hat, scale_ref[...], small(GAIN_FEED))
        middle_grad_ref[...] = middle_grad
        branch_grad = (small(SCALE_ATTENTION) * middle_grad).astype(low)
        branch_grad_ref[...] = branch_grad
        sums_ref[0:1] = rows_sum(cotangent * lowered)
        sums_ref[1:2] = rows_sum(low_grad.astype(jnp.float32))
        sums_ref[2:3] = rows_sum(grad * hat)
        sums_ref[3:4] = rows_sum(grad)
        sums_ref[4:5] = rows_sum(middle_grad * branch_ref[...])
        sums_ref[5:6] = rows_sum(branch_grad.astype(jnp.float32))
        sums_ref[6:8] = jnp.zeros_like(sums_ref[6:8])
    else:
        lowered_ref, back_ref = refs[5:7]
        lowered_ref[...] = lowered
        back_ref[...] = grad
    finish(down_grad, sems.at[tiles + 1])
    for tile in range(tiles):
        finish(up_grad.at[tile], sems.at[tiles + 2 + tile])


def attend_back_kernel(factor, parts_b, *refs):
    slots_ref, branch_grad_ref, query_ref, key_ref, value_ref, probs_ref = refs[:6]
    part_b = refs[6 : 6 + parts_b]
    query_grad, key_grad, value_grad, out_w, sem = refs[-5:]

    @pl.when(pl.program_id(0) == 0)
    def _():
        fetch(slots_ref, part_b, 1, out_w, sem)
        finish(out_w, sem)

    low = jnp.bfloat16
    above = dot(branch_grad_ref[0], out_w[...], 1, 1).astype(low)
    width = key_ref.shape[2] // probs_ref.shape[1]
    for quad in range(probs_ref.shape[1]):
        lanes = slice(width * quad, width * (quad + 1))
        probs_low = probs_ref[0, quad]
        probs = probs_low.astype(jnp.float32)
        heads = by_head(above[:, lanes])
        probs_grad = dot(value_ref[0, :, lanes], heads, 1, 1)
        inner = rows_sum(probs_grad * probs)
        score_grad = (probs * (probs_grad - inner)).astype(low)
        value_grad[0, :, lanes] = dot(probs_low, heads).astype(low)
        key_grad[0, :, lanes] = (dot(score_grad, by_head(query_ref[0, :, lanes])) * factor).astype(low)
        query_grad[0, :, lanes] = (from_heads(dot(score_grad, key_ref[0, :, lanes], 0, 0)) * factor).astype(low)


def input_back_kernel(parts_a, parts_b, *refs):
    slots_ref, query_grad, key_grad, value_grad, key_hat_ref, value_hat_ref, key_scale_ref, value_scale_ref = refs[:8]
    middle_grad_ref, small_ref = refs[8:10]
    part_a, part_b, refs = refs[10 : 10 + parts_a], refs[10 + parts_a : 10 + parts_a + parts_b], refs[10 + parts_a + parts_b :]
    masked_refs, latent_refs, (sums_ref, query_w, key_w, value_w, sems) = refs[-9:-7], refs[-7:-5], refs[-5:]

    @pl.when(pl.program_id(0) == 0)
    def _():
        for index, (parts, tile, whole) in enumerate(((part_a, 0, query_w), (part_a, 1, key_w), (part_b, 0, value_w))):
            fetch(slots_ref, parts, tile, whole, sems.at[index])
        for index, whole in enumerate((query_w, key_w, value_w)):
            finish(whole, sems.at[index])

    small = lambda row: small_ref[row : row + 1]
    count = query_grad.shape[1]

    @pl.when(pl.program_id(0) == 0)
    def _():
        sums_ref[...] = jnp.zeros_like(sums_ref)

    key_hat, key_scale = key_hat_ref[0], key_scale_ref[0]
    query_hat = key_hat[:count]
    value_hat = value_hat_ref[0]
    from_query = dot(query_grad[0], query_w[...], 1, 1)
    from_key = dot(key_grad[0], key_w[...], 1, 1)
    from_value = dot(value_grad[0], value_w[...], 1, 1)
    sums_ref[0:1] += rows_sum(from_query * query_hat)
    sums_ref[1:2] += rows_sum(from_query)
    sums_ref[2:3] += rows_sum(from_key * key_hat)
    sums_ref[3:4] += rows_sum(from_value * value_hat)
    sums_ref[4:5] += rows_sum(from_value)
    sums_ref[5:6] += rows_sum(wide(query_grad.at[0]))
    sums_ref[6:7] += rows_sum(wide(value_grad.at[0]))
    both = standard_back(from_key, key_hat, key_scale, small(GAIN_KEY)) + standard_back(
        from_value, value_hat, value_scale_ref[0], small(GAIN_VALUE)
    )
    query_part = standard_back(from_query, query_hat, key_scale[:count], small(GAIN_QUERY))
    masked = middle_grad_ref[0] + query_part + both[:count]
    sizes = [ref.shape[1] for ref in (masked_refs[0], latent_refs[0])]
    starts, _ = layout(sizes[1], sizes[0])
    for index in range(2):
        ref = masked_refs[index]
        ref[0] = masked[starts[index] : starts[index] + sizes[0]].astype(ref.dtype)
        ref = latent_refs[index]
        ref[0] = both[starts[2 + index] : starts[2 + index] + sizes[1]].astype(ref.dtype)


def weights_back_kernel(*refs):
    out_slots_ref, query_grad, key_grad, value_grad, branch_grad, key_hat_ref, value_hat_ref, attended_ref, small_ref = refs[:9]
    keep_a, send_a, keep_b, send_b, query_out, key_out, value_out, out_out, sems = refs[-9:]
    small = lambda row: small_ref[row : row + 1]
    low = jnp.bfloat16
    crops = key_hat_ref.shape[0]
    count = query_grad.shape[0] // crops
    queries, keys, values = [], [], []
    for crop in range(crops):
        hat = key_hat_ref[crop]
        queries.append((hat[:count] * small(GAIN_QUERY) + small(SHIFT_QUERY)).astype(low))
        keys.append((hat * small(GAIN_KEY)).astype(low))
        values.append((value_hat_ref[crop] * small(GAIN_VALUE) + small(SHIFT_VALUE)).astype(low))
    join = lambda parts: jnp.concatenate(parts, axis=0)
    out_out[...] = dot(attended_ref[...], branch_grad[...], 0, 0).astype(low)
    store(out_slots_ref, out_out, keep_b, send_b, 1, sems.at[0])
    value_out[...] = dot(join(values), value_grad[...], 0, 0).astype(low)
    store(out_slots_ref, value_out, keep_b, send_b, 0, sems.at[1])
    key_out[...] = dot(join(keys), key_grad[...], 0, 0).astype(low)
    store(out_slots_ref, key_out, keep_a, send_a, 1, sems.at[2])
    query_out[...] = dot(join(queries), query_grad[...], 0, 0).astype(low)
    store(out_slots_ref, query_out, keep_a, send_a, 0, sems.at[3])
    for index, whole in enumerate((out_out, value_out, key_out, query_out)):
        finish(whole, sems.at[index])


def call(name, kernel, grid, ins, outs, operands, scratch=(), after=(), us=8):
    ins = list(ins) + [ANY] * len(after)
    operands = tuple(operands) + tuple(after)

    def spec(entry, shape):
        if entry is None:
            return pl.BlockSpec(shape, lambda *i: (0,) * len(shape))
        if entry is ANY or entry is SMEM:
            return pl.BlockSpec(memory_space=entry)
        return pl.BlockSpec(*entry)

    return pl.pallas_call(
        kernel,
        name=name,
        grid=grid,
        in_specs=[spec(entry, operand.shape) for entry, operand in zip(ins, operands, strict=True)],
        out_specs=[spec(entry, shape) for entry, shape, _ in outs],
        out_shape=[jax.ShapeDtypeStruct(shape, dtype) for _, shape, dtype in outs],
        scratch_shapes=list(scratch),
        compiler_params=pltpu.CompilerParams(vmem_limit_bytes=56 << 20),
        cost_estimate=pl.CostEstimate(flops=int(us * 1.1e9), bytes_accessed=int(us * 3.5e6), transcendentals=0),
    )(*operands)


def by_crop(shape):
    block = (1,) + tuple(shape[1:])
    return block, lambda i: (i,) + (0,) * (len(block) - 1)


def pack_kernel(vectors, *refs):
    *in_refs, out_ref = refs
    low = jnp.bfloat16
    parts = [wide(ref) for ref in in_refs[vectors + bool(vectors) :]]
    if vectors:
        device_ref, thin, bias_ref = in_refs[0], in_refs[1:vectors], in_refs[vectors]
        width = out_ref.shape[1]
        device = device_ref[0]
        shard, half = thin[0].shape[0], bias_ref.shape[0] // 2
        rows = jnp.concatenate(
            [pad_lanes(wide(ref).reshape(1, -1), 128) for ref in thin]
            + [jnp.zeros((BIAS_ROW - len(thin), 128), jnp.float32)], axis=0
        )
        value = lax.broadcasted_iota(jnp.int32, (128, width), 0)
        lane = lax.broadcasted_iota(jnp.int32, (128, width), 1)
        there = (lane == shard * device + value) & (value < shard)
        line = [dot(rows.astype(low), jnp.where(there, 1.0, 0.0).astype(low))]
        bias = jnp.broadcast_to(pad_lanes(wide(bias_ref).reshape(1, -1), 128), (8, 128)).astype(low)
        row = lax.broadcasted_iota(jnp.int32, (8, width), 0)
        across = width // half
        strips = jnp.zeros((8, width), jnp.float32)
        for part in range(2):
            inside = (value >= half * part) & (value < half * (part + 1))
            there = (lane == half * lax.rem(device, across) + value - half * part) & inside
            spot = row == lax.div(device, across) + part * ((LINE_ROWS - BIAS_ROW) // 4)
            strips = jnp.where(spot, dot(bias, jnp.where(there, 1.0, 0.0).astype(low)), strips)
        middle = len(parts) // 2
        parts = parts[:middle] + line + [strips] + parts[middle:]
    out_ref[...] = jnp.concatenate(parts, axis=0).astype(out_ref.dtype)


def pad_lanes(rows, width):
    if rows.shape[1] == width:
        return rows
    return jnp.concatenate([rows, jnp.zeros((rows.shape[0], width - rows.shape[1]), rows.dtype)], axis=1)


def pack(parts, device=None, vectors=()):
    width, dtype = parts[0].shape[1], parts[0].dtype
    first = (device.reshape(1), *vectors) if vectors else ()
    ins = [SMEM] + [None] * len(vectors) if vectors else []
    run = lambda operands: call(
        "pack", functools.partial(pack_kernel, len(vectors)), (), ins + [None] * len(operands),
        [(None, (sum(part.shape[0] for part in operands) + LINE_ROWS * bool(vectors), width), dtype)], (*first, *operands), us=1,
    )[0]
    if all(part.shape[0] % 8 == 0 for part in parts):
        return run(parts)
    if not vectors:
        return jnp.concatenate(parts)
    half = len(parts) // 2
    blank = jnp.zeros((8, width), dtype)
    line = run([blank, blank])[8 : 8 + LINE_ROWS]
    return jnp.concatenate([*parts[:half], line, *parts[half:]])


def stage(*values):
    return lax.optimization_barrier(values)


def position_table(width):
    quarter = width // 4
    frequency = 10000.0 ** (-np.arange(quarter) / quarter)
    angle = np.arange(16)[:, None] * frequency
    wave = np.concatenate([np.sin(angle), np.cos(angle)], axis=1)
    table = np.zeros((32, width))
    table[:16, : width // 2] = wave
    table[16:, width // 2 :] = wave
    table = table.astype(np.float32)
    high = table.astype(ml_dtypes.bfloat16)
    low = (table - high.astype(np.float32)).astype(ml_dtypes.bfloat16)
    return np.concatenate([high, low])


def local(
    latents, queries, order, weight_query, bias_query, weight_key, weight_value, bias_value, weight_out, bias_out,
    gain_query, shift_query, gain_key, gain_value, shift_value, scale_attention, weight_up, bias_up, weight_down,
    bias_down, gain_feed, shift_feed, scale_feed, cotangent,
):
    low = jnp.bfloat16
    net = Net()
    slot = lax.axis_index("query")
    crops = latents.shape[0] // 2
    visible, masked = latents.shape[1], queries.shape[1]
    shard, width = weight_query.shape
    count = net.count
    _, rows = layout(visible, masked)
    block = lambda values, which: lax.dynamic_slice_in_dim(values, which * crops, crops, 0)
    own_latents, own_queries, own_cot = [block(v, slot) for v in (latents, queries, cotangent)]
    own_order = block(order, slot)
    part = lambda start, size, which: lax.dynamic_slice_in_dim(own_order, start + which * size, size, 1)
    gap = jnp.full((crops, rows // 2 - masked - visible), -1, jnp.int32)
    indices = jnp.concatenate(
        [
            part(2 * visible, masked, slot), part(2 * visible, masked, 1 - slot),
            part(0, visible, slot), gap, part(0, visible, 1 - slot), gap,
        ],
        axis=1,
    )
    steps = jnp.stack([indices // GRID, jnp.where(indices < 0, -1, indices % GRID)], axis=-1)

    vectors = [
        bias_query, bias_value, bias_out, gain_query, shift_query, gain_key, gain_value, shift_value, scale_attention,
        bias_down, gain_feed, shift_feed, scale_feed, bias_up,
    ]
    device = (2 * lax.axis_index("batch") + slot).astype(jnp.int32)
    deep = weight_down.shape[0]
    ups = weight_up.reshape(shard, count, 2, deep // 2)
    up_tiles = count * deep // 2 // width
    flat = lambda values: values.reshape(-1, values.shape[-1])
    up_half = lambda k: flat(jnp.moveaxis(ups[:, :, k].reshape(shard, up_tiles, width), 1, 0))
    down_half = lambda k: weight_down[k * deep // 2 : (k + 1) * deep // 2]

    half = deep // 2
    f32 = jnp.float32
    own_a = pack([weight_query, weight_key, weight_value, weight_out], device, vectors)
    rings_a = net.turns(own_a)
    came_queries, came_latents = net.swap_y(block(queries, 1 - slot)), net.swap_y(block(latents, 1 - slot))
    own_b, own_c = [pack([down_half(k), up_half(k)]) for k in range(2)]
    away_cot = block(cotangent, 1 - slot)
    rings_a, came_queries, came_latents, own_b, own_c, away_cot, own_cot, steps, own_queries, own_latents = stage(
        rings_a, came_queries, came_latents, own_b, own_c, away_cot, own_cot, steps, own_queries, own_latents
    )

    cut = 2 * shard
    line = sum(piece[cut : cut + LINE_ROWS] for piece in rings_a[1:]) + rings_a[0][cut : cut + LINE_ROWS]
    one = jnp.concatenate([piece[:cut] for piece in rings_a] + [line])
    two = jnp.stack([piece[cut + LINE_ROWS :] for piece in rings_a])
    one_x, two_y = net.swap_x(one), net.swap_y(two)
    rings_b = net.turns(own_b)
    came_cot = net.swap_y(away_cot)
    crop_out = lambda shape, dtype: (by_crop(shape), shape, dtype)
    wide_shape, thin_shape = (crops, rows, width), (crops, rows, 1)
    table = jnp.asarray(position_table(width))
    operands = (steps, own_queries, came_queries, own_latents, came_latents, table)
    key_hat, value_hat, key_scale, value_scale = call(
        "prepare", prepare_kernel, (crops,), [by_crop(a.shape) for a in operands[:5]] + [None],
        [crop_out(wide_shape, f32)] * 2 + [crop_out(thin_shape, f32)] * 2, operands, scratch=[pltpu.VMEM((rows, width), f32)],
        us=1,
    )
    one, one_x, two, two_y, rings_b, own_c, came_cot, key_hat, value_hat, key_scale, value_scale = stage(
        one, one_x, two, two_y, rings_b, own_c, came_cot, key_hat, value_hat, key_scale, value_scale
    )

    ring = net.ring
    line = one[ring * cut :] + one_x[ring * cut :]
    one = jnp.concatenate([one[: ring * cut], one_x[: ring * cut], line])
    two = net.pair(two, two_y, 2)
    one_y, two_x = net.swap_y(one), net.swap_x(two)
    rings_c = net.turns(own_c)
    one, one_y, two, two_x, rings_b, rings_c = stage(one, one_y, two, two_x, rings_b, rings_c)

    line = one[2 * ring * cut :] + one_y[2 * ring * cut :]
    units = lambda values: values[: 2 * ring * cut].reshape(2 * ring, cut, width)
    one = net.pair(units(one), units(one_y), 2)
    part_a, part_b = net.core_pairs([one]), net.core_pairs([two, two_x])
    small = line.astype(f32) + net.swap_core(line).astype(f32)
    (part_a, places), (part_b, _) = net.aligned(part_a), net.aligned(part_b)
    pieces = list(zip(rings_b, rings_c))
    downs = jnp.stack([jnp.concatenate([b[:half], c[:half]]) for b, c in pieces])
    ups_all = jnp.stack([jnp.concatenate([b[half:], c[half:]]) for b, c in pieces])
    downs_x, ups_y = net.swap_x(downs), net.swap_y(ups_all)
    slots, out_places = net.slots(width)

    ask_shape = (crops, 2 * masked, width)
    dma = pltpu.SemaphoreType.DMA
    square_vmem = pltpu.VMEM((width, width), low)
    quads = HEADS // GROUP
    factor = (width // HEADS) ** -0.5
    probs_shape = (crops, quads, rows, GROUP * 2 * masked)
    operands = (places, key_hat, value_hat, own_queries, came_queries, small, *part_a, *part_b)
    parts = len(part_a) + len(part_b)
    query_p, key_p, value_p, probs, attended, branch, feed_hat, feed_scale, feed = call(
        "attend", functools.partial(attend_kernel, visible, factor, len(part_a), len(part_b)), (crops,),
        [SMEM] + [by_crop(a.shape) for a in operands[1:5]] + [None] + [ANY] * parts,
        [
            crop_out(ask_shape, low), crop_out(wide_shape, low), crop_out(wide_shape, low), crop_out(probs_shape, low),
            crop_out(ask_shape, low), crop_out(ask_shape, f32), crop_out(ask_shape, f32),
            crop_out((crops, 2 * masked, 1), f32), crop_out(ask_shape, low),
        ],
        operands, scratch=[square_vmem] * 4 + [dma((4,))], us=1,
    )
    downs, downs_x, ups_all, ups_y, query_p, key_p, value_p, probs, attended, branch, feed_hat, feed_scale, feed = stage(
        downs, downs_x, ups_all, ups_y, query_p, key_p, value_p, probs, attended, branch, feed_hat, feed_scale, feed
    )

    up_rows = up_tiles * shard
    thirds = []
    for k in range(2):
        one = jnp.concatenate([downs[:, half * k : half * (k + 1)], downs_x[:, half * k : half * (k + 1)]])
        two = net.pair(ups_all[:, up_rows * k : up_rows * (k + 1)], ups_y[:, up_rows * k : up_rows * (k + 1)], up_tiles)
        if k == 1:
            (one, two), thirds[0] = stage((one, two), thirds[0])
        thirds.append((one, net.swap_y(one), two, net.swap_x(two)))
    asks = crops * 2 * masked
    flat_shape = (asks, width)
    halves = lambda tiles, total: [(ANY, (tiles, slots // 2, total // slots, width), low)] * 2
    feed_grads = []
    lowered = back = None
    for k in range(2):
        one, one_y, two, two_x = thirds[k]
        if k == 1:
            (one, one_y, two, two_x), lowered, back, grads_b = stage((one, one_y, two, two_x), lowered, back, grads_b)
            first_b = net.scatter_first(*grads_b)
        one = net.pair(one, one_y, 1)
        (down_parts, _), (up_parts, _) = net.aligned(net.core_pairs([one])), net.aligned(net.core_pairs([two, two_x]))
        if k == 1:
            down_parts, up_parts, first_b = stage(down_parts, up_parts, first_b)
            second_b = net.scatter_second(first_b)
        last = k == 1
        operands = (places, out_places, flat(feed), own_cot, came_cot, small)
        if last:
            operands += (lowered, back, own_queries, came_queries, flat(branch), flat(feed_hat), flat(feed_scale))
        ins = [SMEM] * 2 + [None] * (len(operands) - 2) + [ANY] * (len(down_parts) + len(up_parts))
        down_outs = halves(1, up_tiles * width)
        if slots == net.units and half % 16 == 0:
            down_outs = [(ANY, (1, 2, slots // 2, half, width), low)] * 2
        outs = down_outs + halves(up_tiles, width) + [(None, (up_tiles, width), f32)]
        if last:
            half_shape = (crops, masked, width)
            outs += [(None, half_shape, low)] * 2
            outs += [(None, flat_shape, f32), (None, flat_shape, low), (None, (8, width), f32)]
        else:
            outs += [(None, flat_shape, f32), (None, flat_shape, f32)]
        tall, tiled = pltpu.VMEM((up_tiles * width, width), low), pltpu.VMEM((up_tiles, width, width), low)
        result = call(
            "feed" + str(k), functools.partial(feed_kernel, last, len(down_parts), len(up_parts)), (), ins, outs,
            operands + (*down_parts, *up_parts), scratch=[tall, tiled, tall, tiled, dma((2 * up_tiles + 2,))], us=1,
        )
        feed_grads.append(result[4])
        if last:
            mixed_own, mixed_came, middle_grad, branch_grad, feed_sums = result[5:]
            first_c = net.scatter_first(result[:2], result[2:4])
        else:
            lowered, back = result[5:]
            grads_b = (result[:2], result[2:4])
    branch_grad, middle_grad, second_b, mixed_came = stage(branch_grad, middle_grad, second_b, mixed_came)

    home_mixed = net.swap_y(mixed_came)
    third_b = net.scatter_third(second_b)
    operands = (places, branch_grad.reshape(ask_shape), query_p, key_p, value_p, probs, *part_b)
    query_grad, key_grad, value_grad = call(
        "attend_back", functools.partial(attend_back_kernel, factor, len(part_b)), (crops,),
        [SMEM] + [by_crop(a.shape) for a in operands[1:6]] + [ANY] * len(part_b),
        [crop_out(ask_shape, low), crop_out(wide_shape, low), crop_out(wide_shape, low)], operands,
        scratch=[square_vmem, dma(())], us=1,
    )
    query_grad, key_grad, value_grad, first_c, third_b, home_mixed = stage(
        query_grad, key_grad, value_grad, first_c, third_b, home_mixed
    )

    second_c = net.scatter_second(first_c)
    operands = (
        out_places, flat(query_grad), flat(key_grad), flat(value_grad), branch_grad, key_hat, value_hat, flat(attended), small
    )
    keep_a, send_a, keep_b, send_b = call(
        "weights_back", weights_back_kernel, (), [SMEM] + [None] * 8, halves(2, width) * 2, operands,
        scratch=[square_vmem] * 4 + [dma((4,))], us=1,
    )
    fourth_b = net.scatter_fourth(third_b)
    keep_a, send_a, keep_b, send_b, second_c, query_grad, key_grad, value_grad = stage(
        keep_a, send_a, keep_b, send_b, second_c, query_grad, key_grad, value_grad
    )

    first_a = net.scatter_first((keep_a, send_a), (keep_b, send_b))
    third_c = net.scatter_third(second_c)
    operands = (
        places, query_grad, key_grad, value_grad, key_hat, value_hat, key_scale, value_scale,
        middle_grad.reshape(ask_shape), small, *part_a, *part_b,
    )
    masked_shape, latent_shape = (crops, masked, width), (crops, visible, width)
    masked_own, masked_came, latent_own, latent_came, input_sums = call(
        "input_back", functools.partial(input_back_kernel, len(part_a), len(part_b)), (crops,),
        [SMEM] + [by_crop(a.shape) for a in operands[1:9]] + [None] + [ANY] * parts,
        [
            crop_out(masked_shape, f32), crop_out(masked_shape, low), crop_out(latent_shape, f32), crop_out(latent_shape, low),
            (None, (8, width), f32),
        ],
        operands, scratch=[square_vmem] * 3 + [dma((3,))], us=1,
    )
    lines = jnp.concatenate([input_sums, feed_sums, *feed_grads, jnp.zeros((LINE_ROWS - BIAS_ROW - 2 * up_tiles, width), f32)])
    masked_own, masked_came, latent_own, latent_came, lines, first_a, third_c = stage(
        masked_own, masked_came, latent_own, latent_came, lines, first_a, third_c
    )

    second_a = net.scatter_second(first_a)
    fourth_c = net.scatter_fourth(third_c)
    lines = net.turns(lines + net.swap_core(lines))
    second_a, lines = stage(second_a, lines)

    third_a = net.scatter_third(second_a)
    lines = sum(lines[1:], lines[0])
    lines = (lines, net.swap_y(lines))
    third_a, lines, masked_came, latent_came = stage(third_a, lines, masked_came, latent_came)

    fourth_a = net.scatter_fourth(third_a)
    home_masked, home_latent = net.swap_y(masked_came), net.swap_y(latent_came)
    lines = lines[0] + lines[1]
    lines = lines + net.swap_x(lines)
    sum_a, sum_b = net.scatter_last(fourth_a)
    sum_b = sum_b.reshape(sum_a.shape)
    feed_results = []
    for fourth in (fourth_b, fourth_c):
        down_sum, up_sum = net.scatter_last(fourth)
        feed_results.append((jnp.moveaxis(up_sum.reshape(up_tiles, shard, width), 0, 1).reshape(shard, count, deep // 2), down_sum[0]))
    vector = lax.dynamic_slice(lines, (0, shard * device), (BIAS_ROW, shard))
    across = width // half
    strip = lambda k: lax.dynamic_slice(lines, (BIAS_ROW + k * up_tiles + device // across, half * (device % across)), (1, half))
    bias_up_sum = jnp.concatenate([strip(0)[0], strip(1)[0]])
    up_sum = jnp.stack([up for up, _ in feed_results], axis=2).reshape(shard, count * deep)
    down_sum = jnp.concatenate([down for _, down in feed_results])

    def home(keep, came, dtype):
        keep, came = keep.astype(dtype), came.astype(dtype)
        return jnp.concatenate([jnp.where(slot == 0, keep, came), jnp.where(slot == 0, came, keep)], axis=0)

    return (
        home(mixed_own, home_mixed, low),
        home(latent_own, home_latent, f32),
        home(masked_own, home_masked, f32),
        sum_a[0],
        vector[5],
        sum_a[1],
        sum_b[0],
        vector[6],
        sum_b[1],
        vector[13],
        vector[0],
        vector[1],
        vector[2],
        vector[3],
        vector[4],
        vector[12],
        up_sum,
        bias_up_sum,
        down_sum,
        vector[9],
        vector[10],
        vector[11],
        vector[8],
    )


def solution(mesh):
    in_specs = (
        P("batch", "query", None),
        P("batch", "query", None),
        P("batch", None),
        P(("batch", "query"), None),
        P(("batch", "query")),
        P(("batch", "query"), None),
        P(("batch", "query"), None),
        P(("batch", "query")),
        P(("batch", "query"), None),
        P(("batch", "query")),
        P(("batch", "query")),
        P(("batch", "query")),
        P(("batch", "query")),
        P(("batch", "query")),
        P(("batch", "query")),
        P(("batch", "query")),
        P(("batch", "query"), None),
        P(("batch", "query")),
        P(("batch", "query"), None),
        P(("batch", "query")),
        P(("batch", "query")),
        P(("batch", "query")),
        P(("batch", "query")),
        P("batch", "query", None),
    )
    out_specs = (
        P("batch", "query", None),
        P("batch", "query", None),
        P("batch", "query", None),
        P(("batch", "query"), None),
        P(("batch", "query")),
        P(("batch", "query"), None),
        P(("batch", "query"), None),
        P(("batch", "query")),
        P(("batch", "query"), None),
        P(("batch", "query")),
        P(("batch", "query")),
        P(("batch", "query")),
        P(("batch", "query")),
        P(("batch", "query")),
        P(("batch", "query")),
        P(("batch", "query")),
        P(("batch", "query"), None),
        P(("batch", "query")),
        P(("batch", "query"), None),
        P(("batch", "query")),
        P(("batch", "query")),
        P(("batch", "query")),
        P(("batch", "query")),
    )
    return jax.shard_map(local, mesh=mesh, in_specs=in_specs, out_specs=out_specs, check_vma=False)
```

```python
import functools
import math

import jax
import jax.numpy as jnp
import ml_dtypes
import numpy as np
from jax import lax
from jax.experimental import pallas as pl
from jax.experimental.pallas import tpu as pltpu
from jax.sharding import Mesh
from jax.sharding import PartitionSpec as P

BATCH = ("ring", "x", "core")
HEADS = 12
GRID = 14
GROUP = 4
CHUNK = 768
EPSILON = 1e-06
BIAS_QUERY = 0
BIAS_VALUE = 1
BIAS_OUT = 2
GAIN_QUERY = 3
SHIFT_QUERY = 4
GAIN_KEY = 5
GAIN_VALUE = 6
SHIFT_VALUE = 7
SCALE_ATTENTION = 8
BIAS_DOWN = 9
GAIN_FEED = 10
SHIFT_FEED = 11
SCALE_FEED = 12
SMALLS = 13
BIAS_ROW = 16
LINE_ROWS = 24
ANY = pl.ANY
SMEM = pltpu.SMEM


class Net:
    def __init__(self):
        self.ring = lax.axis_size("ring")
        batch = 4 * self.ring
        self.units = batch
        self.count = batch * lax.axis_size("query")
        self.at_ring, self.at_x, self.at_core = lax.axis_index("ring"), lax.axis_index("x"), lax.axis_index("core")
        self.at_y = lax.axis_index("query")
        slot = jnp.arange(batch)
        core, x, step = slot // (2 * self.ring), (slot // self.ring) % 2, slot % self.ring
        rest = 2 * (x ^ self.at_x) + (core ^ self.at_core)
        self.gathered = (4 * ((self.at_ring - step) % self.ring) + rest).astype(jnp.int32)
        self.scattered = (4 * ((self.at_ring + step) % self.ring) + rest).astype(jnp.int32)

    def turn(self, values, step):
        return lax.ppermute(values, "ring", [(place, (place + step) % self.ring) for place in range(self.ring)])

    def turns(self, values):
        return [values] + [self.turn(values, step) for step in range(1, self.ring)]

    def swap_x(self, values):
        return lax.ppermute(values, "x", [(0, 1), (1, 0)])

    def swap_core(self, values):
        return lax.ppermute(values, "core", [(0, 1), (1, 0)])

    def swap_y(self, values):
        return lax.ppermute(values, "query", [(0, 1), (1, 0)])

    def pair(self, own, came, tiles):
        first = jnp.where(self.at_y == 0, own, came)
        last = jnp.where(self.at_y == 0, came, own)
        slots, rows, width = own.shape
        both = jnp.stack([part.reshape(slots, tiles, -1, width) for part in (first, last)], axis=2)
        return both.reshape(slots, tiles, -1, width)

    def core_pairs(self, parts):
        return list(parts) + [self.swap_core(part) for part in parts]

    def aligned(self, parts, units):
        places = self.gathered[:units] if units == self.units else self.gathered[:units] // 2
        if parts[0].shape[2] % 16 == 0:
            return parts, places
        _, tiles, _, width = parts[0].shape
        back = jnp.zeros_like(places).at[places].set(jnp.arange(units, dtype=jnp.int32))
        whole = jnp.swapaxes(jnp.concatenate(parts)[back], 0, 1)
        count = whole.shape[1] * whole.shape[2] // 48
        return [jnp.swapaxes(whole.reshape(tiles, count, 48, width), 0, 1)], jnp.arange(count, dtype=jnp.int32)

    def aligned_cores(self, parts):
        if parts[0].shape[2] % 16 == 0:
            return parts, self.gathered
        flat = jnp.concatenate([part[:, core] for core in range(2) for part in parts])[:, None]
        return self.aligned([flat], self.units)

    def feed_units(self, following, units):
        down, down_y, up, up_x = following
        down_parts, down_places = self.aligned([self.pair(down, down_y, 1)], units)
        up_parts, up_places = self.aligned_cores([up, up_x])
        down_plan = [(0, (index, 0)) for index in range(down_parts[0].shape[0])]
        up_plan = [
            (1 + part, (index, tile))
            for tile in range(up_parts[0].shape[1]) for part, array in enumerate(up_parts) for index in range(array.shape[0])
        ]
        return [*down_parts, *up_parts], (down_plan, down_places, up_plan, up_places)

    def slots(self, rows):
        if rows // self.units % 16 == 0:
            return self.units, self.scattered
        return rows // 48, jnp.arange(rows // 48, dtype=jnp.int32)

    def unaligned(self, keep, send):
        tiles, _, _, width = keep.shape
        if keep.shape[1] * 2 != self.units or keep.shape[2] % 16 != 0:
            whole = jnp.concatenate([keep, send], axis=1).reshape(tiles, self.units, -1, width)[:, self.scattered]
            keep, send = whole[:, : self.units // 2], whole[:, self.units // 2 :]
        return [part.reshape(tiles, self.units // 2, 2, -1, width) for part in (keep, send)]

    def mine(self, part):
        return lax.dynamic_index_in_dim(part, self.at_y, 2, keepdims=False).astype(jnp.float32)

    def other(self, part):
        return lax.dynamic_index_in_dim(part, 1 - self.at_y, 2, keepdims=False).astype(jnp.float32)

    def moves(self, sends, *others):
        kinds = dict(x=self.swap_x, y=self.swap_y, core=self.swap_core, turn=self.turn)
        values, others = lax.optimization_barrier(([send[1] for send in sends], others))
        came = [kinds[kind](value, *rest) for (kind, _, *rest), value in zip(sends, values)]
        return came, others

    def scatter_second(self, first):
        keep_a, keep_b, came_a, came_b = first
        ring, f32, low = self.ring, jnp.float32, jnp.bfloat16
        away_a = (keep_a[:, ring:].astype(f32) + came_a[:, ring:].astype(f32)).astype(low)
        away_b = (self.other(keep_b) + self.other(came_b)).astype(low)
        return ((keep_a[:, :ring], came_a[:, :ring]), (keep_b, came_b)), [("x", away_a), ("y", away_b)]

    def feed_second(self, keep, send, up):
        return ((keep,), (up,)), [("x", send), ("y", self.other(up).astype(up.dtype))]

    def scatter_third(self, kept, came):
        (parts_a, parts_b), (next_a, next_b) = kept, came
        ring, f32, low = self.ring, jnp.float32, jnp.bfloat16
        total = lambda pick, parts: sum((pick(part) for part in parts[1:]), pick(parts[0]))
        parts_a = (*parts_a, next_a)
        away_a = total(self.other, parts_a).astype(low)
        away_b = total(lambda part: self.mine(part[:, ring:]), parts_b) + next_b[:, ring:].astype(f32)
        return (parts_a, (parts_b, next_b)), [("y", away_a), ("x", away_b.astype(low))]

    def scatter_fourth(self, kept, came):
        (parts_a, (parts_b, next_b)), (last_a, last_b) = kept, came
        ring, f32, low = self.ring, jnp.float32, jnp.bfloat16
        total = lambda pick, parts: sum((pick(part) for part in parts[1:]), pick(parts[0]))
        sum_a = total(self.mine, parts_a) + last_a.astype(f32)
        sum_b = total(lambda part: self.mine(part[:, :ring]), parts_b) + next_b[:, :ring].astype(f32) + last_b.astype(f32)
        flat = lambda part: part.reshape(-1, part.shape[-1])
        pieces = [jnp.concatenate([flat(sum_a[:, step]), flat(sum_b[:, step])]) for step in range(self.ring)]
        shape = (sum_a.shape[0],) + sum_a.shape[2:]
        return (shape, pieces[0]), [("turn", pieces[step].astype(low), step) for step in range(1, self.ring)]

    def scatter_last(self, kept, came):
        shape, total = kept
        for piece in came:
            total = total + piece.astype(jnp.float32)
        rows = shape[0] * shape[1]
        return total[:rows].reshape(shape), total[rows:]


def standard(values):
    centered = values - jnp.mean(values, axis=-1, keepdims=True)
    scale = lax.rsqrt(jnp.mean(centered * centered, axis=-1, keepdims=True) + EPSILON)
    return centered * scale, scale


def standard_back(grad, normed, scale, gain):
    slope = grad * gain
    inner = jnp.mean(slope * normed, axis=-1, keepdims=True)
    return (slope - jnp.mean(slope, axis=-1, keepdims=True) - normed * inner) * scale


def wide(ref):
    return ref[...].astype(jnp.float32)


def dot(left, right, left_dim=1, right_dim=0):
    return lax.dot_general(left, right, (((left_dim,), (right_dim,)), ((), ())), preferred_element_type=jnp.float32)


def rows_sum(values):
    return jnp.sum(values, axis=0, keepdims=True)


def by_head(rows):
    lane = lax.broadcasted_iota(jnp.int32, rows.shape, 1)
    head = rows.shape[1] // GROUP
    zero = jnp.zeros_like(rows)
    return jnp.concatenate(
        [jnp.where((lane >= head * h) & (lane < head * (h + 1)), rows, zero) for h in range(GROUP)], axis=0
    )


def from_heads(stacked):
    count = stacked.shape[0] // GROUP
    head = stacked.shape[1] // GROUP
    lane = lax.broadcasted_iota(jnp.int32, (count, stacked.shape[1]), 1)
    result = stacked[:count]
    for h in range(1, GROUP):
        result = jnp.where(lane >= head * h, stacked[count * h : count * (h + 1)], result)
    return result


def fetch(slots_ref, units, whole, sem):
    for slot, unit in enumerate(units):
        rows = unit.shape[0]
        place = pl.multiple_of(slots_ref[slot] * rows, 16)
        pltpu.make_async_copy(unit, whole.at[pl.ds(place, rows)], sem).start()


def units_of(parts, tile):
    return [part.at[index, tile] for part in parts for index in range(part.shape[0])]


def store(slots_ref, whole, parts, sem):
    slot = 0
    for part in parts:
        rows = part.shape[-2]
        for index in range(part.shape[-3]):
            if len(part.shape) == 3:
                place = pl.multiple_of(slots_ref[slot] * rows, 16)
                pltpu.make_async_copy(whole.at[pl.ds(place, rows)], part.at[index], sem).start()
            else:
                for half in range(2):
                    place = pl.multiple_of((2 * slots_ref[slot] + half) * rows, 16)
                    pltpu.make_async_copy(whole.at[pl.ds(place, rows)], part.at[half, index], sem).start()
            slot += 1


def finish(whole, sem):
    pltpu.make_async_copy(whole, whole, sem).wait()


def layout(visible, masked):
    padded = -(-visible // 8) * 8
    starts = (0, masked, 2 * masked, 2 * masked + padded)
    return starts, -(-(2 * masked + 2 * padded) // 16) * 16


def prepare_kernel(
    place_ref, own_ref, own_latent_ref, came_ref, table_ref, key_ref, value_ref, key_scale_ref, value_scale_ref, rows_ref
):
    masked, visible = own_ref.shape[1], own_latent_ref.shape[1]
    starts, _ = layout(visible, masked)
    rows_ref[...] = jnp.zeros_like(rows_ref)
    rows_ref[:masked] = wide(own_ref.at[0])
    rows_ref[masked : 2 * masked] = came_ref[0, :masked].astype(jnp.float32)
    rows_ref[starts[2] : starts[2] + visible] = wide(own_latent_ref.at[0])
    rows_ref[starts[3] : starts[3] + visible] = came_ref[0, 2 * masked :].astype(jnp.float32)
    rows = rows_ref[...]
    place = place_ref[0]
    lane = lax.broadcasted_iota(jnp.int32, (rows.shape[0], table_ref.shape[0]), 1)
    wanted = jnp.where((lane & 16) == 0, place[:, 0:1], place[:, 1:2])
    chosen = jnp.where((lane & 15) == wanted, 1.0, 0.0).astype(jnp.bfloat16)
    position = dot(chosen, table_ref[...])
    key_ref[0], key_scale_ref[0] = standard(rows + position)
    value_ref[0], value_scale_ref[0] = standard(rows)


def attend_kernel(visible, factor, parts_a, parts_b, *refs):
    slots_ref, key_hat_ref, value_hat_ref, own_ref, came_ref, small_ref = refs[:6]
    part_a, part_b, refs = refs[6 : 6 + parts_a], refs[6 + parts_a : 6 + parts_a + parts_b], refs[6 + parts_a + parts_b :]
    query_ref, key_ref, value_ref, probs_ref, attended_ref, branch_ref, feed_hat_ref, feed_scale_ref, feed_ref = refs[-17:-8]
    normed_refs = refs[-8:-5]
    query_w, key_w, value_w, out_w, sems = refs[-5:]

    @pl.when(pl.program_id(0) == 0)
    def _():
        for index, (parts, tile, whole) in enumerate(
            ((part_a, 0, query_w), (part_a, 1, key_w), (part_b, 0, value_w), (part_b, 1, out_w))
        ):
            fetch(slots_ref, units_of(parts, tile), whole, sems.at[index])
        for index, whole in enumerate((query_w, key_w, value_w, out_w)):
            finish(whole, sems.at[index])

    small = lambda row: small_ref[row : row + 1]
    count = attended_ref.shape[1]
    low = jnp.bfloat16
    query_normed = (key_hat_ref[0, :count] * small(GAIN_QUERY) + small(SHIFT_QUERY)).astype(low)
    key_normed = (key_hat_ref[0] * small(GAIN_KEY)).astype(low)
    value_normed = (value_hat_ref[0] * small(GAIN_VALUE) + small(SHIFT_VALUE)).astype(low)
    for ref, value in zip(normed_refs, (query_normed, key_normed, value_normed)):
        ref[0] = value
    query_ref[0] = (dot(query_normed, query_w[...]) + small(BIAS_QUERY)).astype(low)
    key_ref[0] = dot(key_normed, key_w[...]).astype(low)
    value_ref[0] = (dot(value_normed, value_w[...]) + small(BIAS_VALUE)).astype(low)
    width = key_ref.shape[2] // probs_ref.shape[1]
    for quad in range(probs_ref.shape[1]):
        lanes = slice(width * quad, width * (quad + 1))
        scores = dot(key_ref[0, :, lanes], by_head(query_ref[0, :, lanes]), 1, 1) * factor
        row = lax.broadcasted_iota(jnp.int32, scores.shape, 0)
        starts, _ = layout(visible, own_ref.shape[1])
        real = (row < starts[2] + visible) | ((row >= starts[3]) & (row < starts[3] + visible))
        scores = jnp.where(real, scores, -1e30)
        raised = jnp.exp(scores - jnp.max(scores, axis=0, keepdims=True))
        probs = (raised * (1.0 / rows_sum(raised))).astype(low)
        probs_ref[0, quad] = probs
        attended_ref[0, :, lanes] = from_heads(dot(probs, value_ref[0, :, lanes], 0, 0)).astype(low)
    branch = dot(attended_ref[0], out_w[...]) + small(BIAS_OUT)
    branch_ref[0] = branch
    queries = jnp.concatenate([wide(own_ref.at[0]), wide(came_ref.at[0])], axis=0)
    hat, scale = standard(queries + small(SCALE_ATTENTION) * branch)
    feed_hat_ref[0] = hat
    feed_scale_ref[0] = scale
    feed_ref[0] = (hat * small(GAIN_FEED) + small(SHIFT_FEED)).astype(low)


def feed_kernel(last, down_plan, up_plan, parts, *refs):
    slots_ref, down_slots_ref, out_slots_ref, down_out_slots_ref, core_ref = refs[:5]
    feed_ref, feed_other_ref, cot_refs, small_ref, refs = refs[5], refs[6], refs[7:11], refs[11], refs[12:]
    part_refs = refs[:parts]
    down_w, up_w, down_grad, up_grad, sems = refs[-5:]
    refs = refs[parts:-5]
    outs, refs = refs[:3], refs[3:]
    low = jnp.bfloat16
    small = lambda row: small_ref[row : row + 1]
    fetch(slots_ref, [part_refs[part].at[where] for part, where in up_plan], up_w, sems.at[0])
    fetch(down_slots_ref, [part_refs[part].at[where] for part, where in down_plan], down_w, sems.at[1])
    cotangent = []
    for first, second in (cot_refs[:2], cot_refs[2:]):
        for crop in range(first.shape[0]):
            cotangent += [wide(first.at[crop]), wide(second.at[crop])]
    low_grad = (small(SCALE_FEED) * jnp.concatenate(cotangent, axis=0)).astype(low)
    feed = jnp.concatenate([feed_ref[...], feed_other_ref[...]], axis=0)
    bias = small_ref[pl.ds(BIAS_ROW + 2 * last + core_ref[0], 1)]
    finish(up_w, sems.at[0])
    raised = dot(feed, up_w[...]) + bias
    share = 0.5 * (1.0 + lax.erf(raised * (0.5**0.5)))
    activated = (raised * share).astype(low)
    slope = share + raised * jnp.exp(-0.5 * raised * raised) * ((2.0 * math.pi) ** -0.5)
    down_grad[...] = dot(activated, low_grad, 0, 0).astype(low)
    keep, send, up_out = outs
    store(down_out_slots_ref, down_grad, [keep.at[0], send.at[0]], sems.at[2])
    finish(down_w, sems.at[1])
    raised_grad = (dot(low_grad, down_w[...], 1, 1) * slope).astype(low)
    up_grad[...] = dot(feed, raised_grad, 0, 0).astype(low)
    store(out_slots_ref, up_grad, [up_out.at[tile] for tile in range(up_out.shape[0])], sems.at[3])
    refs[0][...] = rows_sum(raised_grad.astype(jnp.float32))
    lowered = dot(activated, down_w[...])
    grad = dot(raised_grad, up_w[...], 1, 1)
    rows = feed_ref.shape[0]
    for index, value in enumerate((lowered, grad)):
        refs[1 + index][...] = value[:rows]
        if last:
            refs[3 + index][...] = value[rows:].astype(low)
        else:
            refs[3][rows * index : rows * (index + 1)] = value[rows:].astype(low)
    finish(down_grad, sems.at[2])
    finish(up_grad, sems.at[3])


def attend_back_kernel(factor, parts_b, *refs):
    slots_ref, query_ref, key_ref, value_ref, probs_ref = refs[:5]
    lowered_refs, back_refs = refs[5:9], refs[9:13]
    cot_own_ref, cot_came_ref, own_ref, came_ref, branch_ref, hat_ref, scale_ref, small_ref = refs[13:21]
    part_b = refs[21 : 21 + parts_b]
    mixed_own_ref, mixed_came_ref, middle_grad_ref, branch_grad_ref, sums_ref = refs[-10:-5]
    query_grad, key_grad, value_grad, out_w, sem = refs[-5:]
    small = lambda row: small_ref[row : row + 1]
    low = jnp.bfloat16

    @pl.when(pl.program_id(0) == 0)
    def _():
        fetch(slots_ref, units_of(part_b, 1), out_w, sem)
        sums_ref[...] = jnp.zeros_like(sums_ref)

    join = lambda first, second: jnp.concatenate([wide(first.at[0]), wide(second.at[0])], axis=0)
    cotangent = join(cot_own_ref, cot_came_ref)
    lowered = sum((wide(ref.at[0]) for ref in lowered_refs), small(BIAS_DOWN))
    branch = branch_ref[0]
    middle = join(own_ref, came_ref) + small(SCALE_ATTENTION) * branch
    mixed = (middle + small(SCALE_FEED) * lowered).astype(low)
    half = mixed_own_ref.shape[1]
    mixed_own_ref[0] = mixed[:half]
    mixed_came_ref[0] = mixed[half:]
    grad = sum((wide(ref.at[0]) for ref in back_refs[1:]), wide(back_refs[0].at[0]))
    hat = hat_ref[0]
    middle_grad = cotangent + standard_back(grad, hat, scale_ref[0], small(GAIN_FEED))
    middle_grad_ref[0] = middle_grad
    branch_grad = (small(SCALE_ATTENTION) * middle_grad).astype(low)
    branch_grad_ref[0] = branch_grad
    sums_ref[0:1] += rows_sum(cotangent * lowered)
    sums_ref[1:2] += rows_sum((small(SCALE_FEED) * cotangent).astype(low).astype(jnp.float32))
    sums_ref[2:3] += rows_sum(grad * hat)
    sums_ref[3:4] += rows_sum(grad)
    sums_ref[4:5] += rows_sum(middle_grad * branch)
    sums_ref[5:6] += rows_sum(branch_grad.astype(jnp.float32))

    @pl.when(pl.program_id(0) == 0)
    def _():
        finish(out_w, sem)

    above = dot(branch_grad, out_w[...], 1, 1).astype(low)
    width = key_ref.shape[2] // probs_ref.shape[1]
    for quad in range(probs_ref.shape[1]):
        lanes = slice(width * quad, width * (quad + 1))
        probs_low = probs_ref[0, quad]
        probs = probs_low.astype(jnp.float32)
        heads = by_head(above[:, lanes])
        probs_grad = dot(value_ref[0, :, lanes], heads, 1, 1)
        inner = rows_sum(probs_grad * probs)
        score_grad = (probs * (probs_grad - inner)).astype(low)
        value_grad[0, :, lanes] = dot(probs_low, heads).astype(low)
        key_grad[0, :, lanes] = (dot(score_grad, by_head(query_ref[0, :, lanes])) * factor).astype(low)
        query_grad[0, :, lanes] = (from_heads(dot(score_grad, key_ref[0, :, lanes], 0, 0)) * factor).astype(low)


def input_back_kernel(parts_a, parts_b, *refs):
    slots_ref, query_grad, key_grad, value_grad, key_hat_ref, value_hat_ref, key_scale_ref, value_scale_ref = refs[:8]
    middle_grad_ref, mixed_ref, small_ref = refs[8:11]
    part_a, part_b, refs = refs[11 : 11 + parts_a], refs[11 + parts_a : 11 + parts_a + parts_b], refs[11 + parts_a + parts_b :]
    masked_ref, latent_ref, away_ref, sums_ref, query_w, key_w, value_w, sems = refs[-8:]

    @pl.when(pl.program_id(0) == 0)
    def _():
        for index, (parts, tile, whole) in enumerate(((part_a, 0, query_w), (part_a, 1, key_w), (part_b, 0, value_w))):
            fetch(slots_ref, units_of(parts, tile), whole, sems.at[index])
        for index, whole in enumerate((query_w, key_w, value_w)):
            finish(whole, sems.at[index])

    small = lambda row: small_ref[row : row + 1]
    count = query_grad.shape[1]

    @pl.when(pl.program_id(0) == 0)
    def _():
        sums_ref[...] = jnp.zeros_like(sums_ref)

    key_hat, key_scale = key_hat_ref[0], key_scale_ref[0]
    query_hat = key_hat[:count]
    value_hat = value_hat_ref[0]
    from_query = dot(query_grad[0], query_w[...], 1, 1)
    from_key = dot(key_grad[0], key_w[...], 1, 1)
    from_value = dot(value_grad[0], value_w[...], 1, 1)
    sums_ref[0:1] += rows_sum(from_query * query_hat)
    sums_ref[1:2] += rows_sum(from_query)
    sums_ref[2:3] += rows_sum(from_key * key_hat)
    sums_ref[3:4] += rows_sum(from_value * value_hat)
    sums_ref[4:5] += rows_sum(from_value)
    sums_ref[5:6] += rows_sum(wide(query_grad.at[0]))
    sums_ref[6:7] += rows_sum(wide(value_grad.at[0]))
    both = standard_back(from_key, key_hat, key_scale, small(GAIN_KEY)) + standard_back(
        from_value, value_hat, value_scale_ref[0], small(GAIN_VALUE)
    )
    query_part = standard_back(from_query, query_hat, key_scale[:count], small(GAIN_QUERY))
    masked = middle_grad_ref[0] + query_part + both[:count]
    size, visible = masked_ref.shape[1], latent_ref.shape[1]
    starts, _ = layout(visible, size)
    masked_ref[0] = masked[:size]
    latent_ref[0] = both[starts[2] : starts[2] + visible]
    away_ref[0, :size] = masked[size:].astype(away_ref.dtype)
    away_ref[0, size : 2 * size] = mixed_ref[0]
    away_ref[0, 2 * size :] = both[starts[3] : starts[3] + visible].astype(away_ref.dtype)


def weights_back_kernel(
    out_slots_ref, attended, branch_grad, value_normed, value_grad, key_normed, key_grad, query_normed, query_grad,
    keep_a, send_a, keep_b, send_b, *refs,
):
    inputs = (attended, branch_grad, value_normed, value_grad, key_normed, key_grad, query_normed, query_grad)
    held, wholes, sems = refs[:8], refs[8:12], refs[12]
    copies = [pltpu.make_async_copy(ref, scratch, sems.at[4 + k]) for k, (ref, scratch) in enumerate(zip(inputs, held))]
    for copy in copies:
        copy.start()
    targets = ((keep_b, send_b, 1), (keep_b, send_b, 0), (keep_a, send_a, 1), (keep_a, send_a, 0))
    for index, (keep, send, tile) in enumerate(targets):
        copies[2 * index].wait()
        copies[2 * index + 1].wait()
        wholes[index][...] = dot(held[2 * index][...], held[2 * index + 1][...], 0, 0).astype(jnp.bfloat16)
        store(out_slots_ref, wholes[index], [keep.at[tile], send.at[tile]], sems.at[index])
    for index in range(4):
        finish(wholes[index], sems.at[index])


def call(name, kernel, grid, ins, outs, operands, scratch=(), after=(), us=1):
    ins = list(ins) + [ANY] * len(after)
    operands = tuple(operands) + tuple(after)

    def spec(entry, shape):
        if entry is None:
            return pl.BlockSpec(shape, lambda *i: (0,) * len(shape))
        if entry is ANY or entry is SMEM:
            return pl.BlockSpec(memory_space=entry)
        return pl.BlockSpec(*entry)

    return pl.pallas_call(
        kernel,
        name=name,
        grid=grid,
        in_specs=[spec(entry, operand.shape) for entry, operand in zip(ins, operands, strict=True)],
        out_specs=[spec(entry, shape) for entry, shape, _ in outs],
        out_shape=[jax.ShapeDtypeStruct(shape, dtype) for _, shape, dtype in outs],
        scratch_shapes=list(scratch),
        compiler_params=pltpu.CompilerParams(vmem_limit_bytes=56 << 20),
        cost_estimate=pl.CostEstimate(flops=int(us * 1.1e9), bytes_accessed=int(us * 3.5e6), transcendentals=0),
    )(*operands)


def by_crop(shape):
    block = (1,) + tuple(shape[1:])
    return block, lambda i: (i,) + (0,) * (len(block) - 1)


def pack_kernel(vectors, *refs):
    *in_refs, out_ref = refs
    low = jnp.bfloat16
    parts = [wide(ref) for ref in in_refs[vectors + bool(vectors) :]]
    if vectors:
        device_ref, thin, bias_ref = in_refs[0], in_refs[1:vectors], in_refs[vectors]
        width = out_ref.shape[1]
        device = device_ref[0]
        shard, half = thin[0].shape[0], bias_ref.shape[0] // 2
        rows = jnp.concatenate(
            [pad_lanes(wide(ref).reshape(1, -1), 128) for ref in thin]
            + [jnp.zeros((BIAS_ROW - len(thin), 128), jnp.float32)], axis=0
        )
        value = lax.broadcasted_iota(jnp.int32, (128, width), 0)
        lane = lax.broadcasted_iota(jnp.int32, (128, width), 1)
        there = (lane == shard * device + value) & (value < shard)
        line = [dot(rows.astype(low), jnp.where(there, 1.0, 0.0).astype(low))]
        bias = jnp.broadcast_to(pad_lanes(wide(bias_ref).reshape(1, -1), 128), (8, 128)).astype(low)
        row = lax.broadcasted_iota(jnp.int32, (8, width), 0)
        strips = jnp.zeros((8, width), jnp.float32)
        column = half * (2 * lax.div(device, 4) + lax.rem(device, 2))
        for part in range(2):
            inside = (value >= half * part) & (value < half * (part + 1))
            there = (lane == column + value - half * part) & inside
            spot = row == 2 * part + lax.rem(lax.div(device, 2), 2)
            strips = jnp.where(spot, dot(bias, jnp.where(there, 1.0, 0.0).astype(low)), strips)
        middle = len(parts) // 2
        parts = parts[:middle] + line + [strips] + parts[middle:]
    out_ref[...] = jnp.concatenate(parts, axis=0).astype(out_ref.dtype)


def pad_lanes(rows, width):
    if rows.shape[1] == width:
        return rows
    return jnp.concatenate([rows, jnp.zeros((rows.shape[0], width - rows.shape[1]), rows.dtype)], axis=1)


def pack(parts, device=None, vectors=()):
    width, dtype = parts[0].shape[1], parts[0].dtype
    first = (device.reshape(1), *vectors) if vectors else ()
    ins = [SMEM] + [None] * len(vectors) if vectors else []
    run = lambda operands: call(
        "pack", functools.partial(pack_kernel, len(vectors)), (), ins + [None] * len(operands),
        [(None, (sum(part.shape[0] for part in operands) + LINE_ROWS * bool(vectors), width), dtype)], (*first, *operands), us=1,
    )[0]
    if all(part.shape[0] % 8 == 0 for part in parts):
        return run(parts)
    if not vectors:
        return jnp.concatenate(parts)
    half = len(parts) // 2
    blank = jnp.zeros((8, width), dtype)
    line = run([blank, blank])[8 : 8 + LINE_ROWS]
    return jnp.concatenate([*parts[:half], line, *parts[half:]])


def stage(*values):
    return lax.optimization_barrier(values)


def position_table(width):
    quarter = width // 4
    frequency = 10000.0 ** (-np.arange(quarter) / quarter)
    angle = np.arange(16)[:, None] * frequency
    wave = np.concatenate([np.sin(angle), np.cos(angle)], axis=1)
    table = np.zeros((32, width))
    table[:16, : width // 2] = wave
    table[16:, width // 2 :] = wave
    table = table.astype(np.float32)
    high = table.astype(ml_dtypes.bfloat16)
    low = (table - high.astype(np.float32)).astype(ml_dtypes.bfloat16)
    return np.concatenate([high, low])


def local(
    latents, queries, order, weight_query, bias_query, weight_key, weight_value, bias_value, weight_out, bias_out,
    gain_query, shift_query, gain_key, gain_value, shift_value, scale_attention, weight_up, bias_up, weight_down,
    bias_down, gain_feed, shift_feed, scale_feed, cotangent,
):
    low = jnp.bfloat16
    net = Net()
    slot = lax.axis_index("query")
    crops = latents.shape[0] // 2
    visible, masked = latents.shape[1], queries.shape[1]
    shard, width = weight_query.shape
    count = net.count
    _, rows = layout(visible, masked)
    block = lambda values, which: lax.dynamic_slice_in_dim(values, which * crops, crops, 0)
    own_latents, own_queries, own_cot = [block(v, slot) for v in (latents, queries, cotangent)]
    vectors = [
        bias_query, bias_value, bias_out, gain_query, shift_query, gain_key, gain_value, shift_value, scale_attention,
        bias_down, gain_feed, shift_feed, scale_feed, bias_up,
    ]
    device = (2 * (4 * net.at_ring + 2 * net.at_x + net.at_core) + slot).astype(jnp.int32)
    deep = weight_down.shape[0]
    half = deep // 2
    f32 = jnp.float32
    ring = net.ring
    pairs = 2 * ring
    flat = lambda values: values.reshape(-1, values.shape[-1])

    own_a = pack([weight_query, weight_key, weight_value, weight_out], device, vectors)
    turn_all = lambda value: [("turn", value, step) for step in range(1, ring)]
    away = jnp.concatenate([block(values, 1 - slot) for values in (queries, cotangent, latents)], axis=1)
    (*rings_a, came), (own_a, weight_up, weight_down, own_cot, order) = net.moves(
        [*turn_all(own_a), ("y", away)], own_a, weight_up, weight_down, own_cot, order
    )
    rings_a = [own_a, *rings_a]
    ups = jnp.moveaxis(weight_up.reshape(shard, pairs, 2, 2, 2, half), (2, 4), (0, 1)).reshape(2, 2, shard, width)
    up_own = lax.dynamic_index_in_dim(ups, net.at_core, 0, keepdims=False)
    up_came = net.swap_core(lax.dynamic_index_in_dim(ups, 1 - net.at_core, 0, keepdims=False))
    table = jnp.asarray(position_table(width))
    own_order = block(order, slot)
    part = lambda start, size, which: lax.dynamic_slice_in_dim(own_order, start + which * size, size, 1)
    gap = jnp.full((crops, rows // 2 - masked - visible), -1, jnp.int32)
    indices = jnp.concatenate(
        [
            part(2 * visible, masked, slot), part(2 * visible, masked, 1 - slot),
            part(0, visible, slot), gap, part(0, visible, 1 - slot), gap,
        ],
        axis=1,
    )
    steps = jnp.stack([indices // GRID, jnp.where(indices < 0, -1, indices % GRID)], axis=-1)
    own_b, own_c = [pack([weight_down[half * k : half * (k + 1)], up_own[k], up_came[k]]) for k in range(2)]
    rings_a, came, own_b, own_c, steps = stage(rings_a, came, own_b, own_c, steps)

    cut = 2 * shard
    line = sum(piece[cut : cut + LINE_ROWS] for piece in rings_a[1:]) + rings_a[0][cut : cut + LINE_ROWS]
    one = jnp.concatenate([piece[:cut] for piece in rings_a] + [line])
    two = jnp.stack([piece[cut + LINE_ROWS :] for piece in rings_a])
    (*rings_b, one_x, two_y), (own_b, one, two, came) = net.moves(
        [*turn_all(own_b), ("x", one), ("y", two)], own_b, one, two, came
    )
    crop_out = lambda shape, dtype: (by_crop(shape), shape, dtype)
    wide_shape, thin_shape = (crops, rows, width), (crops, rows, 1)
    operands = (steps, own_queries, own_latents, came, table)
    key_hat, value_hat, key_scale, value_scale = call(
        "prepare", prepare_kernel, (crops,), [by_crop(a.shape) for a in operands[:4]] + [None],
        [crop_out(wide_shape, f32)] * 2 + [crop_out(thin_shape, f32)] * 2, operands, scratch=[pltpu.VMEM((rows, width), f32)],
    )
    one_x, two_y, rings_b, key_hat, value_hat, key_scale, value_scale = stage(
        one_x, two_y, [own_b, *rings_b], key_hat, value_hat, key_scale, value_scale
    )

    line = one[ring * cut :] + one_x[ring * cut :]
    one = jnp.concatenate([one[: ring * cut], one_x[: ring * cut], line])
    two = net.pair(two, two_y, 2)
    (*rings_c, one_y, two_x), (own_c, one, two) = net.moves([*turn_all(own_c), ("y", one), ("x", two)], own_c, one, two)
    one_y, two_x, rings_c = stage(one_y, two_x, [own_c, *rings_c])

    line = one[pairs * cut :] + one_y[pairs * cut :]
    units = lambda values: values[: pairs * cut].reshape(pairs, cut, width)
    one = net.pair(units(one), units(one_y), 2)
    pieces = list(zip(rings_b, rings_c))
    downs = jnp.stack([jnp.concatenate([b[:half], c[:half]]) for b, c in pieces])
    ups = jnp.stack([jnp.concatenate([b[half:], c[half:]]) for b, c in pieces])
    sends = [("core", value) for value in (one, two, two_x, line)]
    (downs_x, ups_y, one_core, two_core, two_x_core, line_core), (one, two, two_x, line, downs, ups) = net.moves(
        [("x", downs), ("y", ups), *sends], one, two, two_x, line, downs, ups
    )
    part_a, part_b = [one, one_core], [two, two_x, two_core, two_x_core]
    small = line.astype(f32) + line_core.astype(f32)
    part_a, part_b, small = stage(part_a, part_b, small)
    (part_a, places), (part_b, _) = net.aligned(part_a, net.units), net.aligned(part_b, net.units)
    slots, out_places = net.slots(width)
    ask_shape = (crops, 2 * masked, width)
    dma = pltpu.SemaphoreType.DMA
    square_vmem = pltpu.VMEM((width, width), low)
    quads = HEADS // GROUP
    factor = (width // HEADS) ** -0.5
    probs_shape = (crops, quads, rows, GROUP * 2 * masked)
    of_came = lambda part: ((1, masked, width), lambda i: (i, part, 0))
    operands = (places, key_hat, value_hat, own_queries, came, small, *part_a, *part_b)
    parts = len(part_a) + len(part_b)
    query_p, key_p, value_p, probs, attended, branch, feed_hat, feed_scale, feed, *normed = call(
        "attend", functools.partial(attend_kernel, visible, factor, len(part_a), len(part_b)), (crops,),
        [SMEM] + [by_crop(a.shape) for a in operands[1:4]] + [of_came(0), None] + [ANY] * parts,
        [
            crop_out(ask_shape, low), crop_out(wide_shape, low), crop_out(wide_shape, low), crop_out(probs_shape, low),
            crop_out(ask_shape, low), crop_out(ask_shape, f32), crop_out(ask_shape, f32),
            crop_out((crops, 2 * masked, 1), f32), crop_out(ask_shape, low),
            crop_out(ask_shape, low), crop_out(wide_shape, low), crop_out(wide_shape, low),
        ],
        operands, scratch=[square_vmem] * 4 + [dma((4,))],
    )
    downs_x, ups_y, query_p, key_p, value_p, probs, attended, branch, feed_hat, feed_scale, feed, normed = stage(
        downs_x, ups_y, query_p, key_p, value_p, probs, attended, branch, feed_hat, feed_scale, feed, normed
    )

    def second_of(k):
        own, other = slice(half * k, half * (k + 1)), slice(2 * shard * k, 2 * shard * (k + 1))
        return jnp.concatenate([downs[:, own], downs_x[:, own]]), net.pair(ups[:, other], ups_y[:, other], 2)

    feed = flat(feed)
    down_b, up_b = second_of(0)
    (down_b_y, up_b_x, feed_other, *other_cot), (down_b, up_b, feed, own_cot, came) = net.moves(
        [("y", down_b), ("x", up_b), ("core", feed), ("core", own_cot), ("core", came)], down_b, up_b, feed, own_cot, came
    )
    down_c, up_c = second_of(1)
    down_b_y, up_b_x, feed_other, other_cot, down_c, up_c = stage(down_b_y, up_b_x, feed_other, other_cot, down_c, up_c)
    parts_b, where_b = net.feed_units((down_b, down_b_y, up_b, up_b_x), pairs)
    (down_c_y, up_c_x), (down_c, up_c, parts_b) = net.moves([("y", down_c), ("x", up_c)], down_c, up_c, parts_b)
    asks = crops * 2 * masked
    core = net.at_core.reshape(1).astype(jnp.int32)
    aligned = slots == net.units and half % 16 == 0
    down_out_places = out_places[:pairs] // 2 if aligned else out_places

    def feed_call(name, parts, where, last):
        down_plan, down_places, up_plan, up_places = where
        operands = (
            up_places, down_places, out_places, down_out_places, core, feed, feed_other, own_cot, came, *other_cot, small,
        )
        of_cot = ((crops, masked, width), lambda i: (0, 1, 0))
        ins = [SMEM] * 5 + [None] * 3 + [of_cot, None, of_cot, None] + [ANY] * len(parts)
        down_shape = (1, 2, ring, half, width) if aligned else (1, slots // 2, width // slots, width)
        outs = [(ANY, down_shape, low)] * 2 + [(ANY, (2, slots // 2, width // slots, width), low), (None, (1, width), f32)]
        outs += [(None, (asks, width), f32)] * 2 + [(None, (asks if last else 2 * asks, width), low)] * (1 + last)
        return call(
            name, functools.partial(feed_kernel, last, down_plan, up_plan, len(parts)), (1,), ins, outs,
            (*operands, *parts), scratch=[square_vmem] * 4 + [dma((4,))],
        )

    def feed_grads(keep, send, up):
        if aligned:
            keep, send = jnp.moveaxis(keep, 1, 2), jnp.moveaxis(send, 1, 2)
            up = up.reshape(2, pairs, 2, shard, width)
        else:
            down = jnp.concatenate([keep, send], axis=1).reshape(1, pairs, 2, half, width)[:, net.scattered[:pairs] // 2]
            keep, send = down[:, :ring], down[:, ring:]
            up = up.reshape(net.units, 2, shard, width)[net.scattered].reshape(2, pairs, 2, shard, width)
        return net.feed_second(keep, send, up)

    down_keep, down_send, up_out, bias_b, *partial_b = feed_call("feed0", parts_b, where_b, 0)
    down_c_y, up_c_x, down_keep, down_send, up_out, bias_b, partial_b = stage(
        down_c_y, up_c_x, down_keep, down_send, up_out, bias_b, partial_b
    )

    parts_c, where_c = net.feed_units((down_c, down_c_y, up_c, up_c_x), pairs)
    kept_b, sends = feed_grads(down_keep, down_send, up_out)
    (swapped_b, *came_b), (kept_b, partial_b, parts_c) = net.moves(
        [("core", partial_b[2]), *sends], kept_b, partial_b, parts_c
    )
    down_keep, down_send, up_out, bias_c, *partial_c = feed_call("feed1", parts_c, where_c, 1)
    swapped_c = [net.swap_core(values) for values in partial_c[2:]]
    came_b, down_keep, down_send, up_out, bias_c, swapped_b, partial_c, swapped_c = stage(
        came_b, down_keep, down_send, up_out, bias_c, swapped_b, partial_c, swapped_c
    )
    of_crops = lambda values: values.reshape(ask_shape)
    swapped = [swapped_b.reshape(2 * crops, *ask_shape[1:]), *[of_crops(values) for values in swapped_c]]
    partials = [of_crops(values) for values in (partial_b[0], partial_c[0], partial_b[1], partial_c[1])]

    kept_c, sends = feed_grads(down_keep, down_send, up_out)
    came_c, (kept_c, partials, swapped) = net.moves(sends, kept_c, partials, swapped)
    operands = (
        places, query_p, key_p, value_p, probs, *partials[:2], *swapped[:2], *partials[2:], swapped[0], swapped[2],
        own_cot, came, own_queries, came, branch, feed_hat, feed_scale, small, *part_b,
    )
    of_swapped = lambda part: [((1, *ask_shape[1:]), lambda i: (i + part * crops, 0, 0)), by_crop(ask_shape)]
    masked_shape, latent_shape = (crops, masked, width), (crops, visible, width)
    sums_out = (None, (8, width), f32)
    mixed_own, mixed_came, middle_grad, branch_grad, feed_sums, query_grad, key_grad, value_grad = call(
        "attend_back", functools.partial(attend_back_kernel, factor, len(part_b)), (crops,),
        [SMEM] + [by_crop(a.shape) for a in operands[1:7]] + of_swapped(0) + [by_crop(ask_shape)] * 2 + of_swapped(1)
        + [by_crop(own_cot.shape), of_came(1), by_crop(own_queries.shape), of_came(0)]
        + [by_crop(a.shape) for a in operands[17:20]] + [None] + [ANY] * len(part_b),
        [
            crop_out(masked_shape, low), crop_out(masked_shape, low), crop_out(ask_shape, f32), crop_out(ask_shape, low),
            sums_out, crop_out(ask_shape, low), crop_out(wide_shape, low), crop_out(wide_shape, low),
        ],
        operands, scratch=[square_vmem, dma(())],
    )
    came_c, mixed_own, mixed_came, middle_grad, branch_grad, feed_sums, query_grad, key_grad, value_grad = stage(
        came_c, mixed_own, mixed_came, middle_grad, branch_grad, feed_sums, query_grad, key_grad, value_grad
    )

    kept_b, sends_b = net.scatter_third(kept_b, came_b)
    kept_c, sends_c = net.scatter_third(kept_c, came_c)
    came, (kept_b, kept_c, query_grad, key_grad, value_grad) = net.moves(
        [*sends_b, *sends_c], kept_b, kept_c, query_grad, key_grad, value_grad
    )
    came_b, came_c = came[:2], came[2:]
    operands = (
        attended, branch_grad, normed[2], value_grad, normed[1], key_grad, normed[0], query_grad,
    )
    operands = [flat(operand) for operand in operands]
    keep_a, send_a, keep_b, send_b = call(
        "weights_back", weights_back_kernel, (), [SMEM] + [ANY] * 8,
        [(ANY, (2, slots // 2, width // slots, width), low)] * 4, (out_places, *operands),
        scratch=[pltpu.VMEM(operand.shape, low) for operand in operands] + [square_vmem] * 4 + [dma((12,))],
    )
    came_b, came_c, keep_a, send_a, keep_b, send_b = stage(came_b, came_c, keep_a, send_a, keep_b, send_b)

    (keep_a, send_a), (keep_b, send_b) = net.unaligned(keep_a, send_a), net.unaligned(keep_b, send_b)
    came, (keep_a, keep_b, query_grad, key_grad, value_grad) = net.moves(
        [("core", send_a), ("core", send_b)], keep_a, keep_b, query_grad, key_grad, value_grad
    )
    first_a = (keep_a, keep_b, *came)
    operands = (
        places, query_grad, key_grad, value_grad, key_hat, value_hat, key_scale, value_scale, middle_grad, mixed_came, small,
        *part_a, *part_b,
    )
    home_rows = 2 * masked + visible
    masked_own, latent_own, away, input_sums = call(
        "input_back", functools.partial(input_back_kernel, len(part_a), len(part_b)), (crops,),
        [SMEM] + [by_crop(a.shape) for a in operands[1:10]] + [None] + [ANY] * parts,
        [
            crop_out(masked_shape, f32), crop_out(latent_shape, f32), crop_out((crops, home_rows, width), low), sums_out,
        ],
        operands, scratch=[square_vmem] * 3 + [dma((3,))],
    )
    masked_own, latent_own, away, input_sums, first_a = stage(masked_own, latent_own, away, input_sums, first_a)

    kept_a, sends_a = net.scatter_second(first_a)
    (shape_b, kept_b), sends_b = net.scatter_fourth(kept_b, came_b)
    strips = jnp.arange(LINE_ROWS - BIAS_ROW)[:, None]
    strips = jnp.where(strips == net.at_core, bias_b, 0.0) + jnp.where(strips == 2 + net.at_core, bias_c, 0.0)
    lines = jnp.concatenate([input_sums, feed_sums, strips])
    came, (kept_a, kept_b, lines) = net.moves([*sends_a, *sends_b, ("core", lines)], kept_a, kept_b, lines)
    came, = stage(came)
    came_a, came_b, line_core = came[:2], came[2:-1], came[-1]

    kept_a, sends_a = net.scatter_third(kept_a, came_a)
    (shape_c, kept_c), sends_c = net.scatter_fourth(kept_c, came_c)
    lines = lines + line_core
    (line_y, *came), (kept_a, kept_c, lines) = net.moves([("y", lines), *sends_a, *sends_c], kept_a, kept_c, lines)
    came_a, came_c = came[:2], came[2:]
    lines = lines + line_y
    lines = lines + net.swap_x(lines)
    came_a, came_c, lines = stage(came_a, came_c, lines)

    (shape_a, kept_a), sends_a = net.scatter_fourth(kept_a, came_a)
    sends_a = [(kind, jnp.concatenate([piece, lines.astype(low)]), step) for kind, piece, step in sends_a]
    (home_rows, *came_a), (kept_a, lines, came_b, came_c) = net.moves(
        [("y", away), *sends_a], kept_a, lines, came_b, came_c
    )
    lines = sum((piece[-LINE_ROWS:].astype(f32) for piece in came_a), lines)
    came_a = [piece[:-LINE_ROWS] for piece in came_a]
    down_sums, up_sums = zip(
        net.scatter_last((shape_b, kept_b), came_b), net.scatter_last((shape_c, kept_c), came_c)
    )
    down_sum = jnp.concatenate([down[0] for down in down_sums])
    up_sums = jnp.stack([up.reshape(2, shard, width) for up in up_sums])
    up_came = net.swap_core(up_sums[:, 1])
    up_sums = jnp.where(net.at_core == 0, jnp.stack([up_sums[:, 0], up_came]), jnp.stack([up_came, up_sums[:, 0]]))
    up_sum = jnp.moveaxis(up_sums.reshape(2, 2, shard, pairs, 2, half), (0, 1), (2, 4)).reshape(shard, count * deep)
    sum_a, sum_b = net.scatter_last((shape_a, kept_a), came_a)
    sum_b = sum_b.reshape(sum_a.shape)

    vector = lax.dynamic_slice(lines, (0, shard * device), (BIAS_ROW, shard))
    column = half * (2 * (device // 4) + device % 2)
    strip = lambda k: lax.dynamic_slice(lines, (BIAS_ROW + 2 * k + net.at_core, column), (1, half))
    bias_up_sum = jnp.concatenate([strip(0)[0], strip(1)[0]])

    def home(keep, came, dtype):
        keep, came = keep.astype(dtype), came.astype(dtype)
        return jnp.concatenate([jnp.where(slot == 0, keep, came), jnp.where(slot == 0, came, keep)], axis=0)

    return (
        home(mixed_own, home_rows[:, masked : 2 * masked], low),
        home(latent_own, home_rows[:, 2 * masked :], f32),
        home(masked_own, home_rows[:, :masked], f32),
        sum_a[0],
        vector[5],
        sum_a[1],
        sum_b[0],
        vector[6],
        sum_b[1],
        vector[13],
        vector[0],
        vector[1],
        vector[2],
        vector[3],
        vector[4],
        vector[12],
        up_sum,
        bias_up_sum,
        down_sum,
        vector[9],
        vector[10],
        vector[11],
        vector[8],
    )


def solution(mesh):
    batch, query = mesh.devices.shape
    split = Mesh(mesh.devices.reshape(batch // 4, 2, 2, query), (*BATCH, "query"))
    crop, rows, flat = P(BATCH, "query", None), P((*BATCH, "query"), None), P((*BATCH, "query"))
    in_specs = (crop, crop, P(BATCH, None), rows, flat, rows, rows, flat, rows, *[flat] * 7, rows, flat, rows, *[flat] * 4, crop)
    out_specs = (crop, crop, crop, rows, flat, rows, rows, flat, rows, *[flat] * 7, rows, flat, rows, *[flat] * 4)
    return jax.shard_map(local, mesh=split, in_specs=in_specs, out_specs=out_specs, check_vma=False)
```

```python
import functools
import math

import jax
import jax.numpy as jnp
import ml_dtypes
import numpy as np
from jax import lax
from jax.experimental import pallas as pl
from jax.experimental.pallas import tpu as pltpu
from jax.sharding import Mesh
from jax.sharding import PartitionSpec as P

BATCH = ("ring", "x", "core")
HEADS = 12
GRID = 14
GROUP = 4
PACK_MIB = 16
CHUNK = 768
EPSILON = 1e-06
BIAS_QUERY = 0
BIAS_VALUE = 1
BIAS_OUT = 2
GAIN_QUERY = 3
SHIFT_QUERY = 4
GAIN_KEY = 5
GAIN_VALUE = 6
SHIFT_VALUE = 7
SCALE_ATTENTION = 8
BIAS_DOWN = 9
GAIN_FEED = 10
SHIFT_FEED = 11
SCALE_FEED = 12
SMALLS = 13
BIAS_ROW = 16
LINE_ROWS = 24
ANY = pl.ANY
SMEM = pltpu.SMEM


class Net:
    def __init__(self):
        self.ring = lax.axis_size("ring")
        batch = 4 * self.ring
        self.units = batch
        self.count = batch * lax.axis_size("query")
        self.at_ring, self.at_x, self.at_core = lax.axis_index("ring"), lax.axis_index("x"), lax.axis_index("core")
        self.at_y = lax.axis_index("query")
        slot = jnp.arange(batch)
        core, x, step = slot // (2 * self.ring), (slot // self.ring) % 2, slot % self.ring
        rest = 2 * (x ^ self.at_x) + (core ^ self.at_core)
        self.gathered = (4 * ((self.at_ring - step) % self.ring) + rest).astype(jnp.int32)
        self.scattered = (4 * ((self.at_ring + step) % self.ring) + rest).astype(jnp.int32)

    def turn(self, values, step):
        return lax.ppermute(values, "ring", [(place, (place + step) % self.ring) for place in range(self.ring)])

    def turns(self, values):
        return [values] + [self.turn(values, step) for step in range(1, self.ring)]

    def swap_x(self, values):
        return lax.ppermute(values, "x", [(0, 1), (1, 0)])

    def swap_core(self, values):
        return lax.ppermute(values, "core", [(0, 1), (1, 0)])

    def swap_y(self, values):
        return lax.ppermute(values, "query", [(0, 1), (1, 0)])

    def pair(self, own, came, tiles):
        first = jnp.where(self.at_y == 0, own, came)
        last = jnp.where(self.at_y == 0, came, own)
        slots, rows, width = own.shape
        both = jnp.stack([part.reshape(slots, tiles, -1, width) for part in (first, last)], axis=2)
        return both.reshape(slots, tiles, -1, width)

    def core_pairs(self, parts):
        return list(parts) + [self.swap_core(part) for part in parts]

    def aligned(self, parts, units):
        places = self.gathered[:units] if units == self.units else self.gathered[:units] // 2
        if parts[0].shape[2] % 16 == 0:
            return parts, places
        _, tiles, _, width = parts[0].shape
        back = jnp.zeros_like(places).at[places].set(jnp.arange(units, dtype=jnp.int32))
        whole = jnp.swapaxes(jnp.concatenate(parts)[back], 0, 1)
        count = whole.shape[1] * whole.shape[2] // 48
        return [jnp.swapaxes(whole.reshape(tiles, count, 48, width), 0, 1)], jnp.arange(count, dtype=jnp.int32)

    def aligned_cores(self, parts):
        if parts[0].shape[2] % 16 == 0:
            return parts, self.gathered
        flat = jnp.concatenate([part[:, core] for core in range(2) for part in parts])[:, None]
        return self.aligned([flat], self.units)

    def feed_units(self, following, units):
        down, down_y, up, up_x = following
        if down.shape[1] % 16 == 0:
            down_parts, places = [down[:, None], down_y[:, None]], 2 * (self.gathered[:units] // 2)
            down_places = jnp.concatenate([places + self.at_y, places + 1 - self.at_y]).astype(jnp.int32)
        else:
            down_parts, down_places = self.aligned([self.pair(down, down_y, 1)], units)
        up_parts, up_places = self.aligned_cores([up, up_x])
        down_plan = [(part, (index, 0)) for part, array in enumerate(down_parts) for index in range(array.shape[0])]
        up_plan = [
            (len(down_parts) + part, (index, tile))
            for tile in range(up_parts[0].shape[1]) for part, array in enumerate(up_parts) for index in range(array.shape[0])
        ]
        return [*down_parts, *up_parts], (down_plan, down_places, up_plan, up_places)

    def slots(self, rows):
        if rows // self.units % 16 == 0:
            return self.units, self.scattered
        return rows // 48, jnp.arange(rows // 48, dtype=jnp.int32)

    def unaligned(self, keep, send):
        tiles, _, _, width = keep.shape
        if keep.shape[1] * 2 != self.units or keep.shape[2] % 16 != 0:
            whole = jnp.concatenate([keep, send], axis=1).reshape(tiles, self.units, -1, width)[:, self.scattered]
            keep, send = whole[:, : self.units // 2], whole[:, self.units // 2 :]
        return [part.reshape(tiles, self.units // 2, 2, -1, width) for part in (keep, send)]

    def mine(self, part):
        return lax.dynamic_index_in_dim(part, self.at_y, 2, keepdims=False).astype(jnp.float32)

    def other(self, part):
        return lax.dynamic_index_in_dim(part, 1 - self.at_y, 2, keepdims=False).astype(jnp.float32)

    def moves(self, sends, *others):
        kinds = dict(x=self.swap_x, y=self.swap_y, core=self.swap_core, turn=self.turn)
        values, others = lax.optimization_barrier(([send[1] for send in sends], others))
        came = [kinds[kind](value, *rest) for (kind, _, *rest), value in zip(sends, values)]
        return came, others

    def scatter_second(self, first):
        keep_a, keep_b, came_a, came_b = first
        ring, f32, low = self.ring, jnp.float32, jnp.bfloat16
        away_a = (keep_a[:, ring:].astype(f32) + came_a[:, ring:].astype(f32)).astype(low)
        away_b = (self.other(keep_b) + self.other(came_b)).astype(low)
        return ((keep_a[:, :ring], came_a[:, :ring]), (keep_b, came_b)), [("x", away_a), ("y", away_b)]

    def feed_second(self, keep, send, up):
        return ((keep,), (up,)), [("x", send), ("y", self.other(up).astype(up.dtype))]

    def scatter_third(self, kept, came):
        (parts_a, parts_b), (next_a, next_b) = kept, came
        ring, f32, low = self.ring, jnp.float32, jnp.bfloat16
        total = lambda pick, parts: sum((pick(part) for part in parts[1:]), pick(parts[0]))
        parts_a = (*parts_a, next_a)
        away_a = total(self.other, parts_a).astype(low)
        away_b = total(lambda part: self.mine(part[:, ring:]), parts_b) + next_b[:, ring:].astype(f32)
        return (parts_a, (parts_b, next_b)), [("y", away_a), ("x", away_b.astype(low))]

    def scatter_fourth(self, kept, came):
        (parts_a, (parts_b, next_b)), (last_a, last_b) = kept, came
        ring, f32, low = self.ring, jnp.float32, jnp.bfloat16
        total = lambda pick, parts: sum((pick(part) for part in parts[1:]), pick(parts[0]))
        sum_a = total(self.mine, parts_a) + last_a.astype(f32)
        sum_b = total(lambda part: self.mine(part[:, :ring]), parts_b) + next_b[:, :ring].astype(f32) + last_b.astype(f32)
        flat = lambda part: part.reshape(-1, part.shape[-1])
        pieces = [jnp.concatenate([flat(sum_a[:, step]), flat(sum_b[:, step])]) for step in range(self.ring)]
        shape = (sum_a.shape[0],) + sum_a.shape[2:]
        return (shape, pieces[0]), [("turn", pieces[step].astype(low), step) for step in range(1, self.ring)]

    def scatter_last(self, kept, came):
        shape, total = kept
        for piece in came:
            total = total + piece.astype(jnp.float32)
        rows = shape[0] * shape[1]
        return total[:rows].reshape(shape), total[rows:]


def standard(values):
    centered = values - jnp.mean(values, axis=-1, keepdims=True)
    scale = lax.rsqrt(jnp.mean(centered * centered, axis=-1, keepdims=True) + EPSILON)
    return centered * scale, scale


def standard_back(grad, normed, scale, gain):
    slope = grad * gain
    inner = jnp.mean(slope * normed, axis=-1, keepdims=True)
    return (slope - jnp.mean(slope, axis=-1, keepdims=True) - normed * inner) * scale


def wide(ref):
    return ref[...].astype(jnp.float32)


def dot(left, right, left_dim=1, right_dim=0):
    return lax.dot_general(left, right, (((left_dim,), (right_dim,)), ((), ())), preferred_element_type=jnp.float32)


def rows_sum(values):
    return jnp.sum(values, axis=0, keepdims=True)


def by_head(rows):
    lane = lax.broadcasted_iota(jnp.int32, rows.shape, 1)
    head = rows.shape[1] // GROUP
    zero = jnp.zeros_like(rows)
    return jnp.concatenate(
        [jnp.where((lane >= head * h) & (lane < head * (h + 1)), rows, zero) for h in range(GROUP)], axis=0
    )


def from_heads(stacked):
    count = stacked.shape[0] // GROUP
    head = stacked.shape[1] // GROUP
    lane = lax.broadcasted_iota(jnp.int32, (count, stacked.shape[1]), 1)
    result = stacked[:count]
    for h in range(1, GROUP):
        result = jnp.where(lane >= head * h, stacked[count * h : count * (h + 1)], result)
    return result


def fetch(slots_ref, units, whole, sem):
    for slot, unit in enumerate(units):
        rows = unit.shape[0]
        place = pl.multiple_of(slots_ref[slot] * rows, 16)
        pltpu.make_async_copy(unit, whole.at[pl.ds(place, rows)], sem).start()


def units_of(parts, tile):
    return [part.at[index, tile] for part in parts for index in range(part.shape[0])]


def store(slots_ref, whole, parts, sem):
    slot = 0
    for part in parts:
        rows = part.shape[-2]
        for index in range(part.shape[-3]):
            if len(part.shape) == 3:
                place = pl.multiple_of(slots_ref[slot] * rows, 16)
                pltpu.make_async_copy(whole.at[pl.ds(place, rows)], part.at[index], sem).start()
            else:
                for half in range(2):
                    place = pl.multiple_of((2 * slots_ref[slot] + half) * rows, 16)
                    pltpu.make_async_copy(whole.at[pl.ds(place, rows)], part.at[half, index], sem).start()
            slot += 1


def finish(whole, sem):
    pltpu.make_async_copy(whole, whole, sem).wait()


def layout(visible, masked):
    padded = -(-visible // 8) * 8
    starts = (0, masked, 2 * masked, 2 * masked + padded)
    return starts, -(-(2 * masked + 2 * padded) // 16) * 16


def prepare_kernel(
    place_ref, own_ref, own_latent_ref, came_ref, table_ref, key_ref, value_ref, key_scale_ref, value_scale_ref, rows_ref
):
    masked, visible = own_ref.shape[1], own_latent_ref.shape[1]
    starts, _ = layout(visible, masked)
    rows_ref[...] = jnp.zeros_like(rows_ref)
    rows_ref[:masked] = wide(own_ref.at[0])
    rows_ref[masked : 2 * masked] = came_ref[0, :masked].astype(jnp.float32)
    rows_ref[starts[2] : starts[2] + visible] = wide(own_latent_ref.at[0])
    rows_ref[starts[3] : starts[3] + visible] = came_ref[0, 2 * masked :].astype(jnp.float32)
    rows = rows_ref[...]
    place = place_ref[0]
    lane = lax.broadcasted_iota(jnp.int32, (rows.shape[0], table_ref.shape[0]), 1)
    wanted = jnp.where((lane & 16) == 0, place[:, 0:1], place[:, 1:2])
    chosen = jnp.where((lane & 15) == wanted, 1.0, 0.0).astype(jnp.bfloat16)
    position = dot(chosen, table_ref[...])
    key_ref[0], key_scale_ref[0] = standard(rows + position)
    value_ref[0], value_scale_ref[0] = standard(rows)


def attend_kernel(visible, factor, parts_a, parts_b, *refs):
    slots_ref, key_hat_ref, value_hat_ref, own_ref, came_ref, small_ref = refs[:6]
    part_a, part_b, refs = refs[6 : 6 + parts_a], refs[6 + parts_a : 6 + parts_a + parts_b], refs[6 + parts_a + parts_b :]
    query_ref, key_ref, value_ref, probs_ref, attended_ref, branch_ref, feed_hat_ref, feed_scale_ref, feed_ref = refs[-17:-8]
    normed_refs = refs[-8:-5]
    query_w, key_w, value_w, out_w, sems = refs[-5:]

    @pl.when(pl.program_id(0) == 0)
    def _():
        for index, (parts, tile, whole) in enumerate(
            ((part_a, 0, query_w), (part_a, 1, key_w), (part_b, 0, value_w), (part_b, 1, out_w))
        ):
            fetch(slots_ref, units_of(parts, tile), whole, sems.at[index])
        for index, whole in enumerate((query_w, key_w, value_w, out_w)):
            finish(whole, sems.at[index])

    small = lambda row: small_ref[row : row + 1]
    count = attended_ref.shape[1]
    low = jnp.bfloat16
    query_normed = (key_hat_ref[0, :count] * small(GAIN_QUERY) + small(SHIFT_QUERY)).astype(low)
    key_normed = (key_hat_ref[0] * small(GAIN_KEY)).astype(low)
    value_normed = (value_hat_ref[0] * small(GAIN_VALUE) + small(SHIFT_VALUE)).astype(low)
    for ref, value in zip(normed_refs, (query_normed, key_normed, value_normed)):
        ref[0] = value
    query_ref[0] = (dot(query_normed, query_w[...]) + small(BIAS_QUERY)).astype(low)
    key_ref[0] = dot(key_normed, key_w[...]).astype(low)
    value_ref[0] = (dot(value_normed, value_w[...]) + small(BIAS_VALUE)).astype(low)
    width = key_ref.shape[2] // probs_ref.shape[1]
    for quad in range(probs_ref.shape[1]):
        lanes = slice(width * quad, width * (quad + 1))
        scores = dot(key_ref[0, :, lanes], by_head(query_ref[0, :, lanes]), 1, 1) * factor
        row = lax.broadcasted_iota(jnp.int32, scores.shape, 0)
        starts, _ = layout(visible, own_ref.shape[1])
        real = (row < starts[2] + visible) | ((row >= starts[3]) & (row < starts[3] + visible))
        scores = jnp.where(real, scores, -1e30)
        raised = jnp.exp(scores - jnp.max(scores, axis=0, keepdims=True))
        probs = (raised * (1.0 / rows_sum(raised))).astype(low)
        probs_ref[0, quad] = probs
        attended_ref[0, :, lanes] = from_heads(dot(probs, value_ref[0, :, lanes], 0, 0)).astype(low)
    branch = dot(attended_ref[0], out_w[...]) + small(BIAS_OUT)
    branch_ref[0] = branch
    queries = jnp.concatenate([wide(own_ref.at[0]), wide(came_ref.at[0])], axis=0)
    hat, scale = standard(queries + small(SCALE_ATTENTION) * branch)
    feed_hat_ref[0] = hat
    feed_scale_ref[0] = scale
    feed_ref[0] = (hat * small(GAIN_FEED) + small(SHIFT_FEED)).astype(low)


def feed_kernel(last, down_plan, up_plan, parts, *refs):
    slots_ref, down_slots_ref, out_slots_ref, down_out_slots_ref, core_ref = refs[:5]
    feed_ref, feed_other_ref, cot_refs, small_ref, refs = refs[5], refs[6], refs[7:11], refs[11], refs[12:]
    part_refs = refs[:parts]
    down_w, up_w, down_grad, up_grad, sems = refs[-5:]
    refs = refs[parts:-5]
    outs, refs = refs[:3], refs[3:]
    low = jnp.bfloat16
    small = lambda row: small_ref[row : row + 1]
    fetch(slots_ref, [part_refs[part].at[where] for part, where in up_plan], up_w, sems.at[0])
    fetch(down_slots_ref, [part_refs[part].at[where] for part, where in down_plan], down_w, sems.at[1])
    cotangent = []
    for first, second in (cot_refs[:2], cot_refs[2:]):
        for crop in range(first.shape[0]):
            cotangent += [wide(first.at[crop]), wide(second.at[crop])]
    low_grad = (small(SCALE_FEED) * jnp.concatenate(cotangent, axis=0)).astype(low)
    feed = jnp.concatenate([feed_ref[...], feed_other_ref[...]], axis=0)
    bias = small_ref[pl.ds(BIAS_ROW + 2 * last + core_ref[0], 1)]
    finish(up_w, sems.at[0])
    raised = dot(feed, up_w[...]) + bias
    share = 0.5 * (1.0 + lax.erf(raised * (0.5**0.5)))
    activated = (raised * share).astype(low)
    slope = share + raised * jnp.exp(-0.5 * raised * raised) * ((2.0 * math.pi) ** -0.5)
    down_grad[...] = dot(activated, low_grad, 0, 0).astype(low)
    keep, send, up_out = outs
    store(down_out_slots_ref, down_grad, [keep.at[0], send.at[0]], sems.at[2])
    finish(down_w, sems.at[1])
    raised_grad = (dot(low_grad, down_w[...], 1, 1) * slope).astype(low)
    up_grad[...] = dot(feed, raised_grad, 0, 0).astype(low)
    store(out_slots_ref, up_grad, [up_out.at[tile] for tile in range(up_out.shape[0])], sems.at[3])
    refs[0][...] = rows_sum(raised_grad.astype(jnp.float32))
    lowered = dot(activated, down_w[...])
    grad = dot(raised_grad, up_w[...], 1, 1)
    rows = feed_ref.shape[0]
    for index, value in enumerate((lowered, grad)):
        refs[1 + index][...] = value[:rows]
        if last:
            refs[3 + index][...] = value[rows:].astype(low)
        else:
            refs[3][rows * index : rows * (index + 1)] = value[rows:].astype(low)
    finish(down_grad, sems.at[2])
    finish(up_grad, sems.at[3])


def attend_back_kernel(factor, parts_b, *refs):
    slots_ref, query_ref, key_ref, value_ref, probs_ref = refs[:5]
    lowered_refs, back_refs = refs[5:9], refs[9:13]
    cot_own_ref, cot_came_ref, own_ref, came_ref, branch_ref, hat_ref, scale_ref, small_ref = refs[13:21]
    part_b = refs[21 : 21 + parts_b]
    mixed_own_ref, mixed_came_ref, middle_grad_ref, branch_grad_ref, sums_ref = refs[-10:-5]
    query_grad, key_grad, value_grad, out_w, sem = refs[-5:]
    small = lambda row: small_ref[row : row + 1]
    low = jnp.bfloat16

    @pl.when(pl.program_id(0) == 0)
    def _():
        fetch(slots_ref, units_of(part_b, 1), out_w, sem)
        sums_ref[...] = jnp.zeros_like(sums_ref)

    join = lambda first, second: jnp.concatenate([wide(first.at[0]), wide(second.at[0])], axis=0)
    cotangent = join(cot_own_ref, cot_came_ref)
    lowered = sum((wide(ref.at[0]) for ref in lowered_refs), small(BIAS_DOWN))
    branch = branch_ref[0]
    middle = join(own_ref, came_ref) + small(SCALE_ATTENTION) * branch
    mixed = (middle + small(SCALE_FEED) * lowered).astype(low)
    half = mixed_own_ref.shape[1]
    mixed_own_ref[0] = mixed[:half]
    mixed_came_ref[0] = mixed[half:]
    grad = sum((wide(ref.at[0]) for ref in back_refs[1:]), wide(back_refs[0].at[0]))
    hat = hat_ref[0]
    middle_grad = cotangent + standard_back(grad, hat, scale_ref[0], small(GAIN_FEED))
    middle_grad_ref[0] = middle_grad
    branch_grad = (small(SCALE_ATTENTION) * middle_grad).astype(low)
    branch_grad_ref[0] = branch_grad
    sums_ref[0:1] += rows_sum(cotangent * lowered)
    sums_ref[1:2] += rows_sum((small(SCALE_FEED) * cotangent).astype(low).astype(jnp.float32))
    sums_ref[2:3] += rows_sum(grad * hat)
    sums_ref[3:4] += rows_sum(grad)
    sums_ref[4:5] += rows_sum(middle_grad * branch)
    sums_ref[5:6] += rows_sum(branch_grad.astype(jnp.float32))

    @pl.when(pl.program_id(0) == 0)
    def _():
        finish(out_w, sem)

    above = dot(branch_grad, out_w[...], 1, 1).astype(low)
    width = key_ref.shape[2] // probs_ref.shape[1]
    for quad in range(probs_ref.shape[1]):
        lanes = slice(width * quad, width * (quad + 1))
        probs_low = probs_ref[0, quad]
        probs = probs_low.astype(jnp.float32)
        heads = by_head(above[:, lanes])
        probs_grad = dot(value_ref[0, :, lanes], heads, 1, 1)
        inner = rows_sum(probs_grad * probs)
        score_grad = (probs * (probs_grad - inner)).astype(low)
        value_grad[0, :, lanes] = dot(probs_low, heads).astype(low)
        key_grad[0, :, lanes] = (dot(score_grad, by_head(query_ref[0, :, lanes])) * factor).astype(low)
        query_grad[0, :, lanes] = (from_heads(dot(score_grad, key_ref[0, :, lanes], 0, 0)) * factor).astype(low)


def input_back_kernel(parts_a, parts_b, *refs):
    slots_ref, query_grad, key_grad, value_grad, key_hat_ref, value_hat_ref, key_scale_ref, value_scale_ref = refs[:8]
    middle_grad_ref, mixed_ref, small_ref = refs[8:11]
    part_a, part_b, refs = refs[11 : 11 + parts_a], refs[11 + parts_a : 11 + parts_a + parts_b], refs[11 + parts_a + parts_b :]
    masked_ref, latent_ref, away_ref, sums_ref, query_w, key_w, value_w, sems = refs[-8:]

    @pl.when(pl.program_id(0) == 0)
    def _():
        for index, (parts, tile, whole) in enumerate(((part_a, 0, query_w), (part_a, 1, key_w), (part_b, 0, value_w))):
            fetch(slots_ref, units_of(parts, tile), whole, sems.at[index])
        for index, whole in enumerate((query_w, key_w, value_w)):
            finish(whole, sems.at[index])

    small = lambda row: small_ref[row : row + 1]
    count = query_grad.shape[1]

    @pl.when(pl.program_id(0) == 0)
    def _():
        sums_ref[...] = jnp.zeros_like(sums_ref)

    key_hat, key_scale = key_hat_ref[0], key_scale_ref[0]
    query_hat = key_hat[:count]
    value_hat = value_hat_ref[0]
    from_query = dot(query_grad[0], query_w[...], 1, 1)
    from_key = dot(key_grad[0], key_w[...], 1, 1)
    from_value = dot(value_grad[0], value_w[...], 1, 1)
    sums_ref[0:1] += rows_sum(from_query * query_hat)
    sums_ref[1:2] += rows_sum(from_query)
    sums_ref[2:3] += rows_sum(from_key * key_hat)
    sums_ref[3:4] += rows_sum(from_value * value_hat)
    sums_ref[4:5] += rows_sum(from_value)
    sums_ref[5:6] += rows_sum(wide(query_grad.at[0]))
    sums_ref[6:7] += rows_sum(wide(value_grad.at[0]))
    both = standard_back(from_key, key_hat, key_scale, small(GAIN_KEY)) + standard_back(
        from_value, value_hat, value_scale_ref[0], small(GAIN_VALUE)
    )
    query_part = standard_back(from_query, query_hat, key_scale[:count], small(GAIN_QUERY))
    masked = middle_grad_ref[0] + query_part + both[:count]
    size, visible = masked_ref.shape[1], latent_ref.shape[1]
    starts, _ = layout(visible, size)
    masked_ref[0] = masked[:size]
    latent_ref[0] = both[starts[2] : starts[2] + visible]
    away_ref[0, :size] = masked[size:].astype(away_ref.dtype)
    away_ref[0, size : 2 * size] = mixed_ref[0]
    away_ref[0, 2 * size :] = both[starts[3] : starts[3] + visible].astype(away_ref.dtype)


def weights_back_kernel(
    out_slots_ref, attended, branch_grad, value_normed, value_grad, key_normed, key_grad, query_normed, query_grad,
    keep_a, send_a, keep_b, send_b, *refs,
):
    inputs = (attended, branch_grad, value_normed, value_grad, key_normed, key_grad, query_normed, query_grad)
    held, wholes, sems = refs[:8], refs[8:12], refs[12]
    copies = [pltpu.make_async_copy(ref, scratch, sems.at[4 + k]) for k, (ref, scratch) in enumerate(zip(inputs, held))]
    for copy in copies:
        copy.start()
    targets = ((keep_b, send_b, 1), (keep_b, send_b, 0), (keep_a, send_a, 1), (keep_a, send_a, 0))
    for index, (keep, send, tile) in enumerate(targets):
        copies[2 * index].wait()
        copies[2 * index + 1].wait()
        wholes[index][...] = dot(held[2 * index][...], held[2 * index + 1][...], 0, 0).astype(jnp.bfloat16)
        store(out_slots_ref, wholes[index], [keep.at[tile], send.at[tile]], sems.at[index])
    for index in range(4):
        finish(wholes[index], sems.at[index])


def call(name, kernel, grid, ins, outs, operands, scratch=(), after=(), us=1, mib=54):
    ins = list(ins) + [ANY] * len(after)
    operands = tuple(operands) + tuple(after)

    def spec(entry, shape):
        if entry is None:
            return pl.BlockSpec(shape, lambda *i: (0,) * len(shape))
        if entry in (ANY, SMEM, pltpu.HBM):
            return pl.BlockSpec(memory_space=entry)
        return pl.BlockSpec(*entry)

    return pl.pallas_call(
        kernel,
        name=name,
        grid=grid,
        in_specs=[spec(pltpu.HBM if entry is ANY else entry, operand.shape) for entry, operand in zip(ins, operands, strict=True)],
        out_specs=[spec(entry, shape) for entry, shape, _ in outs],
        out_shape=[jax.ShapeDtypeStruct(shape, dtype) for _, shape, dtype in outs],
        scratch_shapes=list(scratch),
        compiler_params=pltpu.CompilerParams(vmem_limit_bytes=mib << 20),
        cost_estimate=pl.CostEstimate(flops=int(us * 1.1e9), bytes_accessed=int(us * 3.5e6), transcendentals=0),
    )(*operands)


def by_crop(shape):
    block = (1,) + tuple(shape[1:])
    return block, lambda i: (i,) + (0,) * (len(block) - 1)


def pack_kernel(vectors, *refs):
    *in_refs, out_ref = refs
    low = jnp.bfloat16
    parts = [wide(ref) for ref in in_refs[vectors + bool(vectors) :]]
    if vectors:
        device_ref, thin, bias_ref = in_refs[0], in_refs[1:vectors], in_refs[vectors]
        width = out_ref.shape[1]
        device = device_ref[0]
        shard, half = thin[0].shape[0], bias_ref.shape[0] // 2
        rows = jnp.concatenate(
            [pad_lanes(wide(ref).reshape(1, -1), 128) for ref in thin]
            + [jnp.zeros((BIAS_ROW - len(thin), 128), jnp.float32)], axis=0
        )
        value = lax.broadcasted_iota(jnp.int32, (128, width), 0)
        lane = lax.broadcasted_iota(jnp.int32, (128, width), 1)
        there = (lane == shard * device + value) & (value < shard)
        line = [dot(rows.astype(low), jnp.where(there, 1.0, 0.0).astype(low))]
        bias = jnp.broadcast_to(pad_lanes(wide(bias_ref).reshape(1, -1), 128), (8, 128)).astype(low)
        row = lax.broadcasted_iota(jnp.int32, (8, width), 0)
        strips = jnp.zeros((8, width), jnp.float32)
        column = half * (2 * lax.div(device, 4) + lax.rem(device, 2))
        for part in range(2):
            inside = (value >= half * part) & (value < half * (part + 1))
            there = (lane == column + value - half * part) & inside
            spot = row == 2 * part + lax.rem(lax.div(device, 2), 2)
            strips = jnp.where(spot, dot(bias, jnp.where(there, 1.0, 0.0).astype(low)), strips)
        middle = len(parts) // 2
        parts = parts[:middle] + line + [strips] + parts[middle:]
    out_ref[...] = jnp.concatenate(parts, axis=0).astype(out_ref.dtype)


def pad_lanes(rows, width):
    if rows.shape[1] == width:
        return rows
    return jnp.concatenate([rows, jnp.zeros((rows.shape[0], width - rows.shape[1]), rows.dtype)], axis=1)


def pack(parts, device=None, vectors=()):
    width, dtype = parts[0].shape[1], parts[0].dtype
    first = (device.reshape(1), *vectors) if vectors else ()
    ins = [SMEM] + [None] * len(vectors) if vectors else []
    run = lambda operands: call(
        "pack", functools.partial(pack_kernel, len(vectors)), (), ins + [None] * len(operands),
        [(None, (sum(part.shape[0] for part in operands) + LINE_ROWS * bool(vectors), width), dtype)], (*first, *operands), mib=PACK_MIB,
    )[0]
    if all(part.shape[0] % 8 == 0 for part in parts):
        return run(parts)
    if not vectors:
        return jnp.concatenate(parts)
    half = len(parts) // 2
    blank = jnp.zeros((8, width), dtype)
    line = run([blank, blank])[8 : 8 + LINE_ROWS]
    return jnp.concatenate([*parts[:half], line, *parts[half:]])


def stage(*values):
    return lax.optimization_barrier(values)


def position_table(width):
    quarter = width // 4
    frequency = 10000.0 ** (-np.arange(quarter) / quarter)
    angle = np.arange(16)[:, None] * frequency
    wave = np.concatenate([np.sin(angle), np.cos(angle)], axis=1)
    table = np.zeros((32, width))
    table[:16, : width // 2] = wave
    table[16:, width // 2 :] = wave
    table = table.astype(np.float32)
    high = table.astype(ml_dtypes.bfloat16)
    low = (table - high.astype(np.float32)).astype(ml_dtypes.bfloat16)
    return np.concatenate([high, low])


def local(
    latents, queries, order, weight_query, bias_query, weight_key, weight_value, bias_value, weight_out, bias_out,
    gain_query, shift_query, gain_key, gain_value, shift_value, scale_attention, weight_up, bias_up, weight_down,
    bias_down, gain_feed, shift_feed, scale_feed, cotangent,
):
    low = jnp.bfloat16
    net = Net()
    slot = lax.axis_index("query")
    crops = latents.shape[0] // 2
    visible, masked = latents.shape[1], queries.shape[1]
    shard, width = weight_query.shape
    count = net.count
    _, rows = layout(visible, masked)
    block = lambda values, which: lax.dynamic_slice_in_dim(values, which * crops, crops, 0)
    own_latents, own_queries, own_cot = [block(v, slot) for v in (latents, queries, cotangent)]
    vectors = [
        bias_query, bias_value, bias_out, gain_query, shift_query, gain_key, gain_value, shift_value, scale_attention,
        bias_down, gain_feed, shift_feed, scale_feed, bias_up,
    ]
    device = (2 * (4 * net.at_ring + 2 * net.at_x + net.at_core) + slot).astype(jnp.int32)
    deep = weight_down.shape[0]
    half = deep // 2
    f32 = jnp.float32
    ring = net.ring
    pairs = 2 * ring
    flat = lambda values: values.reshape(-1, values.shape[-1])

    own_a = pack([weight_query, weight_key, weight_value, weight_out], device, vectors)
    turn_all = lambda value: [("turn", value, step) for step in range(1, ring)]
    away = jnp.concatenate([block(values, 1 - slot) for values in (queries, cotangent, latents)], axis=1)
    (*rings_a, came), (own_a, weight_up, weight_down, own_cot, order) = net.moves(
        [*turn_all(own_a), ("y", away)], own_a, weight_up, weight_down, own_cot, order
    )
    rings_a = [own_a, *rings_a]
    ups = jnp.moveaxis(weight_up.reshape(shard, pairs, 2, 2, 2, half), (2, 4), (0, 1)).reshape(2, 2, shard, width)
    up_own = lax.dynamic_index_in_dim(ups, net.at_core, 0, keepdims=False)
    up_came = net.swap_core(lax.dynamic_index_in_dim(ups, 1 - net.at_core, 0, keepdims=False))
    table = jnp.asarray(position_table(width))
    own_order = block(order, slot)
    part = lambda start, size, which: lax.dynamic_slice_in_dim(own_order, start + which * size, size, 1)
    gap = jnp.full((crops, rows // 2 - masked - visible), -1, jnp.int32)
    indices = jnp.concatenate(
        [
            part(2 * visible, masked, slot), part(2 * visible, masked, 1 - slot),
            part(0, visible, slot), gap, part(0, visible, 1 - slot), gap,
        ],
        axis=1,
    )
    steps = jnp.stack([indices // GRID, jnp.where(indices < 0, -1, indices % GRID)], axis=-1)
    own_b, own_c = [pack([weight_down[half * k : half * (k + 1)], up_own[k], up_came[k]]) for k in range(2)]
    rings_a, came, own_b, own_c, steps = stage(rings_a, came, own_b, own_c, steps)

    cut = 2 * shard
    line = sum(piece[cut : cut + LINE_ROWS] for piece in rings_a[1:]) + rings_a[0][cut : cut + LINE_ROWS]
    one = jnp.concatenate([piece[:cut] for piece in rings_a] + [line])
    two = jnp.stack([piece[cut + LINE_ROWS :] for piece in rings_a])
    (*rings_b, one_x, two_y), (own_b, one, two, came) = net.moves(
        [*turn_all(own_b), ("x", one), ("y", two)], own_b, one, two, came
    )
    crop_out = lambda shape, dtype: (by_crop(shape), shape, dtype)
    wide_shape, thin_shape = (crops, rows, width), (crops, rows, 1)
    operands = (steps, own_queries, own_latents, came, table)
    key_hat, value_hat, key_scale, value_scale = call(
        "prepare", prepare_kernel, (crops,), [by_crop(a.shape) for a in operands[:4]] + [None],
        [crop_out(wide_shape, f32)] * 2 + [crop_out(thin_shape, f32)] * 2, operands, scratch=[pltpu.VMEM((rows, width), f32)], mib=54,
    )
    one_x, two_y, rings_b, key_hat, value_hat, key_scale, value_scale = stage(
        one_x, two_y, [own_b, *rings_b], key_hat, value_hat, key_scale, value_scale
    )

    line = one[ring * cut :] + one_x[ring * cut :]
    one = jnp.concatenate([one[: ring * cut], one_x[: ring * cut], line])
    two = net.pair(two, two_y, 2)
    (*rings_c, one_y, two_x), (own_c, one, two) = net.moves([*turn_all(own_c), ("y", one), ("x", two)], own_c, one, two)
    one_y, two_x, rings_c = stage(one_y, two_x, [own_c, *rings_c])

    line = one[pairs * cut :] + one_y[pairs * cut :]
    units = lambda values: values[: pairs * cut].reshape(pairs, cut, width)
    one = net.pair(units(one), units(one_y), 2)
    pieces = list(zip(rings_b, rings_c))
    downs = jnp.stack([jnp.concatenate([b[:half], c[:half]]) for b, c in pieces])
    ups = jnp.stack([jnp.concatenate([b[half:], c[half:]]) for b, c in pieces])
    sends = [("core", value) for value in (one, two, two_x, line)]
    (downs_x, ups_y, one_core, two_core, two_x_core, line_core), (one, two, two_x, line, downs, ups) = net.moves(
        [("x", downs), ("y", ups), *sends], one, two, two_x, line, downs, ups
    )
    part_a, part_b = [one, one_core], [two, two_x, two_core, two_x_core]
    small = line.astype(f32) + line_core.astype(f32)
    part_a, part_b, small = stage(part_a, part_b, small)
    (part_a, places), (part_b, _) = net.aligned(part_a, net.units), net.aligned(part_b, net.units)
    slots, out_places = net.slots(width)
    ask_shape = (crops, 2 * masked, width)
    dma = pltpu.SemaphoreType.DMA
    square_vmem = pltpu.VMEM((width, width), low)
    quads = HEADS // GROUP
    factor = (width // HEADS) ** -0.5
    probs_shape = (crops, quads, rows, GROUP * 2 * masked)
    of_came = lambda part: ((1, masked, width), lambda i: (i, part, 0))
    operands = (places, key_hat, value_hat, own_queries, came, small, *part_a, *part_b)
    parts = len(part_a) + len(part_b)
    query_p, key_p, value_p, probs, attended, branch, feed_hat, feed_scale, feed, *normed = call(
        "attend", functools.partial(attend_kernel, visible, factor, len(part_a), len(part_b)), (crops,),
        [SMEM] + [by_crop(a.shape) for a in operands[1:4]] + [of_came(0), None] + [ANY] * parts,
        [
            crop_out(ask_shape, low), crop_out(wide_shape, low), crop_out(wide_shape, low), crop_out(probs_shape, low),
            crop_out(ask_shape, low), crop_out(ask_shape, f32), crop_out(ask_shape, f32),
            crop_out((crops, 2 * masked, 1), f32), crop_out(ask_shape, low),
            crop_out(ask_shape, low), crop_out(wide_shape, low), crop_out(wide_shape, low),
        ],
        operands, scratch=[square_vmem] * 4 + [dma((4,))],
    )
    downs_x, ups_y, query_p, key_p, value_p, probs, attended, branch, feed_hat, feed_scale, feed, normed = stage(
        downs_x, ups_y, query_p, key_p, value_p, probs, attended, branch, feed_hat, feed_scale, feed, normed
    )

    def second_of(k):
        own, other = slice(half * k, half * (k + 1)), slice(2 * shard * k, 2 * shard * (k + 1))
        return jnp.concatenate([downs[:, own], downs_x[:, own]]), net.pair(ups[:, other], ups_y[:, other], 2)

    feed = flat(feed)
    down_b, up_b = second_of(0)
    (down_b_y, up_b_x, feed_other, *other_cot), (down_b, up_b, feed, own_cot, came) = net.moves(
        [("y", down_b), ("x", up_b), ("core", feed), ("core", own_cot), ("core", came)], down_b, up_b, feed, own_cot, came
    )
    down_c, up_c = second_of(1)
    down_b_y, up_b_x, feed_other, other_cot, down_c, up_c = stage(down_b_y, up_b_x, feed_other, other_cot, down_c, up_c)
    parts_b, where_b = net.feed_units((down_b, down_b_y, up_b, up_b_x), pairs)
    (down_c_y, up_c_x), (down_c, up_c, parts_b) = net.moves([("y", down_c), ("x", up_c)], down_c, up_c, parts_b)
    asks = crops * 2 * masked
    core = net.at_core.reshape(1).astype(jnp.int32)
    aligned = slots == net.units and half % 16 == 0
    down_out_places = out_places[:pairs] // 2 if aligned else out_places

    def feed_call(name, parts, where, last):
        down_plan, down_places, up_plan, up_places = where
        operands = (
            up_places, down_places, out_places, down_out_places, core, feed, feed_other, own_cot, came, *other_cot, small,
        )
        of_cot = ((crops, masked, width), lambda i: (0, 1, 0))
        ins = [SMEM] * 5 + [None] * 3 + [of_cot, None, of_cot, None] + [ANY] * len(parts)
        down_shape = (1, 2, ring, half, width) if aligned else (1, slots // 2, width // slots, width)
        outs = [(ANY, down_shape, low)] * 2 + [(ANY, (2, slots // 2, width // slots, width), low), (None, (1, width), f32)]
        outs += [(None, (asks, width), f32)] * 2 + [(None, (asks if last else 2 * asks, width), low)] * (1 + last)
        return call(
            name, functools.partial(feed_kernel, last, down_plan, up_plan, len(parts)), (1,), ins, outs,
            (*operands, *parts), scratch=[square_vmem] * 4 + [dma((4,))],
        )

    def feed_grads(keep, send, up):
        if aligned:
            keep, send = jnp.moveaxis(keep, 1, 2), jnp.moveaxis(send, 1, 2)
            up = up.reshape(2, pairs, 2, shard, width)
        else:
            down = jnp.concatenate([keep, send], axis=1).reshape(1, pairs, 2, half, width)[:, net.scattered[:pairs] // 2]
            keep, send = down[:, :ring], down[:, ring:]
            up = up.reshape(net.units, 2, shard, width)[net.scattered].reshape(2, pairs, 2, shard, width)
        return net.feed_second(keep, send, up)

    down_keep, down_send, up_out, bias_b, *partial_b = feed_call("feed0", parts_b, where_b, 0)
    down_c_y, up_c_x, down_keep, down_send, up_out, bias_b, partial_b = stage(
        down_c_y, up_c_x, down_keep, down_send, up_out, bias_b, partial_b
    )

    parts_c, where_c = net.feed_units((down_c, down_c_y, up_c, up_c_x), pairs)
    kept_b, sends = feed_grads(down_keep, down_send, up_out)
    (swapped_b, *came_b), (kept_b, partial_b, parts_c) = net.moves(
        [("core", partial_b[2]), *sends], kept_b, partial_b, parts_c
    )
    down_keep, down_send, up_out, bias_c, *partial_c = feed_call("feed1", parts_c, where_c, 1)
    swapped_c = [net.swap_core(values) for values in partial_c[2:]]
    came_b, down_keep, down_send, up_out, bias_c, swapped_b, partial_c, swapped_c = stage(
        came_b, down_keep, down_send, up_out, bias_c, swapped_b, partial_c, swapped_c
    )
    of_crops = lambda values: values.reshape(ask_shape)
    swapped = [swapped_b.reshape(2 * crops, *ask_shape[1:]), *[of_crops(values) for values in swapped_c]]
    partials = [of_crops(values) for values in (partial_b[0], partial_c[0], partial_b[1], partial_c[1])]

    kept_c, sends = feed_grads(down_keep, down_send, up_out)
    came_c, (kept_c, partials, swapped) = net.moves(sends, kept_c, partials, swapped)
    operands = (
        places, query_p, key_p, value_p, probs, *partials[:2], *swapped[:2], *partials[2:], swapped[0], swapped[2],
        own_cot, came, own_queries, came, branch, feed_hat, feed_scale, small, *part_b,
    )
    of_swapped = lambda part: [((1, *ask_shape[1:]), lambda i: (i + part * crops, 0, 0)), by_crop(ask_shape)]
    masked_shape, latent_shape = (crops, masked, width), (crops, visible, width)
    sums_out = (None, (8, width), f32)
    mixed_own, mixed_came, middle_grad, branch_grad, feed_sums, query_grad, key_grad, value_grad = call(
        "attend_back", functools.partial(attend_back_kernel, factor, len(part_b)), (crops,),
        [SMEM] + [by_crop(a.shape) for a in operands[1:7]] + of_swapped(0) + [by_crop(ask_shape)] * 2 + of_swapped(1)
        + [by_crop(own_cot.shape), of_came(1), by_crop(own_queries.shape), of_came(0)]
        + [by_crop(a.shape) for a in operands[17:20]] + [None] + [ANY] * len(part_b),
        [
            crop_out(masked_shape, low), crop_out(masked_shape, low), crop_out(ask_shape, f32), crop_out(ask_shape, low),
            sums_out, crop_out(ask_shape, low), crop_out(wide_shape, low), crop_out(wide_shape, low),
        ],
        operands, scratch=[square_vmem, dma(())],
    )
    came_c, mixed_own, mixed_came, middle_grad, branch_grad, feed_sums, query_grad, key_grad, value_grad = stage(
        came_c, mixed_own, mixed_came, middle_grad, branch_grad, feed_sums, query_grad, key_grad, value_grad
    )

    kept_b, sends_b = net.scatter_third(kept_b, came_b)
    kept_c, sends_c = net.scatter_third(kept_c, came_c)
    came, (kept_b, kept_c, query_grad, key_grad, value_grad) = net.moves(
        [*sends_b, *sends_c], kept_b, kept_c, query_grad, key_grad, value_grad
    )
    came_b, came_c = came[:2], came[2:]
    operands = (
        attended, branch_grad, normed[2], value_grad, normed[1], key_grad, normed[0], query_grad,
    )
    operands = [flat(operand) for operand in operands]
    keep_a, send_a, keep_b, send_b = call(
        "weights_back", weights_back_kernel, (), [SMEM] + [ANY] * 8,
        [(ANY, (2, slots // 2, width // slots, width), low)] * 4, (out_places, *operands),
        scratch=[pltpu.VMEM(operand.shape, low) for operand in operands] + [square_vmem] * 4 + [dma((12,))],
    )
    came_b, came_c, keep_a, send_a, keep_b, send_b = stage(came_b, came_c, keep_a, send_a, keep_b, send_b)

    (keep_a, send_a), (keep_b, send_b) = net.unaligned(keep_a, send_a), net.unaligned(keep_b, send_b)
    came, (keep_a, keep_b, query_grad, key_grad, value_grad) = net.moves(
        [("core", send_a), ("core", send_b)], keep_a, keep_b, query_grad, key_grad, value_grad
    )
    first_a = (keep_a, keep_b, *came)
    operands = (
        places, query_grad, key_grad, value_grad, key_hat, value_hat, key_scale, value_scale, middle_grad, mixed_came, small,
        *part_a, *part_b,
    )
    home_rows = 2 * masked + visible
    masked_own, latent_own, away, input_sums = call(
        "input_back", functools.partial(input_back_kernel, len(part_a), len(part_b)), (crops,),
        [SMEM] + [by_crop(a.shape) for a in operands[1:10]] + [None] + [ANY] * parts,
        [
            crop_out(masked_shape, f32), crop_out(latent_shape, f32), crop_out((crops, home_rows, width), low), sums_out,
        ],
        operands, scratch=[square_vmem] * 3 + [dma((3,))],
    )
    masked_own, latent_own, away, input_sums, first_a = stage(masked_own, latent_own, away, input_sums, first_a)

    kept_a, sends_a = net.scatter_second(first_a)
    (shape_b, kept_b), sends_b = net.scatter_fourth(kept_b, came_b)
    strips = jnp.arange(LINE_ROWS - BIAS_ROW)[:, None]
    strips = jnp.where(strips == net.at_core, bias_b, 0.0) + jnp.where(strips == 2 + net.at_core, bias_c, 0.0)
    lines = jnp.concatenate([input_sums, feed_sums, strips])
    came, (kept_a, kept_b, lines) = net.moves([*sends_a, *sends_b, ("core", lines)], kept_a, kept_b, lines)
    lines = lines + came[-1]
    line_y = net.swap_y(lines)
    came, lines, line_y = stage(came[:-1], lines, line_y)
    came_a, came_b = came[:2], came[2:]

    kept_a, sends_a = net.scatter_third(kept_a, came_a)
    (shape_c, kept_c), sends_c = net.scatter_fourth(kept_c, came_c)
    lines = lines + line_y
    high = lines.astype(low)
    rest = (lines - high.astype(f32)).astype(low)
    ridden = jnp.concatenate([flat(sends_a[1][1]), high, rest])
    shape = sends_a[1][1].shape
    came, (kept_a, kept_c, lines) = net.moves([("x", ridden), sends_a[0], *sends_c], kept_a, kept_c, lines)
    came_x, came_c = came[0], came[2:]
    line_x = came_x[-2 * LINE_ROWS : -LINE_ROWS].astype(f32) + came_x[-LINE_ROWS:].astype(f32)
    came_a = (came[1], came_x[: -2 * LINE_ROWS].reshape(shape))
    lines = lines + line_x
    came_a, lines, away = stage(came_a, lines, away)

    home_rows = net.swap_y(away)
    (shape_a, kept_a), sends_a = net.scatter_fourth(kept_a, came_a)
    sends_a = [(kind, jnp.concatenate([piece, lines.astype(low)]), step) for kind, piece, step in sends_a]
    came_a, (kept_a, lines, came_b, came_c) = net.moves(sends_a, kept_a, lines, came_b, came_c)
    lines = sum((piece[-LINE_ROWS:].astype(f32) for piece in came_a), lines)
    came_a = [piece[:-LINE_ROWS] for piece in came_a]
    down_sums, up_sums = zip(
        net.scatter_last((shape_b, kept_b), came_b), net.scatter_last((shape_c, kept_c), came_c)
    )
    down_sum = jnp.concatenate([down[0] for down in down_sums])
    up_sums = jnp.stack([up.reshape(2, shard, width) for up in up_sums])
    up_came = net.swap_core(up_sums[:, 1])
    up_sums = jnp.where(net.at_core == 0, jnp.stack([up_sums[:, 0], up_came]), jnp.stack([up_came, up_sums[:, 0]]))
    up_sum = jnp.moveaxis(up_sums.reshape(2, 2, shard, pairs, 2, half), (0, 1), (2, 4)).reshape(shard, count * deep)
    sum_a, sum_b = net.scatter_last((shape_a, kept_a), came_a)
    sum_b = sum_b.reshape(sum_a.shape)

    vector = lax.dynamic_slice(lines, (0, shard * device), (BIAS_ROW, shard))
    column = half * (2 * (device // 4) + device % 2)
    strip = lambda k: lax.dynamic_slice(lines, (BIAS_ROW + 2 * k + net.at_core, column), (1, half))
    bias_up_sum = jnp.concatenate([strip(0)[0], strip(1)[0]])

    def home(keep, came, dtype):
        keep, came = keep.astype(dtype), came.astype(dtype)
        return jnp.concatenate([jnp.where(slot == 0, keep, came), jnp.where(slot == 0, came, keep)], axis=0)

    return (
        home(mixed_own, home_rows[:, masked : 2 * masked], low),
        home(latent_own, home_rows[:, 2 * masked :], f32),
        home(masked_own, home_rows[:, :masked], f32),
        sum_a[0],
        vector[5],
        sum_a[1],
        sum_b[0],
        vector[6],
        sum_b[1],
        vector[13],
        vector[0],
        vector[1],
        vector[2],
        vector[3],
        vector[4],
        vector[12],
        up_sum,
        bias_up_sum,
        down_sum,
        vector[9],
        vector[10],
        vector[11],
        vector[8],
    )


def solution(mesh):
    batch, query = mesh.devices.shape
    split = Mesh(mesh.devices.reshape(batch // 4, 2, 2, query), (*BATCH, "query"))
    crop, rows, flat = P(BATCH, "query", None), P((*BATCH, "query"), None), P((*BATCH, "query"))
    in_specs = (crop, crop, P(BATCH, None), rows, flat, rows, rows, flat, rows, *[flat] * 7, rows, flat, rows, *[flat] * 4, crop)
    out_specs = (crop, crop, crop, rows, flat, rows, rows, flat, rows, *[flat] * 7, rows, flat, rows, *[flat] * 4)
    return jax.shard_map(local, mesh=split, in_specs=in_specs, out_specs=out_specs, check_vma=False)
```

```python
import functools
import math

import jax
import jax.numpy as jnp
import ml_dtypes
import numpy as np
from jax import lax
from jax.experimental import pallas as pl
from jax.experimental.pallas import tpu as pltpu
from jax.sharding import Mesh
from jax.sharding import PartitionSpec as P

BATCH = ("ring", "x", "core")
HEADS = 12
GRID = 14
GROUP = 4
PACK_MIB = 16
CHUNK = 768
EPSILON = 1e-06
BIAS_QUERY = 0
BIAS_VALUE = 1
BIAS_OUT = 2
GAIN_QUERY = 3
SHIFT_QUERY = 4
GAIN_KEY = 5
GAIN_VALUE = 6
SHIFT_VALUE = 7
SCALE_ATTENTION = 8
BIAS_DOWN = 9
GAIN_FEED = 10
SHIFT_FEED = 11
SCALE_FEED = 12
SMALLS = 13
BIAS_ROW = 16
LINE_ROWS = 24
ANY = pl.ANY
SMEM = pltpu.SMEM


class Net:
    def __init__(self):
        self.ring = lax.axis_size("ring")
        batch = 4 * self.ring
        self.units = batch
        self.count = batch * lax.axis_size("query")
        self.at_ring, self.at_x, self.at_core = lax.axis_index("ring"), lax.axis_index("x"), lax.axis_index("core")
        self.at_y = lax.axis_index("query")
        slot = jnp.arange(batch)
        core, x, step = slot // (2 * self.ring), (slot // self.ring) % 2, slot % self.ring
        rest = 2 * (x ^ self.at_x) + (core ^ self.at_core)
        self.gathered = (4 * ((self.at_ring - step) % self.ring) + rest).astype(jnp.int32)
        self.scattered = (4 * ((self.at_ring + step) % self.ring) + rest).astype(jnp.int32)

    def turn(self, values, step):
        return lax.ppermute(values, "ring", [(place, (place + step) % self.ring) for place in range(self.ring)])

    def turns(self, values):
        return [values] + [self.turn(values, step) for step in range(1, self.ring)]

    def swap_x(self, values):
        return lax.ppermute(values, "x", [(0, 1), (1, 0)])

    def swap_core(self, values):
        return lax.ppermute(values, "core", [(0, 1), (1, 0)])

    def swap_y(self, values):
        return lax.ppermute(values, "query", [(0, 1), (1, 0)])

    def pair(self, own, came, tiles):
        first = jnp.where(self.at_y == 0, own, came)
        last = jnp.where(self.at_y == 0, came, own)
        slots, rows, width = own.shape
        both = jnp.stack([part.reshape(slots, tiles, -1, width) for part in (first, last)], axis=2)
        return both.reshape(slots, tiles, -1, width)

    def core_pairs(self, parts):
        return list(parts) + [self.swap_core(part) for part in parts]

    def aligned(self, parts, units):
        places = self.gathered[:units] if units == self.units else self.gathered[:units] // 2
        if parts[0].shape[2] % 16 == 0:
            return parts, places
        _, tiles, _, width = parts[0].shape
        back = jnp.zeros_like(places).at[places].set(jnp.arange(units, dtype=jnp.int32))
        whole = jnp.swapaxes(jnp.concatenate(parts)[back], 0, 1)
        count = whole.shape[1] * whole.shape[2] // 48
        return [jnp.swapaxes(whole.reshape(tiles, count, 48, width), 0, 1)], jnp.arange(count, dtype=jnp.int32)

    def aligned_cores(self, parts):
        if parts[0].shape[2] % 16 == 0:
            return parts, self.gathered
        flat = jnp.concatenate([part[:, core] for core in range(2) for part in parts])[:, None]
        return self.aligned([flat], self.units)

    def feed_units(self, following, units):
        down, down_y, up, up_x = following
        if down.shape[1] % 16 == 0:
            down_parts, places = [down[:, None], down_y[:, None]], 2 * (self.gathered[:units] // 2)
            down_places = jnp.concatenate([places + self.at_y, places + 1 - self.at_y]).astype(jnp.int32)
        else:
            down_parts, down_places = self.aligned([self.pair(down, down_y, 1)], units)
        up_parts, up_places = self.aligned_cores([up, up_x])
        down_plan = [(part, (index, 0)) for part, array in enumerate(down_parts) for index in range(array.shape[0])]
        up_plan = [
            (len(down_parts) + part, (index, tile))
            for tile in range(up_parts[0].shape[1]) for part, array in enumerate(up_parts) for index in range(array.shape[0])
        ]
        return [*down_parts, *up_parts], (down_plan, down_places, up_plan, up_places)

    def slots(self, rows):
        if rows // self.units % 16 == 0:
            return self.units, self.scattered
        return rows // 48, jnp.arange(rows // 48, dtype=jnp.int32)

    def unaligned(self, keep, send):
        tiles, _, _, width = keep.shape
        if keep.shape[1] * 2 != self.units or keep.shape[2] % 16 != 0:
            whole = jnp.concatenate([keep, send], axis=1).reshape(tiles, self.units, -1, width)[:, self.scattered]
            keep, send = whole[:, : self.units // 2], whole[:, self.units // 2 :]
        return [part.reshape(tiles, self.units // 2, 2, -1, width) for part in (keep, send)]

    def mine(self, part):
        return lax.dynamic_index_in_dim(part, self.at_y, 2, keepdims=False).astype(jnp.float32)

    def other(self, part):
        return lax.dynamic_index_in_dim(part, 1 - self.at_y, 2, keepdims=False).astype(jnp.float32)

    def moves(self, sends, *others):
        kinds = dict(x=self.swap_x, y=self.swap_y, core=self.swap_core, turn=self.turn)
        values, others = lax.optimization_barrier(([send[1] for send in sends], others))
        came = [kinds[kind](value, *rest) for (kind, _, *rest), value in zip(sends, values)]
        return came, others

    def scatter_second(self, first):
        keep_a, keep_b, came_a, came_b = first
        ring, f32, low = self.ring, jnp.float32, jnp.bfloat16
        away_a = (keep_a[:, ring:].astype(f32) + came_a[:, ring:].astype(f32)).astype(low)
        away_b = (self.other(keep_b) + self.other(came_b)).astype(low)
        return ((keep_a[:, :ring], came_a[:, :ring]), (keep_b, came_b)), [("x", away_a), ("y", away_b)]

    def feed_second(self, keep, send, up):
        return ((keep,), (up,)), [("x", send), ("y", self.other(up).astype(up.dtype))]

    def scatter_third(self, kept, came):
        (parts_a, parts_b), (next_a, next_b) = kept, came
        ring, f32, low = self.ring, jnp.float32, jnp.bfloat16
        total = lambda pick, parts: sum((pick(part) for part in parts[1:]), pick(parts[0]))
        parts_a = (*parts_a, next_a)
        away_a = total(self.other, parts_a).astype(low)
        away_b = total(lambda part: self.mine(part[:, ring:]), parts_b) + next_b[:, ring:].astype(f32)
        return (parts_a, (parts_b, next_b)), [("y", away_a), ("x", away_b.astype(low))]

    def scatter_fourth(self, kept, came):
        (parts_a, (parts_b, next_b)), (last_a, last_b) = kept, came
        ring, f32, low = self.ring, jnp.float32, jnp.bfloat16
        total = lambda pick, parts: sum((pick(part) for part in parts[1:]), pick(parts[0]))
        sum_a = total(self.mine, parts_a) + last_a.astype(f32)
        sum_b = total(lambda part: self.mine(part[:, :ring]), parts_b) + next_b[:, :ring].astype(f32) + last_b.astype(f32)
        flat = lambda part: part.reshape(-1, part.shape[-1])
        pieces = [jnp.concatenate([flat(sum_a[:, step]), flat(sum_b[:, step])]) for step in range(self.ring)]
        shape = (sum_a.shape[0],) + sum_a.shape[2:]
        return (shape, pieces[0]), [("turn", pieces[step].astype(low), step) for step in range(1, self.ring)]

    def scatter_last(self, kept, came):
        shape, total = kept
        for piece in came:
            total = total + piece.astype(jnp.float32)
        rows = shape[0] * shape[1]
        return total[:rows].reshape(shape), total[rows:]


def standard(values):
    centered = values - jnp.mean(values, axis=-1, keepdims=True)
    scale = lax.rsqrt(jnp.mean(centered * centered, axis=-1, keepdims=True) + EPSILON)
    return centered * scale, scale


def standard_back(grad, normed, scale, gain):
    slope = grad * gain
    inner = jnp.mean(slope * normed, axis=-1, keepdims=True)
    return (slope - jnp.mean(slope, axis=-1, keepdims=True) - normed * inner) * scale


def wide(ref):
    return ref[...].astype(jnp.float32)


def dot(left, right, left_dim=1, right_dim=0):
    return lax.dot_general(left, right, (((left_dim,), (right_dim,)), ((), ())), preferred_element_type=jnp.float32)


def rows_sum(values):
    return jnp.sum(values, axis=0, keepdims=True)


def by_head(rows):
    lane = lax.broadcasted_iota(jnp.int32, rows.shape, 1)
    head = rows.shape[1] // GROUP
    zero = jnp.zeros_like(rows)
    return jnp.concatenate(
        [jnp.where((lane >= head * h) & (lane < head * (h + 1)), rows, zero) for h in range(GROUP)], axis=0
    )


def from_heads(stacked):
    count = stacked.shape[0] // GROUP
    head = stacked.shape[1] // GROUP
    lane = lax.broadcasted_iota(jnp.int32, (count, stacked.shape[1]), 1)
    result = stacked[:count]
    for h in range(1, GROUP):
        result = jnp.where(lane >= head * h, stacked[count * h : count * (h + 1)], result)
    return result


def fetch(slots_ref, units, whole, sem):
    for slot, unit in enumerate(units):
        rows = unit.shape[0]
        place = pl.multiple_of(slots_ref[slot] * rows, 16)
        pltpu.make_async_copy(unit, whole.at[pl.ds(place, rows)], sem).start()


def units_of(parts, tile):
    return [part.at[index, tile] for part in parts for index in range(part.shape[0])]


def store(slots_ref, whole, parts, sem):
    slot = 0
    for part in parts:
        rows = part.shape[-2]
        for index in range(part.shape[-3]):
            if len(part.shape) == 3:
                place = pl.multiple_of(slots_ref[slot] * rows, 16)
                pltpu.make_async_copy(whole.at[pl.ds(place, rows)], part.at[index], sem).start()
            else:
                for half in range(2):
                    place = pl.multiple_of((2 * slots_ref[slot] + half) * rows, 16)
                    pltpu.make_async_copy(whole.at[pl.ds(place, rows)], part.at[half, index], sem).start()
            slot += 1


def finish(whole, sem):
    pltpu.make_async_copy(whole, whole, sem).wait()


def layout(visible, masked):
    padded = -(-visible // 8) * 8
    starts = (0, masked, 2 * masked, 2 * masked + padded)
    return starts, -(-(2 * masked + 2 * padded) // 16) * 16


def prepare_kernel(
    place_ref, own_ref, own_latent_ref, came_ref, table_ref, key_ref, value_ref, key_scale_ref, value_scale_ref, rows_ref
):
    masked, visible = own_ref.shape[1], own_latent_ref.shape[1]
    starts, _ = layout(visible, masked)
    rows_ref[...] = jnp.zeros_like(rows_ref)
    rows_ref[:masked] = wide(own_ref.at[0])
    rows_ref[masked : 2 * masked] = came_ref[0, :masked].astype(jnp.float32)
    rows_ref[starts[2] : starts[2] + visible] = wide(own_latent_ref.at[0])
    rows_ref[starts[3] : starts[3] + visible] = came_ref[0, 2 * masked :].astype(jnp.float32)
    rows = rows_ref[...]
    place = place_ref[0]
    lane = lax.broadcasted_iota(jnp.int32, (rows.shape[0], table_ref.shape[0]), 1)
    wanted = jnp.where((lane & 16) == 0, place[:, 0:1], place[:, 1:2])
    chosen = jnp.where((lane & 15) == wanted, 1.0, 0.0).astype(jnp.bfloat16)
    position = dot(chosen, table_ref[...])
    key_ref[0], key_scale_ref[0] = standard(rows + position)
    value_ref[0], value_scale_ref[0] = standard(rows)


def attend_kernel(visible, factor, parts_a, parts_b, *refs):
    slots_ref, key_hat_ref, value_hat_ref, own_ref, came_ref, small_ref = refs[:6]
    part_a, part_b, refs = refs[6 : 6 + parts_a], refs[6 + parts_a : 6 + parts_a + parts_b], refs[6 + parts_a + parts_b :]
    query_ref, key_ref, value_ref, probs_ref, attended_ref, branch_ref, feed_hat_ref, feed_scale_ref, feed_ref = refs[-17:-8]
    normed_refs = refs[-8:-5]
    query_w, key_w, value_w, out_w, sems = refs[-5:]

    @pl.when(pl.program_id(0) == 0)
    def _():
        for index, (parts, tile, whole) in enumerate(
            ((part_a, 0, query_w), (part_a, 1, key_w), (part_b, 0, value_w), (part_b, 1, out_w))
        ):
            fetch(slots_ref, units_of(parts, tile), whole, sems.at[index])
        for index, whole in enumerate((query_w, key_w, value_w, out_w)):
            finish(whole, sems.at[index])

    small = lambda row: small_ref[row : row + 1]
    count = attended_ref.shape[1]
    low = jnp.bfloat16
    query_normed = (key_hat_ref[0, :count] * small(GAIN_QUERY) + small(SHIFT_QUERY)).astype(low)
    key_normed = (key_hat_ref[0] * small(GAIN_KEY)).astype(low)
    value_normed = (value_hat_ref[0] * small(GAIN_VALUE) + small(SHIFT_VALUE)).astype(low)
    for ref, value in zip(normed_refs, (query_normed, key_normed, value_normed)):
        ref[0] = value
    query_ref[0] = (dot(query_normed, query_w[...]) + small(BIAS_QUERY)).astype(low)
    key_ref[0] = dot(key_normed, key_w[...]).astype(low)
    value_ref[0] = (dot(value_normed, value_w[...]) + small(BIAS_VALUE)).astype(low)
    width = key_ref.shape[2] // probs_ref.shape[1]
    for quad in range(probs_ref.shape[1]):
        lanes = slice(width * quad, width * (quad + 1))
        scores = dot(key_ref[0, :, lanes], by_head(query_ref[0, :, lanes]), 1, 1) * factor
        row = lax.broadcasted_iota(jnp.int32, scores.shape, 0)
        starts, _ = layout(visible, own_ref.shape[1])
        real = (row < starts[2] + visible) | ((row >= starts[3]) & (row < starts[3] + visible))
        scores = jnp.where(real, scores, -1e30)
        raised = jnp.exp(scores - jnp.max(scores, axis=0, keepdims=True))
        probs = (raised * (1.0 / rows_sum(raised))).astype(low)
        probs_ref[0, quad] = probs
        attended_ref[0, :, lanes] = from_heads(dot(probs, value_ref[0, :, lanes], 0, 0)).astype(low)
    branch = dot(attended_ref[0], out_w[...]) + small(BIAS_OUT)
    branch_ref[0] = branch
    queries = jnp.concatenate([wide(own_ref.at[0]), wide(came_ref.at[0])], axis=0)
    hat, scale = standard(queries + small(SCALE_ATTENTION) * branch)
    feed_hat_ref[0] = hat
    feed_scale_ref[0] = scale
    feed_ref[0] = (hat * small(GAIN_FEED) + small(SHIFT_FEED)).astype(low)


def feed_kernel(last, down_plan, up_plan, parts, *refs):
    slots_ref, down_slots_ref, out_slots_ref, down_out_slots_ref, core_ref = refs[:5]
    feed_ref, feed_other_ref, cot_refs, small_ref, refs = refs[5], refs[6], refs[7:11], refs[11], refs[12:]
    part_refs = refs[:parts]
    down_w, up_w, down_grad, up_grad, sems = refs[-5:]
    refs = refs[parts:-5]
    outs, refs = refs[:3], refs[3:]
    low = jnp.bfloat16
    small = lambda row: small_ref[row : row + 1]
    fetch(slots_ref, [part_refs[part].at[where] for part, where in up_plan], up_w, sems.at[0])
    fetch(down_slots_ref, [part_refs[part].at[where] for part, where in down_plan], down_w, sems.at[1])
    cotangent = []
    for first, second in (cot_refs[:2], cot_refs[2:]):
        for crop in range(first.shape[0]):
            cotangent += [wide(first.at[crop]), wide(second.at[crop])]
    low_grad = (small(SCALE_FEED) * jnp.concatenate(cotangent, axis=0)).astype(low)
    feed = jnp.concatenate([feed_ref[...], feed_other_ref[...]], axis=0)
    bias = small_ref[pl.ds(BIAS_ROW + 2 * last + core_ref[0], 1)]
    finish(up_w, sems.at[0])
    raised = dot(feed, up_w[...]) + bias
    share = 0.5 * (1.0 + lax.erf(raised * (0.5**0.5)))
    activated = (raised * share).astype(low)
    slope = share + raised * jnp.exp(-0.5 * raised * raised) * ((2.0 * math.pi) ** -0.5)
    down_grad[...] = dot(activated, low_grad, 0, 0).astype(low)
    keep, send, up_out = outs
    store(down_out_slots_ref, down_grad, [keep.at[0], send.at[0]], sems.at[2])
    finish(down_w, sems.at[1])
    raised_grad = (dot(low_grad, down_w[...], 1, 1) * slope).astype(low)
    up_grad[...] = dot(feed, raised_grad, 0, 0).astype(low)
    store(out_slots_ref, up_grad, [up_out.at[tile] for tile in range(up_out.shape[0])], sems.at[3])
    refs[0][...] = rows_sum(raised_grad.astype(jnp.float32))
    lowered = dot(activated, down_w[...])
    grad = dot(raised_grad, up_w[...], 1, 1)
    rows = feed_ref.shape[0]
    for index, value in enumerate((lowered, grad)):
        refs[1 + index][...] = value[:rows]
        if last:
            refs[3 + index][...] = value[rows:].astype(low)
        else:
            refs[3][rows * index : rows * (index + 1)] = value[rows:].astype(low)
    finish(down_grad, sems.at[2])
    finish(up_grad, sems.at[3])


def attend_back_kernel(factor, parts_b, *refs):
    slots_ref, query_ref, key_ref, value_ref, probs_ref = refs[:5]
    lowered_refs, back_refs = refs[5:9], refs[9:13]
    cot_own_ref, cot_came_ref, own_ref, came_ref, branch_ref, hat_ref, scale_ref, small_ref = refs[13:21]
    part_b = refs[21 : 21 + parts_b]
    mixed_own_ref, mixed_came_ref, middle_grad_ref, branch_grad_ref, sums_ref = refs[-10:-5]
    query_grad, key_grad, value_grad, out_w, sem = refs[-5:]
    small = lambda row: small_ref[row : row + 1]
    low = jnp.bfloat16

    @pl.when(pl.program_id(0) == 0)
    def _():
        fetch(slots_ref, units_of(part_b, 1), out_w, sem)
        sums_ref[...] = jnp.zeros_like(sums_ref)

    join = lambda first, second: jnp.concatenate([wide(first.at[0]), wide(second.at[0])], axis=0)
    cotangent = join(cot_own_ref, cot_came_ref)
    lowered = sum((wide(ref.at[0]) for ref in lowered_refs), small(BIAS_DOWN))
    branch = branch_ref[0]
    middle = join(own_ref, came_ref) + small(SCALE_ATTENTION) * branch
    mixed = (middle + small(SCALE_FEED) * lowered).astype(low)
    half = mixed_own_ref.shape[1]
    mixed_own_ref[0] = mixed[:half]
    mixed_came_ref[0] = mixed[half:]
    grad = sum((wide(ref.at[0]) for ref in back_refs[1:]), wide(back_refs[0].at[0]))
    hat = hat_ref[0]
    middle_grad = cotangent + standard_back(grad, hat, scale_ref[0], small(GAIN_FEED))
    middle_grad_ref[0] = middle_grad
    branch_grad = (small(SCALE_ATTENTION) * middle_grad).astype(low)
    branch_grad_ref[0] = branch_grad
    sums_ref[0:1] += rows_sum(cotangent * lowered)
    sums_ref[1:2] += rows_sum((small(SCALE_FEED) * cotangent).astype(low).astype(jnp.float32))
    sums_ref[2:3] += rows_sum(grad * hat)
    sums_ref[3:4] += rows_sum(grad)
    sums_ref[4:5] += rows_sum(middle_grad * branch)
    sums_ref[5:6] += rows_sum(branch_grad.astype(jnp.float32))

    @pl.when(pl.program_id(0) == 0)
    def _():
        finish(out_w, sem)

    above = dot(branch_grad, out_w[...], 1, 1).astype(low)
    width = key_ref.shape[2] // probs_ref.shape[1]
    for quad in range(probs_ref.shape[1]):
        lanes = slice(width * quad, width * (quad + 1))
        probs_low = probs_ref[0, quad]
        probs = probs_low.astype(jnp.float32)
        heads = by_head(above[:, lanes])
        probs_grad = dot(value_ref[0, :, lanes], heads, 1, 1)
        inner = rows_sum(probs_grad * probs)
        score_grad = (probs * (probs_grad - inner)).astype(low)
        value_grad[0, :, lanes] = dot(probs_low, heads).astype(low)
        key_grad[0, :, lanes] = (dot(score_grad, by_head(query_ref[0, :, lanes])) * factor).astype(low)
        query_grad[0, :, lanes] = (from_heads(dot(score_grad, key_ref[0, :, lanes], 0, 0)) * factor).astype(low)


def input_back_kernel(parts_a, parts_b, *refs):
    slots_ref, query_grad, key_grad, value_grad, key_hat_ref, value_hat_ref, key_scale_ref, value_scale_ref = refs[:8]
    middle_grad_ref, mixed_ref, small_ref = refs[8:11]
    part_a, part_b, refs = refs[11 : 11 + parts_a], refs[11 + parts_a : 11 + parts_a + parts_b], refs[11 + parts_a + parts_b :]
    masked_ref, latent_ref, away_ref, sums_ref, query_w, key_w, value_w, sems = refs[-8:]

    @pl.when(pl.program_id(0) == 0)
    def _():
        for index, (parts, tile, whole) in enumerate(((part_a, 0, query_w), (part_a, 1, key_w), (part_b, 0, value_w))):
            fetch(slots_ref, units_of(parts, tile), whole, sems.at[index])
        for index, whole in enumerate((query_w, key_w, value_w)):
            finish(whole, sems.at[index])

    small = lambda row: small_ref[row : row + 1]
    count = query_grad.shape[1]

    @pl.when(pl.program_id(0) == 0)
    def _():
        sums_ref[...] = jnp.zeros_like(sums_ref)

    key_hat, key_scale = key_hat_ref[0], key_scale_ref[0]
    query_hat = key_hat[:count]
    value_hat = value_hat_ref[0]
    from_query = dot(query_grad[0], query_w[...], 1, 1)
    from_key = dot(key_grad[0], key_w[...], 1, 1)
    from_value = dot(value_grad[0], value_w[...], 1, 1)
    sums_ref[0:1] += rows_sum(from_query * query_hat)
    sums_ref[1:2] += rows_sum(from_query)
    sums_ref[2:3] += rows_sum(from_key * key_hat)
    sums_ref[3:4] += rows_sum(from_value * value_hat)
    sums_ref[4:5] += rows_sum(from_value)
    sums_ref[5:6] += rows_sum(wide(query_grad.at[0]))
    sums_ref[6:7] += rows_sum(wide(value_grad.at[0]))
    both = standard_back(from_key, key_hat, key_scale, small(GAIN_KEY)) + standard_back(
        from_value, value_hat, value_scale_ref[0], small(GAIN_VALUE)
    )
    query_part = standard_back(from_query, query_hat, key_scale[:count], small(GAIN_QUERY))
    masked = middle_grad_ref[0] + query_part + both[:count]
    size, visible = masked_ref.shape[1], latent_ref.shape[1]
    starts, _ = layout(visible, size)
    masked_ref[0] = masked[:size]
    latent_ref[0] = both[starts[2] : starts[2] + visible]
    away_ref[0, :size] = masked[size:].astype(away_ref.dtype)
    away_ref[0, size : 2 * size] = mixed_ref[0]
    away_ref[0, 2 * size :] = both[starts[3] : starts[3] + visible].astype(away_ref.dtype)


def weights_back_kernel(
    out_slots_ref, attended, branch_grad, value_normed, value_grad, key_normed, key_grad, query_normed, query_grad,
    keep_a, send_a, keep_b, send_b, *refs,
):
    inputs = (attended, branch_grad, value_normed, value_grad, key_normed, key_grad, query_normed, query_grad)
    held, wholes, sems = refs[:8], refs[8:12], refs[12]
    copies = [pltpu.make_async_copy(ref, scratch, sems.at[4 + k]) for k, (ref, scratch) in enumerate(zip(inputs, held))]
    for copy in copies:
        copy.start()
    targets = ((keep_b, send_b, 1), (keep_b, send_b, 0), (keep_a, send_a, 1), (keep_a, send_a, 0))
    for index, (keep, send, tile) in enumerate(targets):
        copies[2 * index].wait()
        copies[2 * index + 1].wait()
        wholes[index][...] = dot(held[2 * index][...], held[2 * index + 1][...], 0, 0).astype(jnp.bfloat16)
        store(out_slots_ref, wholes[index], [keep.at[tile], send.at[tile]], sems.at[index])
    for index in range(4):
        finish(wholes[index], sems.at[index])


def call(name, kernel, grid, ins, outs, operands, scratch=(), after=(), us=3, mib=54):
    ins = list(ins) + [ANY] * len(after)
    operands = tuple(operands) + tuple(after)

    def spec(entry, shape):
        if entry is None:
            return pl.BlockSpec(shape, lambda *i: (0,) * len(shape))
        if entry in (ANY, SMEM, pltpu.HBM):
            return pl.BlockSpec(memory_space=entry)
        return pl.BlockSpec(*entry)

    return pl.pallas_call(
        kernel,
        name=name,
        grid=grid,
        in_specs=[spec(pltpu.HBM if entry is ANY else entry, operand.shape) for entry, operand in zip(ins, operands, strict=True)],
        out_specs=[spec(entry, shape) for entry, shape, _ in outs],
        out_shape=[jax.ShapeDtypeStruct(shape, dtype) for _, shape, dtype in outs],
        scratch_shapes=list(scratch),
        compiler_params=pltpu.CompilerParams(vmem_limit_bytes=mib << 20),
        cost_estimate=pl.CostEstimate(flops=int(us * 1.1e9), bytes_accessed=int(us * 3.5e6), transcendentals=0),
    )(*operands)


def by_crop(shape):
    block = (1,) + tuple(shape[1:])
    return block, lambda i: (i,) + (0,) * (len(block) - 1)


def pack_kernel(vectors, *refs):
    *in_refs, out_ref = refs
    low = jnp.bfloat16
    parts = [wide(ref) for ref in in_refs[vectors + bool(vectors) :]]
    if vectors:
        device_ref, thin, bias_ref = in_refs[0], in_refs[1:vectors], in_refs[vectors]
        width = out_ref.shape[1]
        device = device_ref[0]
        shard, half = thin[0].shape[0], bias_ref.shape[0] // 2
        rows = jnp.concatenate(
            [pad_lanes(wide(ref).reshape(1, -1), 128) for ref in thin]
            + [jnp.zeros((BIAS_ROW - len(thin), 128), jnp.float32)], axis=0
        )
        value = lax.broadcasted_iota(jnp.int32, (128, width), 0)
        lane = lax.broadcasted_iota(jnp.int32, (128, width), 1)
        there = (lane == shard * device + value) & (value < shard)
        line = [dot(rows.astype(low), jnp.where(there, 1.0, 0.0).astype(low))]
        bias = jnp.broadcast_to(pad_lanes(wide(bias_ref).reshape(1, -1), 128), (8, 128)).astype(low)
        row = lax.broadcasted_iota(jnp.int32, (8, width), 0)
        strips = jnp.zeros((8, width), jnp.float32)
        column = half * (2 * lax.div(device, 4) + lax.rem(device, 2))
        for part in range(2):
            inside = (value >= half * part) & (value < half * (part + 1))
            there = (lane == column + value - half * part) & inside
            spot = row == 2 * part + lax.rem(lax.div(device, 2), 2)
            strips = jnp.where(spot, dot(bias, jnp.where(there, 1.0, 0.0).astype(low)), strips)
        middle = len(parts) // 2
        parts = parts[:middle] + line + [strips] + parts[middle:]
    out_ref[...] = jnp.concatenate(parts, axis=0).astype(out_ref.dtype)


def pad_lanes(rows, width):
    if rows.shape[1] == width:
        return rows
    return jnp.concatenate([rows, jnp.zeros((rows.shape[0], width - rows.shape[1]), rows.dtype)], axis=1)


def pack(parts, device=None, vectors=()):
    width, dtype = parts[0].shape[1], parts[0].dtype
    first = (device.reshape(1), *vectors) if vectors else ()
    ins = [SMEM] + [None] * len(vectors) if vectors else []
    run = lambda operands: call(
        "pack", functools.partial(pack_kernel, len(vectors)), (), ins + [None] * len(operands),
        [(None, (sum(part.shape[0] for part in operands) + LINE_ROWS * bool(vectors), width), dtype)], (*first, *operands), mib=PACK_MIB,
    )[0]
    if all(part.shape[0] % 8 == 0 for part in parts):
        return run(parts)
    if not vectors:
        return jnp.concatenate(parts)
    half = len(parts) // 2
    blank = jnp.zeros((8, width), dtype)
    line = run([blank, blank])[8 : 8 + LINE_ROWS]
    return jnp.concatenate([*parts[:half], line, *parts[half:]])


def stage(*values):
    return lax.optimization_barrier(values)


def position_table(width):
    quarter = width // 4
    frequency = 10000.0 ** (-np.arange(quarter) / quarter)
    angle = np.arange(16)[:, None] * frequency
    wave = np.concatenate([np.sin(angle), np.cos(angle)], axis=1)
    table = np.zeros((32, width))
    table[:16, : width // 2] = wave
    table[16:, width // 2 :] = wave
    table = table.astype(np.float32)
    high = table.astype(ml_dtypes.bfloat16)
    low = (table - high.astype(np.float32)).astype(ml_dtypes.bfloat16)
    return np.concatenate([high, low])


def local(
    latents, queries, order, weight_query, bias_query, weight_key, weight_value, bias_value, weight_out, bias_out,
    gain_query, shift_query, gain_key, gain_value, shift_value, scale_attention, weight_up, bias_up, weight_down,
    bias_down, gain_feed, shift_feed, scale_feed, cotangent,
):
    low = jnp.bfloat16
    net = Net()
    slot = lax.axis_index("query")
    crops = latents.shape[0] // 2
    visible, masked = latents.shape[1], queries.shape[1]
    shard, width = weight_query.shape
    count = net.count
    _, rows = layout(visible, masked)
    block = lambda values, which: lax.dynamic_slice_in_dim(values, which * crops, crops, 0)
    own_latents, own_queries, own_cot = [block(v, slot) for v in (latents, queries, cotangent)]
    vectors = [
        bias_query, bias_value, bias_out, gain_query, shift_query, gain_key, gain_value, shift_value, scale_attention,
        bias_down, gain_feed, shift_feed, scale_feed, bias_up,
    ]
    device = (2 * (4 * net.at_ring + 2 * net.at_x + net.at_core) + slot).astype(jnp.int32)
    deep = weight_down.shape[0]
    half = deep // 2
    f32 = jnp.float32
    ring = net.ring
    pairs = 2 * ring
    flat = lambda values: values.reshape(-1, values.shape[-1])

    own_a = pack([weight_query, weight_key, weight_value, weight_out], device, vectors)
    turn_all = lambda value: [("turn", value, step) for step in range(1, ring)]
    away = jnp.concatenate([block(values, 1 - slot) for values in (queries, cotangent, latents)], axis=1)
    (*rings_a, came), (own_a, weight_up, weight_down, own_cot, order) = net.moves(
        [*turn_all(own_a), ("y", away)], own_a, weight_up, weight_down, own_cot, order
    )
    rings_a = [own_a, *rings_a]
    ups = jnp.moveaxis(weight_up.reshape(shard, pairs, 2, 2, 2, half), (2, 4), (0, 1)).reshape(2, 2, shard, width)
    up_own = lax.dynamic_index_in_dim(ups, net.at_core, 0, keepdims=False)
    up_came = net.swap_core(lax.dynamic_index_in_dim(ups, 1 - net.at_core, 0, keepdims=False))
    table = jnp.asarray(position_table(width))
    own_order = block(order, slot)
    part = lambda start, size, which: lax.dynamic_slice_in_dim(own_order, start + which * size, size, 1)
    gap = jnp.full((crops, rows // 2 - masked - visible), -1, jnp.int32)
    indices = jnp.concatenate(
        [
            part(2 * visible, masked, slot), part(2 * visible, masked, 1 - slot),
            part(0, visible, slot), gap, part(0, visible, 1 - slot), gap,
        ],
        axis=1,
    )
    steps = jnp.stack([indices // GRID, jnp.where(indices < 0, -1, indices % GRID)], axis=-1)
    own_b, own_c = [pack([weight_down[half * k : half * (k + 1)], up_own[k], up_came[k]]) for k in range(2)]
    rings_a, came, own_b, own_c, steps = stage(rings_a, came, own_b, own_c, steps)

    cut = 2 * shard
    line = sum(piece[cut : cut + LINE_ROWS] for piece in rings_a[1:]) + rings_a[0][cut : cut + LINE_ROWS]
    one = jnp.concatenate([piece[:cut] for piece in rings_a] + [line])
    two = jnp.stack([piece[cut + LINE_ROWS :] for piece in rings_a])
    (*rings_b, one_x, two_y), (own_b, one, two, came) = net.moves(
        [*turn_all(own_b), ("x", one), ("y", two)], own_b, one, two, came
    )
    crop_out = lambda shape, dtype: (by_crop(shape), shape, dtype)
    wide_shape, thin_shape = (crops, rows, width), (crops, rows, 1)
    operands = (steps, own_queries, own_latents, came, table)
    key_hat, value_hat, key_scale, value_scale = call(
        "prepare", prepare_kernel, (crops,), [by_crop(a.shape) for a in operands[:4]] + [None],
        [crop_out(wide_shape, f32)] * 2 + [crop_out(thin_shape, f32)] * 2, operands, scratch=[pltpu.VMEM((rows, width), f32)], mib=54,
    )
    one_x, two_y, rings_b, key_hat, value_hat, key_scale, value_scale = stage(
        one_x, two_y, [own_b, *rings_b], key_hat, value_hat, key_scale, value_scale
    )

    line = one[ring * cut :] + one_x[ring * cut :]
    one = jnp.concatenate([one[: ring * cut], one_x[: ring * cut], line])
    two = net.pair(two, two_y, 2)
    (*rings_c, one_y, two_x), (own_c, one, two) = net.moves([*turn_all(own_c), ("y", one), ("x", two)], own_c, one, two)
    one_y, two_x, rings_c = stage(one_y, two_x, [own_c, *rings_c])

    line = one[pairs * cut :] + one_y[pairs * cut :]
    units = lambda values: values[: pairs * cut].reshape(pairs, cut, width)
    one = net.pair(units(one), units(one_y), 2)
    pieces = list(zip(rings_b, rings_c))
    downs = jnp.stack([jnp.concatenate([b[:half], c[:half]]) for b, c in pieces])
    ups = jnp.stack([jnp.concatenate([b[half:], c[half:]]) for b, c in pieces])
    sends = [("core", value) for value in (one, two, two_x, line)]
    (downs_x, ups_y, one_core, two_core, two_x_core, line_core), (one, two, two_x, line, downs, ups) = net.moves(
        [("x", downs), ("y", ups), *sends], one, two, two_x, line, downs, ups
    )
    part_a, part_b = [one, one_core], [two, two_x, two_core, two_x_core]
    small = line.astype(f32) + line_core.astype(f32)
    part_a, part_b, small = stage(part_a, part_b, small)
    (part_a, places), (part_b, _) = net.aligned(part_a, net.units), net.aligned(part_b, net.units)
    slots, out_places = net.slots(width)
    ask_shape = (crops, 2 * masked, width)
    dma = pltpu.SemaphoreType.DMA
    square_vmem = pltpu.VMEM((width, width), low)
    quads = HEADS // GROUP
    factor = (width // HEADS) ** -0.5
    probs_shape = (crops, quads, rows, GROUP * 2 * masked)
    of_came = lambda part: ((1, masked, width), lambda i: (i, part, 0))
    operands = (places, key_hat, value_hat, own_queries, came, small, *part_a, *part_b)
    parts = len(part_a) + len(part_b)
    query_p, key_p, value_p, probs, attended, branch, feed_hat, feed_scale, feed, *normed = call(
        "attend", functools.partial(attend_kernel, visible, factor, len(part_a), len(part_b)), (crops,),
        [SMEM] + [by_crop(a.shape) for a in operands[1:4]] + [of_came(0), None] + [ANY] * parts,
        [
            crop_out(ask_shape, low), crop_out(wide_shape, low), crop_out(wide_shape, low), crop_out(probs_shape, low),
            crop_out(ask_shape, low), crop_out(ask_shape, f32), crop_out(ask_shape, f32),
            crop_out((crops, 2 * masked, 1), f32), crop_out(ask_shape, low),
            crop_out(ask_shape, low), crop_out(wide_shape, low), crop_out(wide_shape, low),
        ],
        operands, scratch=[square_vmem] * 4 + [dma((4,))],
    )
    downs_x, ups_y, query_p, key_p, value_p, probs, attended, branch, feed_hat, feed_scale, feed, normed = stage(
        downs_x, ups_y, query_p, key_p, value_p, probs, attended, branch, feed_hat, feed_scale, feed, normed
    )

    def second_of(k):
        own, other = slice(half * k, half * (k + 1)), slice(2 * shard * k, 2 * shard * (k + 1))
        return jnp.concatenate([downs[:, own], downs_x[:, own]]), net.pair(ups[:, other], ups_y[:, other], 2)

    feed = flat(feed)
    down_b, up_b = second_of(0)
    (down_b_y, up_b_x, feed_other, *other_cot), (down_b, up_b, feed, own_cot, came) = net.moves(
        [("y", down_b), ("x", up_b), ("core", feed), ("core", own_cot), ("core", came)], down_b, up_b, feed, own_cot, came
    )
    down_c, up_c = second_of(1)
    down_b_y, up_b_x, feed_other, other_cot, down_c, up_c = stage(down_b_y, up_b_x, feed_other, other_cot, down_c, up_c)
    parts_b, where_b = net.feed_units((down_b, down_b_y, up_b, up_b_x), pairs)
    (down_c_y, up_c_x), (down_c, up_c, parts_b) = net.moves([("y", down_c), ("x", up_c)], down_c, up_c, parts_b)
    asks = crops * 2 * masked
    core = net.at_core.reshape(1).astype(jnp.int32)
    aligned = slots == net.units and half % 16 == 0
    down_out_places = out_places[:pairs] // 2 if aligned else out_places

    def feed_call(name, parts, where, last):
        down_plan, down_places, up_plan, up_places = where
        operands = (
            up_places, down_places, out_places, down_out_places, core, feed, feed_other, own_cot, came, *other_cot, small,
        )
        of_cot = ((crops, masked, width), lambda i: (0, 1, 0))
        ins = [SMEM] * 5 + [None] * 3 + [of_cot, None, of_cot, None] + [ANY] * len(parts)
        down_shape = (1, 2, ring, half, width) if aligned else (1, slots // 2, width // slots, width)
        outs = [(ANY, down_shape, low)] * 2 + [(ANY, (2, slots // 2, width // slots, width), low), (None, (1, width), f32)]
        outs += [(None, (asks, width), f32)] * 2 + [(None, (asks if last else 2 * asks, width), low)] * (1 + last)
        return call(
            name, functools.partial(feed_kernel, last, down_plan, up_plan, len(parts)), (1,), ins, outs,
            (*operands, *parts), scratch=[square_vmem] * 4 + [dma((4,))],
        )

    def feed_grads(keep, send, up):
        if aligned:
            keep, send = jnp.moveaxis(keep, 1, 2), jnp.moveaxis(send, 1, 2)
            up = up.reshape(2, pairs, 2, shard, width)
        else:
            down = jnp.concatenate([keep, send], axis=1).reshape(1, pairs, 2, half, width)[:, net.scattered[:pairs] // 2]
            keep, send = down[:, :ring], down[:, ring:]
            up = up.reshape(net.units, 2, shard, width)[net.scattered].reshape(2, pairs, 2, shard, width)
        return net.feed_second(keep, send, up)

    down_keep, down_send, up_out, bias_b, *partial_b = feed_call("feed0", parts_b, where_b, 0)
    down_c_y, up_c_x, down_keep, down_send, up_out, bias_b, partial_b = stage(
        down_c_y, up_c_x, down_keep, down_send, up_out, bias_b, partial_b
    )

    parts_c, where_c = net.feed_units((down_c, down_c_y, up_c, up_c_x), pairs)
    kept_b, sends = feed_grads(down_keep, down_send, up_out)
    (swapped_b, *came_b), (kept_b, partial_b, parts_c) = net.moves(
        [("core", partial_b[2]), *sends], kept_b, partial_b, parts_c
    )
    down_keep, down_send, up_out, bias_c, *partial_c = feed_call("feed1", parts_c, where_c, 1)
    swapped_c = [net.swap_core(values) for values in partial_c[2:]]
    came_b, down_keep, down_send, up_out, bias_c, swapped_b, partial_c, swapped_c = stage(
        came_b, down_keep, down_send, up_out, bias_c, swapped_b, partial_c, swapped_c
    )
    of_crops = lambda values: values.reshape(ask_shape)
    swapped = [swapped_b.reshape(2 * crops, *ask_shape[1:]), *[of_crops(values) for values in swapped_c]]
    partials = [of_crops(values) for values in (partial_b[0], partial_c[0], partial_b[1], partial_c[1])]

    kept_c, sends = feed_grads(down_keep, down_send, up_out)
    came_c, (kept_c, partials, swapped) = net.moves(sends, kept_c, partials, swapped)
    operands = (
        places, query_p, key_p, value_p, probs, *partials[:2], *swapped[:2], *partials[2:], swapped[0], swapped[2],
        own_cot, came, own_queries, came, branch, feed_hat, feed_scale, small, *part_b,
    )
    of_swapped = lambda part: [((1, *ask_shape[1:]), lambda i: (i + part * crops, 0, 0)), by_crop(ask_shape)]
    masked_shape, latent_shape = (crops, masked, width), (crops, visible, width)
    sums_out = (None, (8, width), f32)
    mixed_own, mixed_came, middle_grad, branch_grad, feed_sums, query_grad, key_grad, value_grad = call(
        "attend_back", functools.partial(attend_back_kernel, factor, len(part_b)), (crops,),
        [SMEM] + [by_crop(a.shape) for a in operands[1:7]] + of_swapped(0) + [by_crop(ask_shape)] * 2 + of_swapped(1)
        + [by_crop(own_cot.shape), of_came(1), by_crop(own_queries.shape), of_came(0)]
        + [by_crop(a.shape) for a in operands[17:20]] + [None] + [ANY] * len(part_b),
        [
            crop_out(masked_shape, low), crop_out(masked_shape, low), crop_out(ask_shape, f32), crop_out(ask_shape, low),
            sums_out, crop_out(ask_shape, low), crop_out(wide_shape, low), crop_out(wide_shape, low),
        ],
        operands, scratch=[square_vmem, dma(())],
    )
    came_c, mixed_own, mixed_came, middle_grad, branch_grad, feed_sums, query_grad, key_grad, value_grad = stage(
        came_c, mixed_own, mixed_came, middle_grad, branch_grad, feed_sums, query_grad, key_grad, value_grad
    )

    kept_b, sends_b = net.scatter_third(kept_b, came_b)
    kept_c, sends_c = net.scatter_third(kept_c, came_c)
    came, (kept_b, kept_c, query_grad, key_grad, value_grad) = net.moves(
        [*sends_b, *sends_c], kept_b, kept_c, query_grad, key_grad, value_grad
    )
    came_b, came_c = came[:2], came[2:]
    operands = (
        attended, branch_grad, normed[2], value_grad, normed[1], key_grad, normed[0], query_grad,
    )
    operands = [flat(operand) for operand in operands]
    keep_a, send_a, keep_b, send_b = call(
        "weights_back", weights_back_kernel, (), [SMEM] + [ANY] * 8,
        [(ANY, (2, slots // 2, width // slots, width), low)] * 4, (out_places, *operands),
        scratch=[pltpu.VMEM(operand.shape, low) for operand in operands] + [square_vmem] * 4 + [dma((12,))],
    )
    came_b, came_c, keep_a, send_a, keep_b, send_b = stage(came_b, came_c, keep_a, send_a, keep_b, send_b)

    (keep_a, send_a), (keep_b, send_b) = net.unaligned(keep_a, send_a), net.unaligned(keep_b, send_b)
    came, (keep_a, keep_b, query_grad, key_grad, value_grad) = net.moves(
        [("core", send_a), ("core", send_b)], keep_a, keep_b, query_grad, key_grad, value_grad
    )
    first_a = (keep_a, keep_b, *came)
    operands = (
        places, query_grad, key_grad, value_grad, key_hat, value_hat, key_scale, value_scale, middle_grad, mixed_came, small,
        *part_a, *part_b,
    )
    home_rows = 2 * masked + visible
    masked_own, latent_own, away, input_sums = call(
        "input_back", functools.partial(input_back_kernel, len(part_a), len(part_b)), (crops,),
        [SMEM] + [by_crop(a.shape) for a in operands[1:10]] + [None] + [ANY] * parts,
        [
            crop_out(masked_shape, f32), crop_out(latent_shape, f32), crop_out((crops, home_rows, width), low), sums_out,
        ],
        operands, scratch=[square_vmem] * 3 + [dma((3,))],
    )
    masked_own, latent_own, away, input_sums, first_a = stage(masked_own, latent_own, away, input_sums, first_a)

    kept_a, sends_a = net.scatter_second(first_a)
    (shape_b, kept_b), sends_b = net.scatter_fourth(kept_b, came_b)
    strips = jnp.arange(LINE_ROWS - BIAS_ROW)[:, None]
    strips = jnp.where(strips == net.at_core, bias_b, 0.0) + jnp.where(strips == 2 + net.at_core, bias_c, 0.0)
    lines = jnp.concatenate([input_sums, feed_sums, strips])
    came, (kept_a, kept_b, lines) = net.moves([*sends_a, *sends_b, ("core", lines)], kept_a, kept_b, lines)
    lines = lines + came[-1]
    line_y = net.swap_y(lines)
    came, lines, line_y = stage(came[:-1], lines, line_y)
    came_a, came_b = came[:2], came[2:]

    kept_a, sends_a = net.scatter_third(kept_a, came_a)
    (shape_c, kept_c), sends_c = net.scatter_fourth(kept_c, came_c)
    lines = lines + line_y
    high = lines.astype(low)
    rest = (lines - high.astype(f32)).astype(low)
    ridden = jnp.concatenate([flat(sends_a[1][1]), high, rest])
    shape = sends_a[1][1].shape
    came, (kept_a, kept_c, lines) = net.moves([("x", ridden), sends_a[0], *sends_c], kept_a, kept_c, lines)
    came_x, came_c = came[0], came[2:]
    line_x = came_x[-2 * LINE_ROWS : -LINE_ROWS].astype(f32) + came_x[-LINE_ROWS:].astype(f32)
    came_a = (came[1], came_x[: -2 * LINE_ROWS].reshape(shape))
    lines = lines + line_x
    came_a, lines, away = stage(came_a, lines, away)

    home_rows = net.swap_y(away)
    (shape_a, kept_a), sends_a = net.scatter_fourth(kept_a, came_a)
    sends_a = [(kind, jnp.concatenate([piece, lines.astype(low)]), step) for kind, piece, step in sends_a]
    came_a, (kept_a, lines, came_b, came_c) = net.moves(sends_a, kept_a, lines, came_b, came_c)
    lines = sum((piece[-LINE_ROWS:].astype(f32) for piece in came_a), lines)
    came_a = [piece[:-LINE_ROWS] for piece in came_a]
    down_sums, up_sums = zip(
        net.scatter_last((shape_b, kept_b), came_b), net.scatter_last((shape_c, kept_c), came_c)
    )
    down_sum = jnp.concatenate([down[0] for down in down_sums])
    up_sums = jnp.stack([up.reshape(2, shard, width) for up in up_sums])
    up_came = net.swap_core(up_sums[:, 1])
    up_sums = jnp.where(net.at_core == 0, jnp.stack([up_sums[:, 0], up_came]), jnp.stack([up_came, up_sums[:, 0]]))
    up_sum = jnp.moveaxis(up_sums.reshape(2, 2, shard, pairs, 2, half), (0, 1), (2, 4)).reshape(shard, count * deep)
    sum_a, sum_b = net.scatter_last((shape_a, kept_a), came_a)
    sum_b = sum_b.reshape(sum_a.shape)

    vector = lax.dynamic_slice(lines, (0, shard * device), (BIAS_ROW, shard))
    column = half * (2 * (device // 4) + device % 2)
    strip = lambda k: lax.dynamic_slice(lines, (BIAS_ROW + 2 * k + net.at_core, column), (1, half))
    bias_up_sum = jnp.concatenate([strip(0)[0], strip(1)[0]])

    def home(keep, came, dtype):
        keep, came = keep.astype(dtype), came.astype(dtype)
        return jnp.concatenate([jnp.where(slot == 0, keep, came), jnp.where(slot == 0, came, keep)], axis=0)

    return (
        home(mixed_own, home_rows[:, masked : 2 * masked], low),
        home(latent_own, home_rows[:, 2 * masked :], f32),
        home(masked_own, home_rows[:, :masked], f32),
        sum_a[0],
        vector[5],
        sum_a[1],
        sum_b[0],
        vector[6],
        sum_b[1],
        vector[13],
        vector[0],
        vector[1],
        vector[2],
        vector[3],
        vector[4],
        vector[12],
        up_sum,
        bias_up_sum,
        down_sum,
        vector[9],
        vector[10],
        vector[11],
        vector[8],
    )


def solution(mesh):
    batch, query = mesh.devices.shape
    split = Mesh(mesh.devices.reshape(batch // 4, 2, 2, query), (*BATCH, "query"))
    crop, rows, flat = P(BATCH, "query", None), P((*BATCH, "query"), None), P((*BATCH, "query"))
    in_specs = (crop, crop, P(BATCH, None), rows, flat, rows, rows, flat, rows, *[flat] * 7, rows, flat, rows, *[flat] * 4, crop)
    out_specs = (crop, crop, crop, rows, flat, rows, rows, flat, rows, *[flat] * 7, rows, flat, rows, *[flat] * 4)
    return jax.shard_map(local, mesh=split, in_specs=in_specs, out_specs=out_specs, check_vma=False)
```
